32 devices in a mesh: ctx: 8 (over y, x, core), tp: 4 (over z).
Axes of the slice: x: 2, y: 2, z: 4, core: 2. Of those that a mesh axis runs over, the one named last changes fastest.
Arguments:
- block_in: bfloat16 [4096, 2048], P(('ctx', 'tp')), may hold values from -6 to 6
- out_grad: bfloat16 [4096, 2048], P(('ctx', 'tp')), may hold values from -6 to 6
- pair_slot: int32 [8], replicated, may hold values from 0 to 7, each once
- gain_attn: bfloat16 [2048], P('ctx'), may hold values from 0.099609375 to 1.8984375
- wq: bfloat16 [2048, 2048], P('ctx', 'tp'), may hold values from -0.125 to 0.125
- wk: bfloat16 [2048, 512], P('ctx', 'tp'), may hold values from -0.125 to 0.125
- wv: bfloat16 [2048, 512], P('ctx', 'tp'), may hold values from -0.125 to 0.125
- wo: bfloat16 [2048, 2048], P('ctx', 'tp'), may hold values from -2 to 2
- gain_mlp: bfloat16 [2048], P('ctx'), may hold values from 0.099609375 to 1.8984375
- w_gate: bfloat16 [2048, 8192], P('ctx', 'tp'), may hold values from -0.125 to 0.125
- w_up: bfloat16 [2048, 8192], P('ctx', 'tp'), may hold values from -0.125 to 0.125
- w_down: bfloat16 [2048, 8192], P('ctx', 'tp'), may hold values from -0.0625 to 0.0625
Outputs:
- block_out: bfloat16 [4096, 2048], P(('ctx', 'tp'))
- input_grad: float32 [4096, 2048], P(('ctx', 'tp'))
- grad_gain_attn: float32 [2048], P('ctx')
- grad_wq: float32 [2048, 2048], P('ctx', 'tp')
- grad_wk: float32 [2048, 512], P('ctx', 'tp')
- grad_wv: float32 [2048, 512], P('ctx', 'tp')
- grad_wo: float32 [2048, 2048], P('ctx', 'tp')
- grad_gain_mlp: float32 [2048], P('ctx')
- grad_w_gate: float32 [2048, 8192], P('ctx', 'tp')
- grad_w_up: float32 [2048, 8192], P('ctx', 'tp')
- grad_w_down: float32 [2048, 8192], P('ctx', 'tp')
The draws below stay inside these ranges and needn't reach their ends.
Inputs may be any that keep to these rules, and one draw needn't show every extreme that they name: `pair_slot`: each of 0 to 7 appears once.
All inputs are finite; a program needn't handle non-finite values.
Results may differ from the reference program's by a relative error of at most 0.024.
Values may be sent and summed in bfloat16 or wider, within the bound.
No kernel may reach another device: no remote copies, remote signals or barrier semaphores. Data moves between devices by JAX's collectives and lax.ppermute only.
A program may use at most 256 MiB of HBM per device.

```python
import math
import jax
import jax.numpy as jnp
from jax import lax

MODEL_WIDTH = 2048
QUERY_HEADS = 32
KEY_VALUE_HEADS = 8
HEAD_SIZE = 64
FF = 8192
BLOCK = 256
SEQUENCE_TOKENS = 4096
N_CTX = 8


def levels(stream_key, shape, split, least, largest):
    loudness, own = 1.0, jax.random.fold_in(stream_key, 6)
    for position, blocks in split:
        draws = jnp.exp(jax.random.uniform(jax.random.fold_in(own, position), (blocks,), jnp.float32, least / len(split), largest / len(split)))
        loudness = loudness * jnp.repeat(draws, shape[position] // blocks).reshape([-1 if axis == position else 1 for axis in range(len(shape))])
    return loudness


def normal_values(rng, extent, spread, most, split=(), held_as=jnp.bfloat16):
    array = spread * jax.random.normal(rng, extent, jnp.float32)
    if split:
        array = array * levels(rng, extent, split, -0.22, 0.18)
    return jnp.clip(array, -most, most).astype(held_as)


def setup_inputs(seed: int = 0) -> dict:
    keys = jax.random.split(jax.random.key(seed), 13)
    return {
        "block_in": normal_values(keys[0], (SEQUENCE_TOKENS, MODEL_WIDTH), 1.0, 6.0, ((0, 32),)),
        "out_grad": normal_values(keys[1], (SEQUENCE_TOKENS, MODEL_WIDTH), 1.0, 6.0, ((0, 32),)),
        "pair_slot": jax.random.permutation(keys[2], N_CTX).astype(jnp.int32),
        "gain_attn": jnp.clip(1.0 + 0.18 * jax.random.normal(keys[3], (MODEL_WIDTH,), jnp.float32), 0.099609375, 1.8984375).astype(jnp.bfloat16),
        "wq": normal_values(keys[4], (MODEL_WIDTH, QUERY_HEADS * HEAD_SIZE), MODEL_WIDTH ** -0.5, 0.125, ((0, 8), (1, 4))),
        "wk": normal_values(keys[5], (MODEL_WIDTH, KEY_VALUE_HEADS * HEAD_SIZE), MODEL_WIDTH ** -0.5, 0.125, ((0, 8), (1, 4))),
        "wv": normal_values(keys[6], (MODEL_WIDTH, KEY_VALUE_HEADS * HEAD_SIZE), MODEL_WIDTH ** -0.5, 0.125, ((0, 8), (1, 4))),
        "wo": normal_values(keys[7], (MODEL_WIDTH, QUERY_HEADS * HEAD_SIZE), (max(1, QUERY_HEADS * HEAD_SIZE * 16 // SEQUENCE_TOKENS)) ** -0.5, 2.0, ((0, 8), (1, 4))),
        "gain_mlp": jnp.clip(1.0 + 0.18 * jax.random.normal(keys[8], (MODEL_WIDTH,), jnp.float32), 0.099609375, 1.8984375).astype(jnp.bfloat16),
        "w_gate": normal_values(keys[9], (MODEL_WIDTH, FF), MODEL_WIDTH ** -0.5, 0.125, ((0, 8), (1, 4))),
        "w_up": normal_values(keys[10], (MODEL_WIDTH, FF), MODEL_WIDTH ** -0.5, 0.125, ((0, 8), (1, 4))),
        "w_down": normal_values(keys[11], (MODEL_WIDTH, FF), FF ** -0.5, 0.0625, ((0, 8), (1, 4))),
    }


eps_norm = 1e-05
big_negative = -1e+30

@jax.custom_vjp
def lower_block(v):
    return lax.optimization_barrier(v.astype(jnp.bfloat16)).astype(jnp.float32)

@jax.custom_vjp
def low_back(v):
    return v

def low_keep(v):
    return (lower_block(v), None)

def low_pass(kept, grad):
    return (grad,)

def back_keep(v):
    return (v, None)

def back_low(kept, grad):
    return (lower_block(grad),)
lower_block.defvjp(low_keep, low_pass)
low_back.defvjp(back_keep, back_low)

def matmul(left, right):
    return jnp.dot(left, right, precision=lax.Precision.HIGHEST, preferred_element_type=jnp.float32)

def block_positions(pair_slot, block_len):
    pair_count = pair_slot.shape[0]
    offsets = jnp.arange(2 * block_len, dtype=jnp.int32)
    lower_half = offsets < block_len
    block_index = jnp.where(lower_half[None, :], pair_slot[:, None], 2 * pair_count - 1 - pair_slot[:, None])
    return (block_index * block_len + (offsets % block_len)[None, :]).reshape(-1).astype(jnp.int32)

def inverse_freqs(head_dim):
    exponent = jnp.arange(0, head_dim, 2).astype(jnp.float32) / head_dim
    base_freq = 500000.0 ** (-exponent)
    wavelength = 2.0 * math.pi / base_freq
    smooth = (8192.0 / wavelength - 1.0) / 3.0
    blended = (1.0 - smooth) * base_freq / 32.0 + smooth * base_freq
    scaled = jnp.where(wavelength > 8192.0, base_freq / 32.0, base_freq)
    middle = (wavelength >= 2048.0) & (wavelength <= 8192.0)
    return jnp.where(middle, blended, scaled)

def rope_tables(positions, head_dim):
    angles = positions.astype(jnp.float32)[:, None] * inverse_freqs(head_dim)[None, :]
    doubled = jnp.concatenate([angles, angles], axis=1)
    return (jnp.cos(doubled), jnp.sin(doubled))

def apply_rotation(values, cosine_table, sine_table):
    half_dim = values.shape[-1] // 2
    turned = jnp.concatenate([-values[..., half_dim:], values[..., :half_dim]], axis=-1)
    return values * cosine_table[:, None, :] + turned * sine_table[:, None, :]

def rms_scale(values):
    return lax.rsqrt(lax.optimization_barrier(jnp.mean(values * values, axis=-1, keepdims=True)) + eps_norm)

def attend(rows_of_query, rows_of_key, rows_of_value, positions):
    repeat_heads = QUERY_HEADS // KEY_VALUE_HEADS
    block_of_query = math.gcd(128, SEQUENCE_TOKENS)
    score_scale = HEAD_SIZE ** (-0.5)
    heads_of_query = rows_of_query.reshape(SEQUENCE_TOKENS // block_of_query, block_of_query, KEY_VALUE_HEADS, repeat_heads, HEAD_SIZE)
    heads_of_key = rows_of_key.reshape(SEQUENCE_TOKENS, KEY_VALUE_HEADS, HEAD_SIZE)
    heads_of_value = rows_of_value.reshape(SEQUENCE_TOKENS, KEY_VALUE_HEADS, HEAD_SIZE)
    query_pos = positions.reshape(SEQUENCE_TOKENS // block_of_query, block_of_query)

    def attend_block(pieces):
        queries_here, pos_here = pieces
        scores = jnp.einsum('qgrd,kgd->grqk', queries_here, heads_of_key, precision=lax.Precision.HIGHEST)
        scores = low_back(scores * score_scale)
        visible = positions[None, :] <= pos_here[:, None]
        scores = jnp.where(visible, scores, big_negative)
        row_max = lax.optimization_barrier(jnp.max(scores, axis=-1, keepdims=True))
        weights = jnp.where(visible, jnp.exp(scores - row_max), 0.0)
        probabilities = lower_block(weights / lax.optimization_barrier(jnp.sum(weights, axis=-1, keepdims=True)))
        output = jnp.einsum('grqk,kgd->qgrd', probabilities, heads_of_value, precision=lax.Precision.HIGHEST)
        return output.reshape(block_of_query, QUERY_HEADS * HEAD_SIZE)
    return lax.map(jax.checkpoint(attend_block), (heads_of_query, query_pos)).reshape(SEQUENCE_TOKENS, QUERY_HEADS * HEAD_SIZE)

def reference(block_in, out_grad, pair_slot, gain_attn, wq, wk, wv, wo, gain_mlp, w_gate, w_up, w_down):
    positions = block_positions(pair_slot, BLOCK)
    cosine_table, sine_table = rope_tables(positions, HEAD_SIZE)

    def layer(inputs, g_attn, q_w, k_w, v_w, o_w, g_mlp, gate_w, up_w, down_w):
        attn_in = lower_block(inputs * rms_scale(inputs) * g_attn)
        query_raw = low_back(matmul(attn_in, q_w))
        key_unrotated = low_back(matmul(attn_in, k_w))
        values = lower_block(low_back(matmul(attn_in, v_w)))
        queries = lower_block(apply_rotation(query_raw.reshape(SEQUENCE_TOKENS, QUERY_HEADS, HEAD_SIZE), cosine_table, sine_table).reshape(SEQUENCE_TOKENS, QUERY_HEADS * HEAD_SIZE))
        rows_of_key = lower_block(apply_rotation(key_unrotated.reshape(SEQUENCE_TOKENS, KEY_VALUE_HEADS, HEAD_SIZE), cosine_table, sine_table).reshape(SEQUENCE_TOKENS, KEY_VALUE_HEADS * HEAD_SIZE))
        attended = lower_block(low_back(attend(queries, rows_of_key, values, positions)))
        residual = inputs + low_back(matmul(attended, o_w.T))
        mlp_in = lower_block(residual * rms_scale(residual) * g_mlp)
        gate_proj = low_back(matmul(mlp_in, gate_w))
        up_proj = low_back(matmul(mlp_in, up_w))
        hidden = lower_block(jax.nn.silu(gate_proj) * up_proj)
        return residual + low_back(matmul(hidden, down_w.T))
    floats = [argument.astype(jnp.float32) for argument in (block_in, gain_attn, wq, wk, wv, wo, gain_mlp, w_gate, w_up, w_down)]
    result, pullback = jax.vjp(layer, *floats)
    gradient = pullback(out_grad.astype(jnp.float32))
    return (result.astype(jnp.bfloat16), gradient[0], gradient[1], gradient[2], gradient[3], gradient[4], gradient[5], gradient[6], gradient[7], gradient[8], gradient[9])
```

```python
import functools
import math

import jax
import jax.numpy as jnp
from jax import lax
from jax.experimental import pallas as pl
from jax.experimental.pallas import tpu as pltpu
from jax.sharding import PartitionSpec as P

HEAD_SIZE = 64
LANES = 128
KERNEL_VMEM = 56 * 1024 * 1024

eps_norm = 1e-05
big_negative = -1e30

in_smem = pl.BlockSpec(memory_space=pltpu.SMEM)
in_vmem = pl.BlockSpec(memory_space=pltpu.VMEM)


def kernel_params():
    return pltpu.CompilerParams(vmem_limit_bytes=KERNEL_VMEM)


def cost(flops, moved):
    return pl.CostEstimate(flops=int(flops), bytes_accessed=int(moved), transcendentals=0)


def bit_order(bits):
    return [1, 2, 0] + list(range(3, bits)) if bits >= 3 else list(range(bits))


def block_key(position, bits):
    key = 0
    for place, bit in enumerate(bit_order(bits)):
        key = key | (((position >> place) & 1) << bit)
    return key


def key_position(key, bits):
    position = 0
    for place, bit in enumerate(bit_order(bits)):
        position = position | (((key >> bit) & 1) << place)
    return position


def swap(array, bit, bits):
    return lax.ppermute(array, "ctx", [(i, i ^ (1 << bit)) for i in range(1 << bits)])


def gather_ctx(own, bits, axis=0):
    first, second = bit_order(bits)[:2]
    middle = own.shape[axis] // 2
    by_first = swap(own, first, bits)
    by_second = swap(own, second, bits)
    lower = lax.slice_in_dim(by_first, 0, middle, axis=axis)
    upper = lax.slice_in_dim(by_second, middle, 2 * middle, axis=axis)
    both_lower = swap(lower, second, bits)
    both_upper = swap(upper, first, bits)
    parts = [jnp.concatenate([own, by_first, by_second, both_lower, both_upper], axis=axis)]
    for bit in bit_order(bits)[2:]:
        parts = parts + [swap(part, bit, bits) for part in parts]
    return parts


def scatter_pieces(parts, bits):
    for bit in reversed(bit_order(bits)[2:]):
        kept = len(parts) // 2
        received = [swap(part, bit, bits) for part in parts[kept:]]
        parts = [
            (mine.astype(jnp.float32) + other.astype(jnp.float32)).astype(jnp.bfloat16)
            for mine, other in zip(parts[:kept], received)
        ]
    first, second = bit_order(bits)[:2]
    own, at_first, at_second, at_both = jnp.split(parts[0], 4, axis=0)
    middle = own.shape[0] // 2
    lower = swap(at_both[:middle], second, bits)
    upper = swap(at_both[middle:], first, bits)
    to_first = jnp.concatenate([at_first[:middle] + lower, at_first[middle:]], axis=0)
    to_second = jnp.concatenate([at_second[:middle], at_second[middle:] + upper], axis=0)
    return own, swap(to_first, first, bits), swap(to_second, second, bits)


def scatter_ctx(parts, bits):
    own, by_first, by_second = scatter_pieces(parts, bits)
    return own.astype(jnp.float32) + by_first.astype(jnp.float32) + by_second.astype(jnp.float32)


def to_relative(array, me, bits):
    width = array.shape[1] // (1 << bits)
    return jnp.concatenate(
        [
            lax.dynamic_slice_in_dim(array, (me ^ block_key(p, bits)) * width, width, 1)
            for p in range(1 << bits)
        ],
        axis=1,
    )


def to_absolute(array, me, bits):
    width = array.shape[1] // (1 << bits)
    return jnp.concatenate(
        [
            lax.dynamic_slice_in_dim(array, key_position(me ^ c, bits) * width, width, 1)
            for c in range(1 << bits)
        ],
        axis=1,
    )


def block_positions(pair_slot, block_len):
    pair_count = pair_slot.shape[0]
    offsets = jnp.arange(2 * block_len, dtype=jnp.int32)
    lower_half = offsets < block_len
    block_index = jnp.where(
        lower_half[None, :], pair_slot[:, None], 2 * pair_count - 1 - pair_slot[:, None]
    )
    return (block_index * block_len + (offsets % block_len)[None, :]).reshape(-1)


def inverse_freqs(head_dim):
    exponent = jnp.arange(0, head_dim, 2).astype(jnp.float32) / head_dim
    base_freq = 500000.0 ** (-exponent)
    wavelength = 2.0 * math.pi / base_freq
    smooth = (8192.0 / wavelength - 1.0) / 3.0
    blended = (1.0 - smooth) * base_freq / 32.0 + smooth * base_freq
    scaled = jnp.where(wavelength > 8192.0, base_freq / 32.0, base_freq)
    middle = (wavelength >= 2048.0) & (wavelength <= 8192.0)
    return jnp.where(middle, blended, scaled)


def rope_tables(positions):
    angles = positions.astype(jnp.float32)[:, None] * inverse_freqs(HEAD_SIZE)[None, :]
    wide = LANES // (HEAD_SIZE // 2)
    return (jnp.tile(jnp.cos(angles), (1, wide)), jnp.tile(jnp.sin(angles), (1, wide)))


def rms_scale(values):
    return lax.rsqrt(jnp.mean(values * values, axis=-1, keepdims=True) + eps_norm)


def norm_back(gradient, normed, factor):
    return factor * (gradient - normed * jnp.mean(gradient * normed, axis=-1, keepdims=True))


def inner_rows(left, right):
    return lax.dot_general(
        left, right, (((0,), (0,)), ((), ())), preferred_element_type=jnp.float32
    )


def nt(left, right):
    return lax.dot_general(
        left, right, (((1,), (1,)), ((), ())), preferred_element_type=jnp.float32
    )


def nn(left, right):
    return lax.dot_general(
        left, right, (((1,), (0,)), ((), ())), preferred_element_type=jnp.float32
    )


def turned_lanes(values):
    half = HEAD_SIZE // 2
    lane = lax.broadcasted_iota(jnp.int32, values.shape, 1)
    up = pltpu.roll(values, LANES - half, 1)
    down = pltpu.roll(values, half, 1)
    return jnp.where(lane % HEAD_SIZE < half, -up, down)


def rotate(values, cosine, sine):
    return values * cosine + turned_lanes(values) * sine


def rotate_back(gradient, cosine, sine):
    return gradient * cosine - turned_lanes(gradient * sine)


def qkv_kernel(count, x_ref, *refs):
    weights, (cos_ref, sin_ref, q_ref, kv_ref) = refs[:count], refs[count:]
    depth = x_ref.shape[1] // count
    width_q = q_ref.shape[1]
    width_k = kv_ref.shape[1] // 2
    total = width_q + 2 * width_k
    tile = 2 * LANES
    for start in range(0, total, tile):
        product = 0.0
        for index, weight in enumerate(weights):
            product = product + nn(
                x_ref[:, index * depth : (index + 1) * depth], weight[:, start : start + tile]
            )
        for offset in range(0, tile, LANES):
            at = start + offset
            piece = product[:, offset : offset + LANES]
            if at < width_q + width_k:
                piece = rotate(piece, cos_ref[...], sin_ref[...])
            piece = piece.astype(jnp.bfloat16)
            if at < width_q:
                q_ref[:, at : at + LANES] = piece
            else:
                kv_ref[:, at - width_q : at - width_q + LANES] = piece


def project_qkv(attn_in, weights, cosine, sine, width_q, width_k):
    rows, depth = attn_in.shape
    return pl.pallas_call(
        functools.partial(qkv_kernel, len(weights)),
        out_shape=(
            jax.ShapeDtypeStruct((rows, width_q), jnp.bfloat16),
            jax.ShapeDtypeStruct((rows, 2 * width_k), jnp.bfloat16),
        ),
        in_specs=[in_vmem] * (3 + len(weights)),
        out_specs=(in_vmem, in_vmem),
        compiler_params=kernel_params(),
        cost_estimate=cost(2 * rows * depth * (width_q + 2 * width_k), 6 << 20),
        name="qkv",
    )(attn_in, *weights, cosine, sine)


def sequence_block(slots, me, half_block, bits):
    slot = slots[me ^ block_key(half_block // 2, bits)]
    return jnp.where(half_block % 2 == 0, slot, 2 * (1 << bits) - 1 - slot)


def head_lanes(pair, head, heads_per_kv, scale):
    wide = pair.astype(jnp.float32) * scale
    group = head // heads_per_kv
    source = wide if head % 2 == group else pltpu.roll(wide, HEAD_SIZE, 1)
    low = lax.broadcasted_iota(jnp.int32, wide.shape, 1) < HEAD_SIZE
    keep = low if group == 0 else jnp.logical_not(low)
    return jnp.where(keep, source, 0.0).astype(jnp.bfloat16)


def causal_tile(size):
    key_at = lax.broadcasted_iota(jnp.int32, (size, size), 0)
    row_at = lax.broadcasted_iota(jnp.int32, (size, size), 1)
    return key_at <= row_at


def over_blocks(visit, slots, me, bits, half, prepare):
    visit(0, 0, True, True, True)
    visit(1, half, True, True, True)
    visit(1, 0, False, False, False)
    own = slots[me]
    blocks_of_query = (own, 2 * (1 << bits) - 1 - own)

    def step(index, carry):
        block = sequence_block(slots, me, index, bits)
        start = pl.multiple_of(index * half, half)
        prepare(start)
        for q_half in range(2):

            @pl.when(block < blocks_of_query[q_half])
            def _():
                visit(q_half, start, False, False, False)

        return carry

    lax.fori_loop(2, 2 * (1 << bits), step, 0)


def forward_kernel(
    bits, heads, slots, place, q_ref, kv_ref, out_ref, exact_ref, log_ref, qp, run_max, run_sum, acc
):
    rows = q_ref.shape[0]
    half = rows // 2
    per_kv = heads // 2
    for head in range(heads):
        lanes = pl.ds((head // 2) * LANES, LANES)
        qp[head] = head_lanes(q_ref[:, lanes], head, per_kv, HEAD_SIZE ** (-0.5))

    def visit(q_half, key_start, diagonal, first, _):
        keys = kv_ref[pl.ds(key_start, half), 0:LANES]
        values_t = kv_ref[pl.ds(key_start, half), LANES : 2 * LANES].T
        base = q_half * heads
        span = pl.ds(q_half * half, half)
        scores = [nt(keys, qp[head, span, :]) for head in range(heads)]
        if diagonal:
            visible = causal_tile(half)
            scores = [jnp.where(visible, score, big_negative) for score in scores]
        peaks = [jnp.max(score, axis=0, keepdims=True) for score in scores]
        if not first:
            before = [run_max[base + head] for head in range(heads)]
            peaks = [jnp.maximum(peak, old) for peak, old in zip(peaks, before)]
        weights = [jnp.exp(score - peak) for score, peak in zip(scores, peaks)]
        totals = [jnp.sum(weight, axis=0, keepdims=True) for weight in weights]
        outs = []
        for head, weight in enumerate(weights):
            group = head // per_kv
            some = values_t[group * HEAD_SIZE : (group + 1) * HEAD_SIZE]
            outs.append(nn(some, weight.astype(jnp.bfloat16)))
        if not first:
            fades = [jnp.exp(old - peak) for old, peak in zip(before, peaks)]
            totals = [t + run_sum[base + h] * f for h, (t, f) in enumerate(zip(totals, fades))]
            outs = [o + acc[base + h] * f for h, (o, f) in enumerate(zip(outs, fades))]
        for head in range(heads):
            run_max[base + head] = peaks[head]
            run_sum[base + head] = totals[head]
            acc[base + head] = outs[head]

    over_blocks(visit, slots, place[0], bits, half, lambda start: None)
    for q_half in range(2):
        span = pl.ds(q_half * half, half)
        for pair in range(heads // 2):
            parts = []
            for head in (2 * pair, 2 * pair + 1):
                slot = q_half * heads + head
                parts.append(acc[slot] / run_sum[slot])
                log_ref[pl.ds(head, 1), span] = run_max[slot] + jnp.log(run_sum[slot])
            exact = jnp.concatenate(parts, axis=0).T
            exact_ref[span, pl.ds(pair * LANES, LANES)] = exact
            out_ref[span, pl.ds(pair * LANES, LANES)] = exact.astype(jnp.bfloat16)


def attend_forward(slots, place, queries, kv, bits):
    rows, width = queries.shape
    heads = width // HEAD_SIZE
    half = rows // 2
    visits = 2 * (1 << bits) + 1
    return pl.pallas_call(
        functools.partial(forward_kernel, bits, heads),
        out_shape=(
            jax.ShapeDtypeStruct((rows, width), jnp.bfloat16),
            jax.ShapeDtypeStruct((rows, width), jnp.float32),
            jax.ShapeDtypeStruct((heads, rows), jnp.float32),
        ),
        in_specs=[in_smem, in_smem, in_vmem, in_vmem],
        out_specs=(in_vmem, in_vmem, in_vmem),
        scratch_shapes=[
            pltpu.VMEM((heads, rows, LANES), jnp.bfloat16),
            pltpu.VMEM((2 * heads, 1, half), jnp.float32),
            pltpu.VMEM((2 * heads, 1, half), jnp.float32),
            pltpu.VMEM((2 * heads, HEAD_SIZE, half), jnp.float32),
        ],
        compiler_params=kernel_params(),
        cost_estimate=cost(20 * visits * heads * half * half * HEAD_SIZE, 8 << 20),
        name="attention_forward",
    )(slots, place, queries, kv)


def backward_kernel(
    bits,
    heads,
    slots,
    place,
    q_ref,
    kv_ref,
    do_ref,
    exact_ref,
    log_ref,
    cos_ref,
    sin_ref,
    dq_ref,
    dkv_ref,
    qp,
    dop,
    dots,
    dq_acc,
    dkv_acc,
    do_all,
):
    rows = q_ref.shape[0]
    half = rows // 2
    per_kv = heads // 2
    shifts, local, _ = do_ref.shape
    for shift in range(shifts):
        source = lax.rem(place[1] - shift + shifts, shifts)
        do_all[pl.ds(pl.multiple_of(source * local, local), local), :] = do_ref[shift]
    for head in range(heads):
        lanes = pl.ds((head // 2) * LANES, LANES)
        qp[head] = head_lanes(q_ref[:, lanes], head, per_kv, HEAD_SIZE ** (-0.5))
        dop[head] = head_lanes(do_all[:, lanes], head, per_kv, 1.0)
    for pair in range(heads // 2):
        lanes = pl.ds(pair * LANES, LANES)
        product = (do_all[:, lanes].astype(jnp.float32) * exact_ref[:, lanes]).T
        dots[pl.ds(2 * pair, 1), :] = jnp.sum(product[:HEAD_SIZE], axis=0, keepdims=True)
        dots[pl.ds(2 * pair + 1, 1), :] = jnp.sum(product[HEAD_SIZE:], axis=0, keepdims=True)

    def clear(start):
        dkv_acc[pl.ds(start, half), :] = jnp.zeros((half, 2 * LANES), jnp.float32)

    def visit(q_half, key_start, diagonal, first_query, first_key):
        rows_of_key = pl.ds(key_start, half)
        keys = kv_ref[rows_of_key, 0:LANES]
        values = kv_ref[rows_of_key, LANES : 2 * LANES]
        keys_t = keys.T
        base = q_half * heads
        span = pl.ds(q_half * half, half)
        q_heads = [qp[head, span, :] for head in range(heads)]
        do_heads = [dop[head, span, :] for head in range(heads)]
        scores = [nt(keys, q_head) for q_head in q_heads]
        grad_ws = [nt(values, do_head) for do_head in do_heads]
        weights = [
            jnp.exp(score - log_ref[pl.ds(head, 1), span]) for head, score in enumerate(scores)
        ]
        if diagonal:
            visible = causal_tile(half)
            weights = [jnp.where(visible, weight, 0.0) for weight in weights]
        grad_ss = [
            (weight * (grad_w - dots[pl.ds(head, 1), span])).astype(jnp.bfloat16)
            for head, (weight, grad_w) in enumerate(zip(weights, grad_ws))
        ]
        weights = [weight.astype(jnp.bfloat16) for weight in weights]
        grad_v = jnp.zeros((half, LANES), jnp.float32)
        grad_k = jnp.zeros((half, LANES), jnp.float32)
        for weight, do_head in zip(weights, do_heads):
            grad_v = grad_v + nn(weight, do_head)
        for grad_s, q_head in zip(grad_ss, q_heads):
            grad_k = grad_k + nn(grad_s, q_head)
        for head, grad_s in enumerate(grad_ss):
            group = head // per_kv
            grad_q = nn(keys_t[group * HEAD_SIZE : (group + 1) * HEAD_SIZE], grad_s)
            if not first_query:
                grad_q = grad_q + dq_acc[base + head]
            dq_acc[base + head] = grad_q
        if not first_key:
            grad_k = grad_k + dkv_acc[rows_of_key, 0:LANES]
            grad_v = grad_v + dkv_acc[rows_of_key, LANES : 2 * LANES]
        dkv_acc[rows_of_key, 0:LANES] = grad_k
        dkv_acc[rows_of_key, LANES : 2 * LANES] = grad_v

    over_blocks(visit, slots, place[0], bits, half, clear)
    dkv_ref[...] = dkv_acc[...].astype(jnp.bfloat16)
    for q_half in range(2):
        span = pl.ds(q_half * half, half)
        for pair in range(heads // 2):
            slot = q_half * heads + 2 * pair
            gradient = jnp.concatenate([dq_acc[slot], dq_acc[slot + 1]], axis=0).T
            gradient = rotate_back(
                gradient * HEAD_SIZE ** (-0.5), cos_ref[span, :], sin_ref[span, :]
            )
            dq_ref[span, pl.ds(pair * LANES, LANES)] = gradient.astype(jnp.bfloat16)


def attend_backward(slots, place, queries, kv, grad_parts, exact, log_total, cosine, sine, bits):
    rows, width = queries.shape
    heads = width // HEAD_SIZE
    half = rows // 2
    visits = 2 * (1 << bits) + 1
    return pl.pallas_call(
        functools.partial(backward_kernel, bits, heads),
        out_shape=(
            jax.ShapeDtypeStruct((rows, width), jnp.bfloat16),
            jax.ShapeDtypeStruct(kv.shape, jnp.bfloat16),
        ),
        in_specs=[in_smem, in_smem] + [in_vmem] * 7,
        out_specs=(in_vmem, in_vmem),
        scratch_shapes=[
            pltpu.VMEM((heads, rows, LANES), jnp.bfloat16),
            pltpu.VMEM((heads, rows, LANES), jnp.bfloat16),
            pltpu.VMEM((heads, rows), jnp.float32),
            pltpu.VMEM((2 * heads, HEAD_SIZE, half), jnp.float32),
            pltpu.VMEM(kv.shape, jnp.float32),
            pltpu.VMEM((rows, width), jnp.bfloat16),
        ],
        compiler_params=kernel_params(),
        cost_estimate=cost(40 * visits * heads * half * half * HEAD_SIZE, 12 << 20),
        name="attention_backward",
    )(slots, place, queries, kv, grad_parts, exact, log_total, cosine, sine)


def grad_qkv_kernel(dq_ref, own_ref, first_ref, second_ref, cos_ref, sin_ref, out_ref):
    width_q = dq_ref.shape[1]
    out_ref[:, 0:width_q] = dq_ref[...]
    total = (
        own_ref[...].astype(jnp.float32)
        + first_ref[...].astype(jnp.float32)
        + second_ref[...].astype(jnp.float32)
    )
    keys = rotate_back(total[:, 0:LANES], cos_ref[...], sin_ref[...])
    out_ref[:, width_q : width_q + LANES] = keys.astype(jnp.bfloat16)
    out_ref[:, width_q + LANES : width_q + 2 * LANES] = total[:, LANES:].astype(jnp.bfloat16)


def join_grad_qkv(grad_queries, pieces, cosine, sine):
    rows, width_q = grad_queries.shape
    width = width_q + pieces[0].shape[1]
    return pl.pallas_call(
        grad_qkv_kernel,
        out_shape=jax.ShapeDtypeStruct((rows, width), jnp.bfloat16),
        in_specs=[in_vmem] * 6,
        out_specs=in_vmem,
        compiler_params=kernel_params(),
        cost_estimate=cost(rows * width * 8, 3 << 20),
        name="grad_qkv",
    )(grad_queries, *pieces, cosine, sine)


def mlp_kernel(count, x_ref, g_ref, *refs):
    gates, ups, downs = refs[:count], refs[count : 2 * count], refs[2 * count : 3 * count]
    hidden_ref, grad_gate_ref, grad_up_ref = refs[3 * count :]
    depth = x_ref.shape[1] // count

    def product(left, weights):
        total = 0.0
        for index, weight in enumerate(weights):
            total = total + nn(left[:, index * depth : (index + 1) * depth], weight[...])
        return total

    gate = product(x_ref, gates)
    up = product(x_ref, ups)
    grad_hidden = product(g_ref, downs)
    sigmoid = jax.nn.sigmoid(gate)
    silu = gate * sigmoid
    hidden_ref[...] = (silu * up).astype(jnp.bfloat16)
    grad_gate = grad_hidden * up * sigmoid * (1.0 + gate * (1.0 - sigmoid))
    grad_gate_ref[...] = grad_gate.astype(jnp.bfloat16)
    grad_up_ref[...] = (grad_hidden * silu).astype(jnp.bfloat16)


def mlp_inner(mlp_in, grad_rows, gates, ups, downs):
    rows, depth = mlp_in.shape
    units = gates[0].shape[1]
    count = len(gates)
    tile = min(256, units)
    whole = pl.BlockSpec((rows, depth), lambda i: (0, 0))
    weight = pl.BlockSpec((depth // count, tile), lambda i: (0, i))
    out = pl.BlockSpec((rows, tile), lambda i: (0, i))
    shape = jax.ShapeDtypeStruct((rows, units), jnp.bfloat16)
    return pl.pallas_call(
        functools.partial(mlp_kernel, count),
        grid=(units // tile,),
        out_shape=(shape, shape, shape),
        in_specs=[whole, whole] + [weight] * (3 * count),
        out_specs=(out, out, out),
        compiler_params=kernel_params(),
        cost_estimate=cost(6 * rows * depth * units, 6 * depth * units),
        name="mlp_inner",
    )(mlp_in, grad_rows, *gates, *ups, *downs)


def features_kernel(parts, tiles, lefts, *refs):
    out_ref = refs[-1]
    left_refs = refs[:lefts]
    weight_refs = refs[lefts:-1]
    step = pl.program_id(0)
    for part in range(parts):

        @pl.when(step // tiles == part)
        def _():
            total = 0.0
            for left, weight in zip(left_refs, weight_refs[part * lefts : (part + 1) * lefts]):
                for index in range(left.shape[0]):
                    total = total + nt(left[index], weight[index])
            out_ref[...] = total.astype(out_ref.dtype)


def to_features(lefts, weights, out_dtype):
    rows = lefts[0].shape[1]
    features = weights[0][0].shape[1]
    tile = min(256, features)
    tiles = features // tile
    parts = len(weights)
    in_specs = [pl.BlockSpec(left.shape, lambda i: (0, 0, 0)) for left in lefts]
    flops = 0
    for part, group in enumerate(weights):
        for weight in group:
            depth, _, width = weight.shape
            flops += 2 * rows * features * depth * width
            in_specs.append(
                pl.BlockSpec(
                    (depth, tile, width),
                    functools.partial(
                        lambda base, i: (0, jnp.clip(i - base, 0, tiles - 1), 0), part * tiles
                    ),
                )
            )
    return pl.pallas_call(
        functools.partial(features_kernel, parts, tiles, len(lefts)),
        grid=(parts * tiles,),
        out_shape=jax.ShapeDtypeStruct((rows, parts * features), out_dtype),
        in_specs=in_specs,
        out_specs=pl.BlockSpec((rows, tile), lambda i: (0, i)),
        compiler_params=kernel_params(),
        cost_estimate=cost(flops, flops // rows),
        name="to_features",
    )(*lefts, *[weight for group in weights for weight in group])


def groups_kernel(count, place, x_ref, *refs):
    out_ref = refs[-1]
    depth = x_ref.shape[1] // count
    total = 0.0
    for index, weight in enumerate(refs[:-1]):
        total = total + nn(x_ref[:, index * depth : (index + 1) * depth], weight[0])
    out_ref[0] = total.astype(jnp.bfloat16)


def to_groups(place, branch, weights):
    rows, depth = branch.shape
    groups, features, width = weights[0].shape
    count = len(weights)

    def weight_at(shift, place):
        return (lax.rem(place[1] + shift, groups), 0, 0)

    return pl.pallas_call(
        functools.partial(groups_kernel, count),
        grid_spec=pltpu.PrefetchScalarGridSpec(
            num_scalar_prefetch=1,
            grid=(groups,),
            in_specs=[pl.BlockSpec((rows, depth), lambda i, place: (0, 0))]
            + [pl.BlockSpec((1, features, width), weight_at)] * count,
            out_specs=pl.BlockSpec((1, rows, width), lambda i, place: (i, 0, 0)),
        ),
        out_shape=jax.ShapeDtypeStruct((groups, rows, width), jnp.bfloat16),
        compiler_params=kernel_params(),
        cost_estimate=cost(2 * rows * depth * groups * width, 2 * depth * groups * width),
        name="to_groups",
    )(place, branch, *weights)


def weight_gradient(left, right, parts):
    depth = left.shape[1] // parts
    return [
        inner_rows(left[:, index * depth : (index + 1) * depth], right).astype(jnp.bfloat16)
        for index in range(parts)
    ]


def on_device(
    block_in, out_grad, pair_slot, gain_attn, wq, wk, wv, wo, gain_mlp, w_gate, w_up, w_down
):
    bits = (lax.axis_size("ctx") - 1).bit_length()
    shifts = lax.axis_size("tp")
    me = lax.axis_index("ctx")
    tp = lax.axis_index("tp")
    place = jnp.stack([me, tp]).astype(jnp.int32)
    local_rows = block_in.shape[0]
    group_rows = local_rows * shifts
    width_q, width_k = wq.shape[1], wk.shape[1]

    rows_here = to_relative(block_in, me, bits)
    x_all = lax.all_gather(rows_here, "tp", axis=0, tiled=True)
    qkv_w = gather_ctx(jnp.concatenate([wq, wk, wv], axis=1), bits)
    count = len(qkv_w)
    gains = lax.all_gather(jnp.stack([gain_attn, gain_mlp]), "ctx", axis=1, tiled=True)
    gains = to_relative(gains, me, bits).astype(jnp.float32)
    g_attn, g_mlp = gains[0:1], gains[1:2]
    gate_w = gather_ctx(w_gate, bits)
    up_w = gather_ctx(w_up, bits)
    o_w = gather_ctx(lax.all_gather(wo, "tp", axis=0), bits, axis=1)
    down_w = gather_ctx(w_down, bits)
    out_grad_here = to_relative(out_grad, me, bits)
    grad_rows = lax.all_gather(out_grad_here, "tp", axis=0, tiled=True)

    pos_all = block_positions(pair_slot, group_rows // 2)
    pos_rows = lax.dynamic_slice_in_dim(pos_all, me * group_rows, group_rows)
    cosine, sine = rope_tables(pos_rows)

    inputs = x_all.astype(jnp.float32)
    factor_all = rms_scale(inputs)
    attn_in = (inputs * factor_all * g_attn).astype(jnp.bfloat16)
    queries, kv = project_qkv(attn_in, qkv_w, cosine, sine, width_q, width_k)
    kv_all = jnp.concatenate(gather_ctx(kv, bits), axis=0)
    attended, exact, log_total = attend_forward(pair_slot, place, queries, kv_all, bits)

    attended_all = lax.all_gather(attended, "tp", axis=0)
    residual = inputs + to_features([attended_all], [[part] for part in o_w], jnp.float32)
    factor_mlp_all = rms_scale(residual)
    mlp_in = (residual * factor_mlp_all * g_mlp).astype(jnp.bfloat16)
    residual_here = lax.dynamic_slice_in_dim(residual, tp * local_rows, local_rows)
    factor_mlp = lax.dynamic_slice_in_dim(factor_mlp_all, tp * local_rows, local_rows)
    normed_mlp = residual_here * factor_mlp

    hidden, grad_gate, grad_up = mlp_inner(mlp_in, grad_rows, gate_w, up_w, down_w)
    grad_mlp_part = to_features(
        [grad_gate[None], grad_up[None]],
        [[gate[None], up[None]] for gate, up in zip(gate_w, up_w)],
        jnp.bfloat16,
    )
    grad_mlp_in = lax.psum_scatter(
        grad_mlp_part, "tp", scatter_dimension=0, tiled=True
    ).astype(jnp.float32)
    mlp_part = to_features([hidden[None]], [[down[None]] for down in down_w], jnp.bfloat16)
    mlp_out = lax.psum_scatter(mlp_part, "tp", scatter_dimension=0, tiled=True)
    block_out = (residual_here + mlp_out.astype(jnp.float32)).astype(jnp.bfloat16)
    sum_gate_w = scatter_ctx(weight_gradient(mlp_in, grad_gate, count), bits)
    sum_up_w = scatter_ctx(weight_gradient(mlp_in, grad_up, count), bits)
    sum_down_w = scatter_ctx(weight_gradient(grad_rows, hidden, count), bits)

    gain_mlp_part = jnp.sum(grad_mlp_in * normed_mlp, axis=0, keepdims=True)
    grad_residual = out_grad_here.astype(jnp.float32) + norm_back(
        grad_mlp_in * g_mlp, normed_mlp, factor_mlp
    )
    branch_here = grad_residual.astype(jnp.bfloat16)
    grad_groups = to_groups(place, branch_here, o_w)
    grad_parts = jnp.stack(
        [grad_groups[0]]
        + [
            lax.ppermute(grad_groups[d], "tp", [(i, (i + d) % shifts) for i in range(shifts)])
            for d in range(1, shifts)
        ]
    )
    grad_queries, grad_kv = attend_backward(
        pair_slot, place, queries, kv_all, grad_parts, exact, log_total, cosine, sine, bits
    )
    branch_rows = lax.all_gather(branch_here, "tp", axis=0, tiled=True)
    sum_o_w = scatter_ctx(weight_gradient(branch_rows, attended, count), bits)

    grad_kv_pieces = scatter_pieces(jnp.split(grad_kv, count, axis=0), bits)
    grad_qkv = join_grad_qkv(grad_queries, grad_kv_pieces, cosine, sine)
    grad_attn_part = to_features(
        [grad_qkv[None]], [[part[None]] for part in qkv_w], jnp.bfloat16
    )
    grad_attn_in = lax.psum_scatter(
        grad_attn_part, "tp", scatter_dimension=0, tiled=True
    ).astype(jnp.float32)
    sum_qkv_w = scatter_ctx(weight_gradient(attn_in, grad_qkv, count), bits)
    gain_attn_part = jnp.sum(
        grad_attn_part.astype(jnp.float32) * (inputs * factor_all), axis=0, keepdims=True
    )
    gain_parts = to_absolute(jnp.concatenate([gain_attn_part, gain_mlp_part]), me, bits)
    gain_sums = lax.psum(gain_parts, ("ctx", "tp"))
    gain_width = gain_attn.shape[0]
    gain_here = lax.dynamic_slice_in_dim(gain_sums, me * gain_width, gain_width, 1)

    inputs_here = rows_here.astype(jnp.float32)
    factor_attn = lax.dynamic_slice_in_dim(factor_all, tp * local_rows, local_rows)
    input_grad = grad_residual + norm_back(
        grad_attn_in * g_attn, inputs_here * factor_attn, factor_attn
    )
    return (
        to_absolute(block_out, me, bits),
        to_absolute(input_grad, me, bits),
        gain_here[0],
        sum_qkv_w[:, :width_q],
        sum_qkv_w[:, width_q : width_q + width_k],
        sum_qkv_w[:, width_q + width_k :],
        sum_o_w,
        gain_here[1],
        sum_gate_w,
        sum_up_w,
        sum_down_w,
    )


def solution(mesh):
    placed = (
        P(("ctx", "tp"), None),
        P(("ctx", "tp"), None),
        P(),
        P("ctx"),
        P("ctx", "tp"),
        P("ctx", "tp"),
        P("ctx", "tp"),
        P("ctx", "tp"),
        P("ctx"),
        P("ctx", "tp"),
        P("ctx", "tp"),
        P("ctx", "tp"),
    )
    return jax.shard_map(
        on_device,
        mesh=mesh,
        in_specs=placed,
        out_specs=(
            P(("ctx", "tp"), None),
            P(("ctx", "tp"), None),
            P("ctx"),
            P("ctx", "tp"),
            P("ctx", "tp"),
            P("ctx", "tp"),
            P("ctx", "tp"),
            P("ctx"),
            P("ctx", "tp"),
            P("ctx", "tp"),
            P("ctx", "tp"),
        ),
        check_vma=False,
    )
```

```python
import functools
import math

import jax
import jax.numpy as jnp
from jax import lax
from jax.experimental import pallas as pl
from jax.experimental.pallas import tpu as pltpu
from jax.sharding import PartitionSpec as P

HEAD_SIZE = 64
LANES = 128
KERNEL_VMEM = 56 * 1024 * 1024

eps_norm = 1e-05
big_negative = -1e30

in_smem = pl.BlockSpec(memory_space=pltpu.SMEM)
in_vmem = pl.BlockSpec(memory_space=pltpu.VMEM)
unread = pl.BlockSpec(memory_space=pl.ANY)


def kernel_params():
    return pltpu.CompilerParams(vmem_limit_bytes=KERNEL_VMEM)


def cost(micros):
    return pl.CostEstimate(flops=int(micros * 1.1e9), bytes_accessed=1024, transcendentals=0)


def gated(value, *others):
    return pl.pallas_call(
        lambda *refs: None,
        out_shape=jax.ShapeDtypeStruct(value.shape, value.dtype),
        in_specs=[unread] * (1 + len(others)),
        out_specs=unread,
        input_output_aliases={0: 0},
        cost_estimate=cost(0.1),
        name="gated",
    )(value, *others)


def bit_order(bits):
    return [1, 2, 0] + list(range(3, bits)) if bits >= 3 else list(range(bits))


def block_key(position, bits):
    key = 0
    for place, bit in enumerate(bit_order(bits)):
        key = key | (((position >> place) & 1) << bit)
    return key


def key_position(key, bits):
    position = 0
    for place, bit in enumerate(bit_order(bits)):
        position = position | (((key >> bit) & 1) << place)
    return position


def swap(array, bit, bits):
    return lax.ppermute(array, "ctx", [(i, i ^ (1 << bit)) for i in range(1 << bits)])


def halves(array, axis):
    middle = array.shape[axis] // 2
    return (
        lax.slice_in_dim(array, 0, middle, axis=axis),
        lax.slice_in_dim(array, middle, 2 * middle, axis=axis),
    )


def gather_one(own, bits):
    first, second = bit_order(bits)[:2]
    return swap(own, first, bits), swap(own, second, bits)


def gather_two(one, bits, axis=0):
    first, second = bit_order(bits)[:2]
    lower, upper = halves(one[0], axis)[0], halves(one[1], axis)[1]
    return swap(lower, second, bits), swap(upper, first, bits)


def join(pieces, axis=0):
    shape = list(pieces[0].shape)
    shape[axis] = sum(piece.shape[axis] for piece in pieces)

    def kernel(*refs):
        in_refs, out_ref, sems = refs[: len(pieces)], refs[len(pieces)], refs[-1]
        copies, start = [], 0
        for index, in_ref in enumerate(in_refs):
            size = in_ref.shape[axis]
            place = pl.ds(start, size)
            target = out_ref.at[(slice(None),) * axis + (place,)]
            copies.append(pltpu.make_async_copy(in_ref, target, sems.at[index]))
            start += size
        for copy in copies:
            copy.start()
        for copy in copies:
            copy.wait()

    return pl.pallas_call(
        kernel,
        out_shape=jax.ShapeDtypeStruct(shape, pieces[0].dtype),
        in_specs=[unread] * len(pieces),
        out_specs=in_vmem,
        scratch_shapes=[pltpu.SemaphoreType.DMA((len(pieces),))],
        compiler_params=kernel_params(),
        cost_estimate=cost(0.1),
        name="join",
    )(*pieces)


def gather_end(own, one, two, bits, axis=0):
    parts = [join([own, *one, *two], axis)]
    for bit in bit_order(bits)[2:]:
        parts = parts + [swap(part, bit, bits) for part in parts]
    return parts


def gather_small(own, bits):
    stacked = own[None]
    for bit in bit_order(bits):
        stacked = jnp.concatenate([stacked, swap(stacked, bit, bits)], axis=0)
    return stacked


def scatter_step(stacked, bit, bits):
    kept = stacked.shape[0] // 2
    return stacked[:kept] + swap(stacked[kept:], bit, bits)


def sum_small(array, axis):
    size = lax.axis_size(axis)
    shift = 1
    while shift < size:
        array = array + lax.ppermute(array, axis, [(i, i ^ shift) for i in range(size)])
        shift *= 2
    return array


def add_half(left, right):
    return (left.astype(jnp.float32) + right.astype(jnp.float32)).astype(jnp.bfloat16)


def scatter_one(blocks, bits):
    first, second = bit_order(bits)[:2]
    return swap(blocks[3], second, bits), swap(blocks[4], first, bits)


def scatter_two(blocks, one):
    rows, width = blocks[1].shape
    half = rows // 2

    def kernel(first_ref, second_ref, lower_ref, upper_ref, to_first, to_second):
        to_first[0:half, :] = add_half(first_ref[0:half, :], lower_ref[...])
        to_first[half:, :] = first_ref[half:, :]
        to_second[0:half, :] = second_ref[0:half, :]
        to_second[half:, :] = add_half(second_ref[half:, :], upper_ref[...])

    return pl.pallas_call(
        kernel,
        out_shape=[jax.ShapeDtypeStruct((rows, width), jnp.bfloat16)] * 2,
        in_specs=[in_vmem] * 4,
        out_specs=[in_vmem] * 2,
        compiler_params=kernel_params(),
        cost_estimate=cost(0.1),
        name="scatter_two",
    )(blocks[1], blocks[2], *one)


def scatter_three(two, bits):
    first, second = bit_order(bits)[:2]
    return swap(two[0], first, bits), swap(two[1], second, bits)


def finish_sum(blocks, three):
    rows, width = blocks[0].shape

    def kernel(own_ref, first_ref, second_ref, out_ref):
        total = own_ref[...].astype(jnp.float32) + first_ref[...].astype(jnp.float32)
        out_ref[...] = total + second_ref[...].astype(jnp.float32)

    return pl.pallas_call(
        kernel,
        out_shape=jax.ShapeDtypeStruct((rows, width), jnp.float32),
        in_specs=[in_vmem] * 3,
        out_specs=in_vmem,
        compiler_params=kernel_params(),
        cost_estimate=cost(0.1),
        name="finish_sum",
    )(blocks[0], *three)


def scatter_step(stacked, bit, bits):
    kept = stacked.shape[0] // 2
    return stacked[:kept] + swap(stacked[kept:], bit, bits)


def sum_small(array, axis):
    size = lax.axis_size(axis)
    shift = 1
    while shift < size:
        array = array + lax.ppermute(array, axis, [(i, i ^ shift) for i in range(size)])
        shift *= 2
    return array


def tp_shift(array, distance):
    size = lax.axis_size("tp")
    return lax.ppermute(array, "tp", [(i, (i + distance) % size) for i in range(size)])


def tp_gather(array):
    return [array] + [tp_shift(array, d) for d in range(1, lax.axis_size("tp"))]


def tp_ordered(pieces, tp):
    stacked = jnp.stack(pieces)
    count = len(pieces)
    return jnp.concatenate(
        [lax.dynamic_index_in_dim(stacked, (tp - j) % count, 0, keepdims=False) for j in range(count)]
    )


def tp_exchange(array):
    return [array[0]] + [tp_shift(array[d], d) for d in range(1, array.shape[0])]


def tp_sum(pieces):
    return sum(piece.astype(jnp.float32) for piece in pieces)


def after(value, *others):
    return lax.optimization_barrier((value, *others))


def to_relative(array, me, bits):
    width = array.shape[1] // (1 << bits)
    return jnp.concatenate(
        [
            lax.dynamic_slice_in_dim(array, (me ^ block_key(p, bits)) * width, width, 1)
            for p in range(1 << bits)
        ],
        axis=1,
    )


def to_absolute(array, me, bits):
    width = array.shape[1] // (1 << bits)
    return jnp.concatenate(
        [
            lax.dynamic_slice_in_dim(array, key_position(me ^ c, bits) * width, width, 1)
            for c in range(1 << bits)
        ],
        axis=1,
    )


def reorder(place, array, bits, inverse=False):
    width = array.shape[1] // (1 << bits)
    if width % LANES:
        return (to_absolute if inverse else to_relative)(array, place[0], bits)

    def kernel(place, in_ref, out_ref):
        for p in range(1 << bits):
            other = pl.multiple_of((place[0] ^ block_key(p, bits)) * width, LANES)
            if inverse:
                out_ref[:, pl.ds(other, width)] = in_ref[:, p * width : (p + 1) * width]
            else:
                out_ref[:, p * width : (p + 1) * width] = in_ref[:, pl.ds(other, width)]

    return pl.pallas_call(
        kernel,
        out_shape=jax.ShapeDtypeStruct(array.shape, array.dtype),
        in_specs=[in_smem, in_vmem],
        out_specs=in_vmem,
        compiler_params=kernel_params(),
        cost_estimate=cost(0.1),
        name="reorder",
    )(place, array)


def block_positions(pair_slot, block_len):
    pair_count = pair_slot.shape[0]
    offsets = jnp.arange(2 * block_len, dtype=jnp.int32)
    lower_half = offsets < block_len
    block_index = jnp.where(
        lower_half[None, :], pair_slot[:, None], 2 * pair_count - 1 - pair_slot[:, None]
    )
    return (block_index * block_len + (offsets % block_len)[None, :]).reshape(-1)


def inverse_freqs(head_dim):
    exponent = jnp.arange(0, head_dim, 2).astype(jnp.float32) / head_dim
    base_freq = 500000.0 ** (-exponent)
    wavelength = 2.0 * math.pi / base_freq
    smooth = (8192.0 / wavelength - 1.0) / 3.0
    blended = (1.0 - smooth) * base_freq / 32.0 + smooth * base_freq
    scaled = jnp.where(wavelength > 8192.0, base_freq / 32.0, base_freq)
    middle = (wavelength >= 2048.0) & (wavelength <= 8192.0)
    return jnp.where(middle, blended, scaled)


def rope_tables(positions):
    angles = positions.astype(jnp.float32)[:, None] * inverse_freqs(HEAD_SIZE)[None, :]
    wide = LANES // (HEAD_SIZE // 2)
    return (jnp.tile(jnp.cos(angles), (1, wide)), jnp.tile(jnp.sin(angles), (1, wide)))


def rms_scale(values):
    return lax.rsqrt(jnp.mean(values * values, axis=-1, keepdims=True) + eps_norm)


def norm_back(gradient, normed, factor):
    return factor * (gradient - normed * jnp.mean(gradient * normed, axis=-1, keepdims=True))


def inner_rows(left, right):
    return lax.dot_general(
        left, right, (((0,), (0,)), ((), ())), preferred_element_type=jnp.float32
    )


def nt(left, right):
    return lax.dot_general(
        left, right, (((1,), (1,)), ((), ())), preferred_element_type=jnp.float32
    )


def nn(left, right):
    return lax.dot_general(
        left, right, (((1,), (0,)), ((), ())), preferred_element_type=jnp.float32
    )


def turned_lanes(values):
    half = HEAD_SIZE // 2
    lane = lax.broadcasted_iota(jnp.int32, values.shape, 1)
    up = pltpu.roll(values, LANES - half, 1)
    down = pltpu.roll(values, half, 1)
    return jnp.where(lane % HEAD_SIZE < half, -up, down)


def rotate(values, cosine, sine):
    return values * cosine + turned_lanes(values) * sine


def rotate_back(gradient, cosine, sine):
    return gradient * cosine - turned_lanes(gradient * sine)


def norm_rows(place, rows, gain, bits):
    width = rows.shape[1] // (1 << bits)
    whole_lanes = width % LANES == 0
    if not whole_lanes:
        rows = to_relative(rows, place[0], bits)

    def kernel(place, in_ref, gain_ref, rows_ref, out_ref):
        for p in range(1 << bits):
            here = slice(p * width, (p + 1) * width)
            if whole_lanes:
                other = pl.multiple_of((place[0] ^ block_key(p, bits)) * width, LANES)
                rows_ref[:, here] = in_ref[:, pl.ds(other, width)]
        if not whole_lanes:
            rows_ref[...] = in_ref[...]
        values = rows_ref[...].astype(jnp.float32)
        out_ref[...] = (values * rms_scale(values) * gain_ref[...]).astype(jnp.bfloat16)

    shape = jax.ShapeDtypeStruct(rows.shape, jnp.bfloat16)
    return pl.pallas_call(
        kernel,
        out_shape=(shape, shape),
        in_specs=[in_smem, in_vmem, in_vmem],
        out_specs=(in_vmem, in_vmem),
        compiler_params=kernel_params(),
        cost_estimate=cost(0.1),
        name="norm_rows",
    )(place, rows, gain)


def qkv_kernel(count, x_ref, *refs):
    weights, (cos_ref, sin_ref), (q_ref, kv_ref) = refs[:count], refs[count : count + 2], refs[-2:]
    depth = x_ref.shape[1] // count
    width_q = q_ref.shape[1]
    width_k = kv_ref.shape[1] // 2
    total = width_q + 2 * width_k
    tile = 2 * LANES
    for start in range(0, total, tile):
        product = 0.0
        for index, weight in enumerate(weights):
            product = product + nn(
                x_ref[:, index * depth : (index + 1) * depth], weight[:, start : start + tile]
            )
        for offset in range(0, tile, LANES):
            at = start + offset
            piece = product[:, offset : offset + LANES]
            if at < width_q + width_k:
                piece = rotate(piece, cos_ref[...], sin_ref[...])
            piece = piece.astype(jnp.bfloat16)
            if at < width_q:
                q_ref[:, at : at + LANES] = piece
            else:
                kv_ref[:, at - width_q : at - width_q + LANES] = piece


def project_qkv(attn_in, weights, cosine, sine, width_q, width_k, after=()):
    rows, depth = attn_in.shape
    return pl.pallas_call(
        functools.partial(qkv_kernel, len(weights)),
        out_shape=(
            jax.ShapeDtypeStruct((rows, width_q), jnp.bfloat16),
            jax.ShapeDtypeStruct((rows, 2 * width_k), jnp.bfloat16),
        ),
        in_specs=[in_vmem] * (3 + len(weights)) + [unread] * len(after),
        out_specs=(in_vmem, in_vmem),
        compiler_params=kernel_params(),
        cost_estimate=cost(0.1),
        name="qkv",
    )(attn_in, *weights, cosine, sine, *after)


def sequence_block(slots, me, half_block, bits):
    slot = slots[me ^ block_key(half_block // 2, bits)]
    return jnp.where(half_block % 2 == 0, slot, 2 * (1 << bits) - 1 - slot)


def head_lanes(pair, head, heads_per_kv, scale):
    wide = pair.astype(jnp.float32) * scale
    group = head // heads_per_kv
    source = wide if head % 2 == group else pltpu.roll(wide, HEAD_SIZE, 1)
    low = lax.broadcasted_iota(jnp.int32, wide.shape, 1) < HEAD_SIZE
    keep = low if group == 0 else jnp.logical_not(low)
    return jnp.where(keep, source, 0.0).astype(jnp.bfloat16)


def causal_tile(size):
    key_at = lax.broadcasted_iota(jnp.int32, (size, size), 0)
    row_at = lax.broadcasted_iota(jnp.int32, (size, size), 1)
    return key_at <= row_at


def over_blocks(visit, slots, me, bits, half, prepare):
    visit(0, 0, True, True, True)
    visit(1, half, True, True, True)
    visit(1, 0, False, False, False)
    own = slots[me]
    blocks_of_query = (own, 2 * (1 << bits) - 1 - own)

    def step(index, carry):
        block = sequence_block(slots, me, index, bits)
        start = pl.multiple_of(index * half, half)
        prepare(start)
        for q_half in range(2):

            @pl.when(block < blocks_of_query[q_half])
            def _():
                visit(q_half, start, False, False, False)

        return carry

    lax.fori_loop(2, 2 * (1 << bits), step, 0)


def forward_kernel(bits, heads, slots, place, q_ref, kv_ref, *refs):
    out_ref, exact_ref, log_ref, qp, run_max, run_sum, acc = refs[-7:]
    rows = q_ref.shape[0]
    half = rows // 2
    per_kv = heads // 2
    for head in range(heads):
        lanes = pl.ds((head // 2) * LANES, LANES)
        qp[head] = head_lanes(q_ref[:, lanes], head, per_kv, HEAD_SIZE ** (-0.5))

    def visit(q_half, key_start, diagonal, first, _):
        keys = kv_ref[pl.ds(key_start, half), 0:LANES]
        values_t = kv_ref[pl.ds(key_start, half), LANES : 2 * LANES].T
        base = q_half * heads
        span = pl.ds(q_half * half, half)
        scores = [nt(keys, qp[head, span, :]) for head in range(heads)]
        if diagonal:
            visible = causal_tile(half)
            scores = [jnp.where(visible, score, big_negative) for score in scores]
        peaks = [jnp.max(score, axis=0, keepdims=True) for score in scores]
        if not first:
            before = [run_max[base + head] for head in range(heads)]
            peaks = [jnp.maximum(peak, old) for peak, old in zip(peaks, before)]
        weights = [jnp.exp(score - peak) for score, peak in zip(scores, peaks)]
        totals = [jnp.sum(weight, axis=0, keepdims=True) for weight in weights]
        outs = []
        for head, weight in enumerate(weights):
            group = head // per_kv
            some = values_t[group * HEAD_SIZE : (group + 1) * HEAD_SIZE]
            outs.append(nn(some, weight.astype(jnp.bfloat16)))
        if not first:
            fades = [jnp.exp(old - peak) for old, peak in zip(before, peaks)]
            totals = [t + run_sum[base + h] * f for h, (t, f) in enumerate(zip(totals, fades))]
            outs = [o + acc[base + h] * f for h, (o, f) in enumerate(zip(outs, fades))]
        for head in range(heads):
            run_max[base + head] = peaks[head]
            run_sum[base + head] = totals[head]
            acc[base + head] = outs[head]

    over_blocks(visit, slots, place[0], bits, half, lambda start: None)
    for q_half in range(2):
        span = pl.ds(q_half * half, half)
        for pair in range(heads // 2):
            parts = []
            for head in (2 * pair, 2 * pair + 1):
                slot = q_half * heads + head
                parts.append(acc[slot] / run_sum[slot])
                log_ref[pl.ds(head, 1), span] = run_max[slot] + jnp.log(run_sum[slot])
            exact = jnp.concatenate(parts, axis=0).T
            exact_ref[span, pl.ds(pair * LANES, LANES)] = exact
            out_ref[span, pl.ds(pair * LANES, LANES)] = exact.astype(jnp.bfloat16)


def attend_forward(slots, place, queries, kv, bits, after=()):
    rows, width = queries.shape
    heads = width // HEAD_SIZE
    half = rows // 2
    return pl.pallas_call(
        functools.partial(forward_kernel, bits, heads),
        out_shape=(
            jax.ShapeDtypeStruct((rows, width), jnp.bfloat16),
            jax.ShapeDtypeStruct((rows, width), jnp.float32),
            jax.ShapeDtypeStruct((heads, rows), jnp.float32),
        ),
        in_specs=[in_smem, in_smem, in_vmem, in_vmem] + [unread] * len(after),
        out_specs=(in_vmem, in_vmem, in_vmem),
        scratch_shapes=[
            pltpu.VMEM((heads, rows, LANES), jnp.bfloat16),
            pltpu.VMEM((2 * heads, 1, half), jnp.float32),
            pltpu.VMEM((2 * heads, 1, half), jnp.float32),
            pltpu.VMEM((2 * heads, HEAD_SIZE, half), jnp.float32),
        ],
        compiler_params=kernel_params(),
        cost_estimate=cost(19),
        name="attention_forward",
    )(slots, place, queries, kv, *after)


def backward_kernel(bits, heads, slots, place, *refs):
    q_ref, kv_ref, do_ref, exact_ref, log_ref, cos_ref, sin_ref = refs[:7]
    parts = max(1, (1 << bits) // 4)
    dq_ref, dkv_refs = refs[-7 - parts], refs[-6 - parts : -6]
    qp, dop, dots, dq_acc, dkv_acc, do_all = refs[-6:]
    rows = q_ref.shape[0]
    half = rows // 2
    per_kv = heads // 2
    shifts, local, _ = do_ref.shape
    for shift in range(shifts):
        source = lax.rem(place[1] - shift + shifts, shifts)
        do_all[pl.ds(pl.multiple_of(source * local, local), local), :] = do_ref[shift]
    for head in range(heads):
        lanes = pl.ds((head // 2) * LANES, LANES)
        qp[head] = head_lanes(q_ref[:, lanes], head, per_kv, HEAD_SIZE ** (-0.5))
        dop[head] = head_lanes(do_all[:, lanes], head, per_kv, 1.0)
    for pair in range(heads // 2):
        lanes = pl.ds(pair * LANES, LANES)
        product = (do_all[:, lanes].astype(jnp.float32) * exact_ref[:, lanes]).T
        dots[pl.ds(2 * pair, 1), :] = jnp.sum(product[:HEAD_SIZE], axis=0, keepdims=True)
        dots[pl.ds(2 * pair + 1, 1), :] = jnp.sum(product[HEAD_SIZE:], axis=0, keepdims=True)

    def clear(start):
        dkv_acc[pl.ds(start, half), :] = jnp.zeros((half, 2 * LANES), jnp.float32)

    def visit(q_half, key_start, diagonal, first_query, first_key):
        rows_of_key = pl.ds(key_start, half)
        keys = kv_ref[rows_of_key, 0:LANES]
        values = kv_ref[rows_of_key, LANES : 2 * LANES]
        keys_t = keys.T
        base = q_half * heads
        span = pl.ds(q_half * half, half)
        q_heads = [qp[head, span, :] for head in range(heads)]
        do_heads = [dop[head, span, :] for head in range(heads)]
        scores = [nt(keys, q_head) for q_head in q_heads]
        grad_ws = [nt(values, do_head) for do_head in do_heads]
        weights = [
            jnp.exp(score - log_ref[pl.ds(head, 1), span]) for head, score in enumerate(scores)
        ]
        if diagonal:
            visible = causal_tile(half)
            weights = [jnp.where(visible, weight, 0.0) for weight in weights]
        grad_ss = [
            (weight * (grad_w - dots[pl.ds(head, 1), span])).astype(jnp.bfloat16)
            for head, (weight, grad_w) in enumerate(zip(weights, grad_ws))
        ]
        weights = [weight.astype(jnp.bfloat16) for weight in weights]
        grad_v = jnp.zeros((half, LANES), jnp.float32)
        grad_k = jnp.zeros((half, LANES), jnp.float32)
        for weight, do_head in zip(weights, do_heads):
            grad_v = grad_v + nn(weight, do_head)
        for grad_s, q_head in zip(grad_ss, q_heads):
            grad_k = grad_k + nn(grad_s, q_head)
        for head, grad_s in enumerate(grad_ss):
            group = head // per_kv
            grad_q = nn(keys_t[group * HEAD_SIZE : (group + 1) * HEAD_SIZE], grad_s)
            if not first_query:
                grad_q = grad_q + dq_acc[base + head]
            dq_acc[base + head] = grad_q
        if not first_key:
            grad_k = grad_k + dkv_acc[rows_of_key, 0:LANES]
            grad_v = grad_v + dkv_acc[rows_of_key, LANES : 2 * LANES]
        dkv_acc[rows_of_key, 0:LANES] = grad_k
        dkv_acc[rows_of_key, LANES : 2 * LANES] = grad_v

    over_blocks(visit, slots, place[0], bits, half, clear)
    size = dkv_acc.shape[0] // parts
    for part, dkv_ref in enumerate(dkv_refs):
        dkv_ref[...] = dkv_acc[part * size : (part + 1) * size, :].astype(jnp.bfloat16)
    for q_half in range(2):
        span = pl.ds(q_half * half, half)
        for pair in range(heads // 2):
            slot = q_half * heads + 2 * pair
            gradient = jnp.concatenate([dq_acc[slot], dq_acc[slot + 1]], axis=0).T
            gradient = rotate_back(
                gradient * HEAD_SIZE ** (-0.5), cos_ref[span, :], sin_ref[span, :]
            )
            dq_ref[span, pl.ds(pair * LANES, LANES)] = gradient.astype(jnp.bfloat16)


def attend_backward(
    slots, place, queries, kv, grad_parts, exact, log_total, cosine, sine, bits, after=()
):
    parts = max(1, (1 << bits) // 4)
    rows, width = queries.shape
    heads = width // HEAD_SIZE
    half = rows // 2
    return pl.pallas_call(
        functools.partial(backward_kernel, bits, heads),
        out_shape=(
            jax.ShapeDtypeStruct((rows, width), jnp.bfloat16),
            *[jax.ShapeDtypeStruct((kv.shape[0] // parts, kv.shape[1]), jnp.bfloat16)] * parts,
        ),
        in_specs=[in_smem, in_smem] + [in_vmem] * 7 + [unread] * len(after),
        out_specs=(in_vmem,) * (1 + parts),
        scratch_shapes=[
            pltpu.VMEM((heads, rows, LANES), jnp.bfloat16),
            pltpu.VMEM((heads, rows, LANES), jnp.bfloat16),
            pltpu.VMEM((heads, rows), jnp.float32),
            pltpu.VMEM((2 * heads, HEAD_SIZE, half), jnp.float32),
            pltpu.VMEM(kv.shape, jnp.float32),
            pltpu.VMEM((rows, width), jnp.bfloat16),
        ],
        compiler_params=kernel_params(),
        cost_estimate=cost(30),
        name="attention_backward",
    )(slots, place, queries, kv, grad_parts, exact, log_total, cosine, sine, *after)


def grad_qkv_kernel(dq_ref, own_ref, first_ref, second_ref, cos_ref, sin_ref, out_ref):
    width_q = dq_ref.shape[1]
    out_ref[:, 0:width_q] = dq_ref[...]
    total = own_ref[...].astype(jnp.float32) + first_ref[...].astype(jnp.float32)
    total = total + second_ref[...].astype(jnp.float32)
    keys = rotate_back(total[:, 0:LANES], cos_ref[...], sin_ref[...])
    out_ref[:, width_q : width_q + LANES] = keys.astype(jnp.bfloat16)
    out_ref[:, width_q + LANES :] = total[:, LANES:].astype(jnp.bfloat16)


def join_grad_qkv(grad_queries, pieces, cosine, sine):
    rows, width_q = grad_queries.shape
    width = width_q + pieces[0].shape[1]
    return pl.pallas_call(
        grad_qkv_kernel,
        out_shape=jax.ShapeDtypeStruct((rows, width), jnp.bfloat16),
        in_specs=[in_vmem] * 6,
        out_specs=in_vmem,
        compiler_params=kernel_params(),
        cost_estimate=cost(0.1),
        name="grad_qkv",
    )(grad_queries, *pieces, cosine, sine)


def mlp_kernel(count, x_ref, g_ref, *refs):
    weights = refs[:count], refs[count : 2 * count], refs[2 * count : 3 * count]
    hidden_ref, grad_gate_ref, grad_up_ref = refs[3 * count :]
    depth = x_ref.shape[1] // count

    def product(left, parts):
        total = 0.0
        for index, part in enumerate(parts):
            total = total + nn(left[:, index * depth : (index + 1) * depth], part[...])
        return total

    gate = product(x_ref, weights[0])
    up = product(x_ref, weights[1])
    grad_hidden = product(g_ref, weights[2])
    sigmoid = jax.nn.sigmoid(gate)
    silu = gate * sigmoid
    hidden_ref[...] = (silu * up).astype(jnp.bfloat16)
    grad_gate = grad_hidden * up * sigmoid * (1.0 + gate * (1.0 - sigmoid))
    grad_gate_ref[...] = grad_gate.astype(jnp.bfloat16)
    grad_up_ref[...] = (grad_hidden * silu).astype(jnp.bfloat16)


def mlp_inner(mlp_in, grad_rows, gates, ups, downs):
    rows, depth = mlp_in.shape
    units = gates[0].shape[1]
    count = len(gates)
    tile = min(256, units)
    whole = pl.BlockSpec((rows, depth), lambda i: (0, 0))
    part = pl.BlockSpec((depth // count, tile), lambda i: (0, i))
    out = pl.BlockSpec((rows, tile), lambda i: (0, i))
    shape = jax.ShapeDtypeStruct((rows, units), jnp.bfloat16)
    return pl.pallas_call(
        functools.partial(mlp_kernel, count),
        grid=(units // tile,),
        out_shape=(shape, shape, shape),
        in_specs=[whole, whole] + [part] * (3 * count),
        out_specs=(out, out, out),
        compiler_params=kernel_params(),
        cost_estimate=cost(0.1),
        name="mlp_inner",
    )(mlp_in, grad_rows, *gates, *ups, *downs)


def project_part(lefts, part):
    depth, rows, width = lefts.shape
    features = part.shape[1]
    tile = min(256, features)

    def kernel(left_ref, part_ref, out_ref):
        total = 0.0
        for group in range(depth):
            total = total + nt(left_ref[group], part_ref[group])
        out_ref[...] = total

    return pl.pallas_call(
        kernel,
        grid=(features // tile,),
        out_shape=jax.ShapeDtypeStruct((rows, features), jnp.float32),
        in_specs=[
            pl.BlockSpec((depth, rows, width), lambda i: (0, 0, 0)),
            pl.BlockSpec((depth, tile, width), lambda i: (0, i, 0)),
        ],
        out_specs=pl.BlockSpec((rows, tile), lambda i: (0, i)),
        compiler_params=kernel_params(),
        cost_estimate=cost(0.1),
        name="project_part",
    )(lefts, part)


def residual_kernel(place, left_ref, x_ref, gain_ref, part_ref, *refs):
    sums, (mlp_ref, here_ref, residual) = refs[:-3], refs[-3:]
    depth, rows, _ = left_ref.shape
    tile = part_ref.shape[1]
    step = pl.program_id(0)
    total = 0.0
    for group in range(depth):
        total = total + nt(left_ref[group], part_ref[group])
    residual[step] = total

    @pl.when(step == pl.num_programs(0) - 1)
    def _():
        width = x_ref.shape[1]
        before = sum(ref.shape[1] for ref in sums)
        squares = jnp.zeros((rows, 1), jnp.float32)
        pieces = []
        for ref in sums:
            pieces += [(ref, slice(k, k + tile)) for k in range(0, ref.shape[1], tile)]
        count = (width - before) // tile
        local = rows // depth
        here = pl.ds(pl.multiple_of(place[1] * local, local), local)
        for index in range(width // tile):
            columns = slice(index * tile, (index + 1) * tile)
            values = x_ref[:, columns].astype(jnp.float32)
            if index < len(pieces):
                ref, at = pieces[index]
                values = values + ref[:, at]
                ref[:, at] = values
            else:
                values = values + residual[index - len(pieces)]
                residual[index - len(pieces)] = values
            squares = squares + jnp.sum(values * values, axis=1, keepdims=True)
        factor = lax.rsqrt(squares / width + eps_norm)
        for index in range(width // tile):
            columns = slice(index * tile, (index + 1) * tile)
            if index < len(pieces):
                ref, at = pieces[index]
                values, mine = ref[:, at], ref[here, at]
            else:
                values = residual[index - len(pieces)]
                mine = residual[index - len(pieces), here, :]
            mlp_ref[:, columns] = (values * factor * gain_ref[:, columns]).astype(jnp.bfloat16)
            here_ref[:, columns] = mine


def project_residual(place, lefts, rows, gain, parts):
    depth, count, width = lefts.shape
    total = rows.shape[1]
    sums = [project_part(lefts, part) for part in parts[:-1]]
    features = parts[-1].shape[1]
    tile = min(256, features)
    whole = lambda i: (0, 0)
    return pl.pallas_call(
        residual_kernel,
        grid=(features // tile,),
        out_shape=(
            jax.ShapeDtypeStruct((count, total), jnp.bfloat16),
            jax.ShapeDtypeStruct((count // depth, total), jnp.float32),
        ),
        in_specs=[
            in_smem,
            pl.BlockSpec((depth, count, width), lambda i: (0, 0, 0)),
            pl.BlockSpec((count, total), whole),
            pl.BlockSpec((1, total), whole),
            pl.BlockSpec((depth, tile, width), lambda i: (0, i, 0)),
        ]
        + [pl.BlockSpec(each.shape, whole) for each in sums],
        out_specs=(
            pl.BlockSpec((count, total), whole),
            pl.BlockSpec((count // depth, total), whole),
        ),
        scratch_shapes=[pltpu.VMEM((features // tile, count, tile), jnp.float32)],
        compiler_params=kernel_params(),
        cost_estimate=cost(0.1),
        name="project_residual",
    )(place, lefts, rows, gain, parts[-1], *sums)


def to_features(lefts, weights):
    rows = lefts[0].shape[0]
    count = len(weights[0])
    features = weights[0][0].shape[0]
    tile = min(256, features)
    tiles = features // tile

    def kernel(*refs):
        left_refs, part_refs, out_ref = refs[: len(lefts)], refs[len(lefts) : -1], refs[-1]
        step = pl.program_id(0)
        for part in range(count):

            @pl.when(step // tiles == part)
            def _():
                total = 0.0
                for source, left_ref in enumerate(left_refs):
                    total = total + nt(left_ref[...], part_refs[source * count + part][...])
                out_ref[...] = total.astype(jnp.bfloat16)

    def part_at(base, i):
        return (jnp.clip(i - base, 0, tiles - 1), 0)

    return pl.pallas_call(
        kernel,
        grid=(count * tiles,),
        out_shape=jax.ShapeDtypeStruct((rows, count * features), jnp.bfloat16),
        in_specs=[pl.BlockSpec(left.shape, lambda i: (0, 0)) for left in lefts]
        + [
            pl.BlockSpec((tile, parts[part].shape[1]), functools.partial(part_at, part * tiles))
            for parts in weights
            for part in range(count)
        ],
        out_specs=pl.BlockSpec((rows, tile), lambda i: (0, i)),
        compiler_params=kernel_params(),
        cost_estimate=cost(0.1),
        name="to_features",
    )(*lefts, *[part for parts in weights for part in parts])


def to_groups(place, branch, parts):
    rows, depth = branch.shape
    groups, features, width = parts[0].shape
    count = len(parts)

    def kernel(place, x_ref, *refs):
        total = 0.0
        for index, part in enumerate(refs[:count]):
            columns = x_ref[:, index * features : (index + 1) * features]
            total = total + nn(columns, part[0])
        refs[-1][0] = total.astype(jnp.bfloat16)

    def weight_at(shift, place):
        return (lax.rem(place[1] + shift, groups), 0, 0)

    return pl.pallas_call(
        kernel,
        grid_spec=pltpu.PrefetchScalarGridSpec(
            num_scalar_prefetch=1,
            grid=(groups,),
            in_specs=[pl.BlockSpec((rows, depth), lambda i, place: (0, 0))]
            + [pl.BlockSpec((1, features, width), weight_at)] * count,
            out_specs=pl.BlockSpec((1, rows, width), lambda i, place: (i, 0, 0)),
        ),
        out_shape=jax.ShapeDtypeStruct((groups, rows, width), jnp.bfloat16),
        compiler_params=kernel_params(),
        cost_estimate=cost(0.1),
        name="to_groups",
    )(place, branch, *parts)


def to_block_groups(place, rows, bits, groups):
    local, depth = rows.shape
    width = depth >> bits
    count = (1 << bits) // groups
    if width % LANES:
        blocks = to_absolute(rows, place[0], bits)
        blocks = blocks.reshape(local, groups, count, width).transpose(1, 2, 0, 3)
        return jnp.stack(
            [
                lax.dynamic_index_in_dim(blocks, (place[1] + d) % groups, 0, keepdims=False)
                for d in range(groups)
            ]
        )

    def kernel(place, in_ref, out_ref):
        for d in range(groups):
            for index in range(count):
                block = lax.rem(place[1] + d, groups) * count + index
                start = key_position(place[0] ^ block, bits) * width
                out_ref[d, index] = in_ref[:, pl.ds(pl.multiple_of(start, LANES), width)]

    return pl.pallas_call(
        kernel,
        out_shape=jax.ShapeDtypeStruct((groups, count, local, width), rows.dtype),
        in_specs=[in_smem, in_vmem],
        out_specs=in_vmem,
        compiler_params=kernel_params(),
        cost_estimate=cost(0.1),
        name="to_block_groups",
    )(place, rows)


def gradient_out(place, branch, attended, bits):
    shifts = len(branch)
    count, local, features = branch[0].shape
    groups, rows, width = attended.shape
    parts = (1 << bits) // 4

    def kernel(place, *refs):
        lefts, right_ref, outs = refs[:shifts], refs[shifts], refs[shifts + 1 :]
        step = pl.program_id(0)
        total = 0.0
        for distance, left in enumerate(lefts):
            start = lax.rem(place[1] - distance + shifts, shifts) * local
            here = pl.ds(pl.multiple_of(start, local), local)
            total = total + inner_rows(left[0], right_ref[0, here, :])
        for part, out_ref in enumerate(outs):

            @pl.when(step // 4 == part)
            def _():
                out_ref[...] = total.astype(jnp.bfloat16)

    def left_at(p, place):
        return (lax.rem(place[0] ^ block_key(p, bits), count), 0, 0)

    def right_at(p, place):
        return ((place[0] ^ block_key(p, bits)) // count, 0, 0)

    def out_at(base, p, place):
        return (jnp.clip(p - base, 0, 3), 0)

    return pl.pallas_call(
        kernel,
        grid_spec=pltpu.PrefetchScalarGridSpec(
            num_scalar_prefetch=1,
            grid=(1 << bits,),
            in_specs=[pl.BlockSpec((1, local, features), left_at)] * shifts
            + [pl.BlockSpec((1, rows, width), right_at)],
            out_specs=[
                pl.BlockSpec((features, width), functools.partial(out_at, 4 * part))
                for part in range(parts)
            ],
        ),
        out_shape=[jax.ShapeDtypeStruct((4 * features, width), jnp.bfloat16)] * parts,
        compiler_params=kernel_params(),
        cost_estimate=cost(0.1),
        name="gradient_out",
    )(place, *branch, attended)


def to_owners(array, count):
    ctx, tp = lax.axis_size("ctx"), lax.axis_size("tp")
    moves = []
    for c in range(ctx):
        for t in range(tp):
            moves.append((c * tp + t, (count * t + c % count) * tp + c // count))
    return lax.ppermute(array, ("ctx", "tp"), moves)


def block_rows(rows):
    quarter = rows // 4
    return [quarter, quarter, quarter, quarter // 2, quarter // 2]


def gradient_part(left, right, parts, part, received=()):
    rows, depth = left.shape
    depth = depth // parts
    width = right.shape[1]
    tile = next(t for t in (1024, 768, 512, 256, LANES, width) if width % t == 0)
    sizes = block_rows(depth) if received else [depth // 4] * 4
    step = depth // 4

    def kernel(left_ref, right_ref, *refs):
        total = inner_rows(left_ref[...], right_ref[...])
        start = 0
        for size, out_ref in zip(sizes, refs[len(received) :]):
            piece = total[start : start + size]
            if received:
                offset = start % step
                other = refs[start // step][offset : offset + size, :]
                piece = piece + other.astype(jnp.float32)
            out_ref[...] = piece.astype(jnp.bfloat16)
            start += size

    return pl.pallas_call(
        kernel,
        grid=(width // tile,),
        out_shape=[jax.ShapeDtypeStruct((size, width), jnp.bfloat16) for size in sizes],
        in_specs=[
            pl.BlockSpec((rows, depth), lambda i: (0, part)),
            pl.BlockSpec((rows, tile), lambda i: (0, i)),
        ]
        + [pl.BlockSpec((step, tile), lambda i: (0, i))] * len(received),
        out_specs=[pl.BlockSpec((size, tile), lambda i: (0, i)) for size in sizes],
        compiler_params=kernel_params(),
        cost_estimate=cost(0.1),
        name="gradient_part",
    )(left, right, *received)


def gradient_begin(left, right, bits):
    parts = (1 << bits) // 4
    bit = bit_order(bits)[-1]
    return [
        [swap(block, bit, bits) for block in gradient_part(left, right, parts, part)]
        for part in range(parts // 2, parts)
    ]


def gradient_end(left, right, received, bits):
    parts = (1 << bits) // 4
    if parts == 2:
        return gradient_part(left, right, parts, 0, received[0])
    kept = [jnp.concatenate(gradient_part(left, right, parts, p)) for p in range(parts // 2)]
    kept = [add_half(mine, jnp.concatenate(other)) for mine, other in zip(kept, received)]
    return sum_parts(kept, bits, bit_order(bits)[2:-1])


def sum_parts(parts, bits, over):
    for bit in reversed(over):
        count = len(parts) // 2
        came = [swap(part, bit, bits) for part in parts[count:]]
        if count == 1:
            return split_blocks(parts[0], came[0])
        parts = [add_half(mine, other) for mine, other in zip(parts[:count], came)]


def split_blocks(kept, received):
    sizes = block_rows(kept.shape[0])

    def kernel(kept_ref, other_ref, *refs):
        start = 0
        for size, out_ref in zip(sizes, refs):
            here = slice(start, start + size)
            out_ref[...] = add_half(kept_ref[here, :], other_ref[here, :])
            start += size

    return pl.pallas_call(
        kernel,
        out_shape=[jax.ShapeDtypeStruct((size, kept.shape[1]), jnp.bfloat16) for size in sizes],
        in_specs=[in_vmem] * 2,
        out_specs=[in_vmem] * 5,
        compiler_params=kernel_params(),
        cost_estimate=cost(0.1),
        name="split_blocks",
    )(kept, received)


def rows_begin(parts, bits):
    return sum_parts(parts, bits, bit_order(bits)[2:])


def window(*values):
    return lax.optimization_barrier(values)


def cut(values, *sizes):
    out, start = [], 0
    for size in sizes:
        out.append(values[start : start + size])
        start += size
    return out


def on_device(
    block_in, out_grad, pair_slot, gain_attn, wq, wk, wv, wo, gain_mlp, w_gate, w_up, w_down
):
    bits = (lax.axis_size("ctx") - 1).bit_length()
    shifts = lax.axis_size("tp")
    me = lax.axis_index("ctx")
    tp = lax.axis_index("tp")
    place = jnp.stack([me, tp]).astype(jnp.int32)
    local_rows, model = block_in.shape
    group_rows = local_rows * shifts
    width_q, width_k = wq.shape[1], wk.shape[1]
    count = (1 << bits) // 4

    x_all = lax.all_gather(block_in, "tp", axis=0, tiled=True)
    qkv_here = join([wq, wk, wv], axis=1)
    qkv_one = gather_one(qkv_here, bits)
    gains = gather_small(jnp.stack([gain_attn, gain_mlp]), bits).astype(jnp.float32)
    gains = jnp.swapaxes(gains, 0, 1).reshape(2, -1)
    gate_one = gather_one(w_gate, bits)
    qkv_two = gather_two(qkv_one, bits)
    qkv_w = gather_end(qkv_here, qkv_one, qkv_two, bits)
    pos_all = block_positions(pair_slot, group_rows // 2)
    pos_rows = lax.dynamic_slice_in_dim(pos_all, me * group_rows, group_rows)
    cosine, sine = rope_tables(pos_rows)
    out_grad_here = reorder(place, out_grad, bits)
    both_sent = jnp.concatenate([out_grad_here, wo.reshape(-1, model)], axis=0)
    x_all, both_sent, w_up, gains, cosine, sine, *pieces = window(
        x_all, both_sent, w_up, gains, cosine, sine, *qkv_w, *gate_one
    )
    qkv_w, gate_one = cut(pieces, count, 2)

    g_attn, g_mlp = gains[0:1], gains[1:2]
    both_all = lax.all_gather(both_sent, "tp", axis=0)
    gate_two = gather_two(gate_one, bits)
    rows_all, attn_in = norm_rows(place, x_all, g_attn, bits)
    queries, kv = project_qkv(attn_in, qkv_w, cosine, sine, width_q, width_k)
    kv_one = gather_one(kv, bits)
    kv_all = join(gather_end(kv, kv_one, gather_two(kv_one, bits), bits))
    kv_all, w_up, w_down, *gate_two = window(kv_all, w_up, w_down, *gate_two)

    up_one = gather_one(w_up, bits)
    attended, exact, log_total = attend_forward(pair_slot, place, queries, kv_all, bits)
    attended, both_all, w_down, *up_one = window(attended, both_all, w_down, *up_one)

    attended_all = lax.all_gather(attended, "tp", axis=0)
    grad_rows = both_all[:, :local_rows].reshape(group_rows, model)
    wo_groups = both_all[:, local_rows:].reshape(shifts, *wo.shape)
    o_one = gather_one(wo_groups, bits)
    up_two = gather_two(up_one, bits)
    down_one = gather_one(w_down, bits)
    gate_w = gather_end(w_gate, gate_one, gate_two, bits)
    up_w = gather_end(w_up, up_one, up_two, bits)
    attended_all, grad_rows, *pieces = window(attended_all, grad_rows, *o_one, *gate_w, *up_w)
    o_one, gate_w, up_w = cut(pieces, 2, count, count)

    o_two = gather_two(o_one, bits, 1)
    o_w = gather_end(wo_groups, o_one, o_two, bits, 1)
    down_two = gather_two(down_one, bits)
    down_w = gather_end(w_down, down_one, down_two, bits)
    mlp_in, residual_here = project_residual(place, attended_all, rows_all, g_mlp, o_w)
    factor_mlp = rms_scale(residual_here)
    normed_mlp = residual_here * factor_mlp

    hidden, grad_gate, grad_up = mlp_inner(mlp_in, grad_rows, gate_w, up_w, down_w)
    grad_mlp_part = to_features([grad_gate, grad_up], [gate_w, up_w])
    grad_mlp_part, hidden, grad_gate, grad_up = window(grad_mlp_part, hidden, grad_gate, grad_up)

    grad_mlp_in = lax.psum_scatter(grad_mlp_part, "tp", scatter_dimension=0, tiled=True)
    down_sum = gradient_begin(grad_rows, hidden, bits)
    up_sum = gradient_begin(mlp_in, grad_up, bits)
    gate_sum = gradient_begin(mlp_in, grad_gate, bits)
    down_sum = gradient_end(grad_rows, hidden, down_sum, bits)
    up_sum = gradient_end(mlp_in, grad_up, up_sum, bits)
    gate_sum = gradient_end(mlp_in, grad_gate, gate_sum, bits)
    down_two = scatter_two(down_sum, scatter_one(down_sum, bits))
    up_two = scatter_two(up_sum, scatter_one(up_sum, bits))
    mlp_part = to_features([hidden], [down_w])
    grad_mlp_in, mlp_part, *pieces = window(
        grad_mlp_in, mlp_part, *down_two, *up_two, *gate_sum
    )
    down_two, up_two, gate_sum = cut(pieces, 2, 2, 5)

    down_three = scatter_three(down_two, bits)
    grad_mlp_in = grad_mlp_in.astype(jnp.float32)
    gain_mlp_part = jnp.sum(grad_mlp_in * normed_mlp, axis=0, keepdims=True)
    grad_residual = out_grad_here.astype(jnp.float32) + norm_back(
        grad_mlp_in * g_mlp, normed_mlp, factor_mlp
    )
    branch_here = grad_residual.astype(jnp.bfloat16)
    grad_groups = to_groups(place, branch_here, o_w)
    grad_parts = jnp.stack(tp_exchange(grad_groups))
    branch_blocks = to_block_groups(place, branch_here, bits, shifts)
    grad_parts, branch_blocks, mlp_part, *pieces = window(
        grad_parts, branch_blocks, mlp_part, *down_three, *up_two, *gate_sum
    )
    down_three, up_two, gate_sum = cut(pieces, 2, 2, 5)

    up_three = scatter_three(up_two, bits)
    branch_pieces = tp_exchange(branch_blocks)
    mlp_out = lax.psum_scatter(mlp_part, "tp", scatter_dimension=0, tiled=True)
    grad_queries, *grad_kv = attend_backward(
        pair_slot, place, queries, kv_all, grad_parts, exact, log_total, cosine, sine, bits
    )
    pieces = window(*grad_kv, *branch_pieces, *up_three, *gate_sum)
    grad_kv, branch_pieces, up_three, gate_sum = cut(pieces, count, shifts, 2, 5)

    kv_sum = rows_begin(grad_kv, bits)
    kv_three = scatter_three(scatter_two(kv_sum, scatter_one(kv_sum, bits)), bits)
    gate_one = scatter_one(gate_sum, bits)
    o_sum = gradient_out(place, branch_pieces, attended_all, bits)
    mlp_out, *pieces = window(mlp_out, kv_sum[0], *kv_three, *o_sum, *gate_one)
    kv_pieces, o_sum, gate_one = cut(pieces, 3, count, 2)
    grad_qkv = join_grad_qkv(grad_queries, kv_pieces, cosine, sine)
    grad_attn_part = to_features([grad_qkv], [qkv_w])
    gate_three = scatter_three(scatter_two(gate_sum, gate_one), bits)
    o_sum = rows_begin(o_sum, bits)
    grad_attn_part, grad_qkv, *o_sum = window(grad_attn_part, grad_qkv, *o_sum)

    grad_attn_in = lax.psum_scatter(grad_attn_part, "tp", scatter_dimension=0, tiled=True)
    qkv_sum = gradient_begin(attn_in, grad_qkv, bits)
    qkv_sum = gradient_end(attn_in, grad_qkv, qkv_sum, bits)
    o_two = scatter_two(o_sum, scatter_one(o_sum, bits))
    inputs = rows_all.astype(jnp.float32)
    gain_attn_part = jnp.sum(
        grad_attn_part.astype(jnp.float32) * (inputs * rms_scale(inputs)), axis=0, keepdims=True
    )
    gain_sum = jnp.concatenate([gain_attn_part, gain_mlp_part])
    gain_sum = jnp.swapaxes(gain_sum.reshape(2, 1 << bits, -1), 0, 1)
    order = bit_order(bits)
    for bit in reversed(order[2:]):
        gain_sum = scatter_step(gain_sum, bit, bits)
    gain_sum, *pieces = window(gain_sum, *qkv_sum, *o_two, *gate_three)
    qkv_sum, o_two, gate_three = cut(pieces, 5, 2, 2)

    qkv_two = scatter_two(qkv_sum, scatter_one(qkv_sum, bits))
    o_three = scatter_three(o_two, bits)
    gain_sum = scatter_step(gain_sum, order[1], bits)
    gain_sum, *pieces = window(gain_sum, *qkv_two, *o_three)
    qkv_two, o_three = cut(pieces, 2, 2)

    qkv_three = scatter_three(qkv_two, bits)
    gain_sum = scatter_step(gain_sum, order[0], bits)
    sum_o_w = finish_sum(o_sum, o_three).astype(jnp.bfloat16)
    gain_sum, sum_o_w, *qkv_three = window(gain_sum, sum_o_w, *qkv_three)

    sum_down_w = finish_sum(down_sum, down_three)
    sum_up_w = finish_sum(up_sum, up_three)
    sum_o_w = to_owners(sum_o_w, (1 << bits) // shifts).astype(jnp.float32)
    gain_here = sum(tp_gather(gain_sum[0]))
    sum_qkv_w = finish_sum(qkv_sum, qkv_three)
    sum_gate_w = finish_sum(gate_sum, gate_three)
    block_out = (residual_here + mlp_out.astype(jnp.float32)).astype(jnp.bfloat16)
    block_out = reorder(place, block_out, bits, inverse=True)
    grad_attn_in = grad_attn_in.astype(jnp.float32)
    inputs_here = lax.dynamic_slice_in_dim(rows_all, tp * local_rows, local_rows)
    inputs_here = inputs_here.astype(jnp.float32)
    factor_attn = rms_scale(inputs_here)
    input_grad = grad_residual + norm_back(
        grad_attn_in * g_attn, inputs_here * factor_attn, factor_attn
    )
    return (
        block_out,
        reorder(place, input_grad, bits, inverse=True),
        gain_here[0],
        sum_qkv_w[:, :width_q],
        sum_qkv_w[:, width_q : width_q + width_k],
        sum_qkv_w[:, width_q + width_k :],
        sum_o_w,
        gain_here[1],
        sum_gate_w,
        sum_up_w,
        sum_down_w,
    )


def solution(mesh):
    placed = (
        P(("ctx", "tp"), None),
        P(("ctx", "tp"), None),
        P(),
        P("ctx"),
        P("ctx", "tp"),
        P("ctx", "tp"),
        P("ctx", "tp"),
        P("ctx", "tp"),
        P("ctx"),
        P("ctx", "tp"),
        P("ctx", "tp"),
        P("ctx", "tp"),
    )
    return jax.shard_map(
        on_device,
        mesh=mesh,
        in_specs=placed,
        out_specs=(
            P(("ctx", "tp"), None),
            P(("ctx", "tp"), None),
            P("ctx"),
            P("ctx", "tp"),
            P("ctx", "tp"),
            P("ctx", "tp"),
            P("ctx", "tp"),
            P("ctx"),
            P("ctx", "tp"),
            P("ctx", "tp"),
            P("ctx", "tp"),
        ),
        check_vma=False,
    )
```

```python
import functools
import math

import jax
import jax.numpy as jnp
from jax import lax
from jax.experimental import pallas as pl
from jax.experimental.pallas import tpu as pltpu
from jax.sharding import PartitionSpec as P

HEAD_SIZE = 64
LANES = 128
KERNEL_VMEM = 56 * 1024 * 1024

eps_norm = 1e-05
big_negative = -1e30

in_smem = pl.BlockSpec(memory_space=pltpu.SMEM)
in_vmem = pl.BlockSpec(memory_space=pltpu.VMEM)
unread = pl.BlockSpec(memory_space=pl.ANY)


def kernel_params():
    return pltpu.CompilerParams(vmem_limit_bytes=KERNEL_VMEM)


def cost(micros):
    return pl.CostEstimate(flops=int(micros * 1.1e9), bytes_accessed=1024, transcendentals=0)


def gated(value, *others):
    return pl.pallas_call(
        lambda *refs: None,
        out_shape=jax.ShapeDtypeStruct(value.shape, value.dtype),
        in_specs=[unread] * (1 + len(others)),
        out_specs=unread,
        input_output_aliases={0: 0},
        cost_estimate=cost(0.1),
        name="gated",
    )(value, *others)


def bit_order(bits):
    return [1, 2, 0] + list(range(3, bits)) if bits >= 3 else list(range(bits))


def block_key(position, bits):
    key = 0
    for place, bit in enumerate(bit_order(bits)):
        key = key | (((position >> place) & 1) << bit)
    return key


def key_position(key, bits):
    position = 0
    for place, bit in enumerate(bit_order(bits)):
        position = position | (((key >> bit) & 1) << place)
    return position


def swap(array, bit, bits):
    return lax.ppermute(array, "ctx", [(i, i ^ (1 << bit)) for i in range(1 << bits)])


def halves(array, axis):
    middle = array.shape[axis] // 2
    return (
        lax.slice_in_dim(array, 0, middle, axis=axis),
        lax.slice_in_dim(array, middle, 2 * middle, axis=axis),
    )


def gather_one(own, bits):
    first, second = bit_order(bits)[:2]
    return swap(own, first, bits), swap(own, second, bits)


def gather_two(one, bits, axis=0):
    first, second = bit_order(bits)[:2]
    lower, upper = halves(one[0], axis)[0], halves(one[1], axis)[1]
    return swap(lower, second, bits), swap(upper, first, bits)


def join(pieces, axis=0):
    shape = list(pieces[0].shape)
    shape[axis] = sum(piece.shape[axis] for piece in pieces)

    def kernel(*refs):
        in_refs, out_ref, sems = refs[: len(pieces)], refs[len(pieces)], refs[-1]
        copies, start = [], 0
        for index, in_ref in enumerate(in_refs):
            size = in_ref.shape[axis]
            place = pl.ds(start, size)
            target = out_ref.at[(slice(None),) * axis + (place,)]
            copies.append(pltpu.make_async_copy(in_ref, target, sems.at[index]))
            start += size
        for copy in copies:
            copy.start()
        for copy in copies:
            copy.wait()

    return pl.pallas_call(
        kernel,
        out_shape=jax.ShapeDtypeStruct(shape, pieces[0].dtype),
        in_specs=[unread] * len(pieces),
        out_specs=in_vmem,
        scratch_shapes=[pltpu.SemaphoreType.DMA((len(pieces),))],
        compiler_params=kernel_params(),
        cost_estimate=cost(0.1),
        name="join",
    )(*pieces)


def gather_end(own, one, two, bits, axis=0):
    parts = [join([own, *one, *two], axis)]
    for bit in bit_order(bits)[2:]:
        parts = parts + [swap(part, bit, bits) for part in parts]
    return parts


def gather_small(own, bits):
    stacked = own[None]
    for bit in bit_order(bits):
        stacked = jnp.concatenate([stacked, swap(stacked, bit, bits)], axis=0)
    return stacked


def scatter_step(stacked, bit, bits):
    kept = stacked.shape[0] // 2
    return stacked[:kept] + swap(stacked[kept:], bit, bits)


def sum_step(array, shift, axis):
    size = lax.axis_size(axis)
    return array + lax.ppermute(array, axis, [(i, i ^ shift) for i in range(size)])


def add_half(left, right):
    return (left.astype(jnp.float32) + right.astype(jnp.float32)).astype(jnp.bfloat16)


def scatter_one(blocks, bits):
    first, second = bit_order(bits)[:2]
    return swap(blocks[3], second, bits), swap(blocks[4], first, bits)


def scatter_two(blocks, one):
    rows, width = blocks[1].shape
    half = rows // 2

    def kernel(first_ref, second_ref, lower_ref, upper_ref, to_first, to_second):
        to_first[0:half, :] = add_half(first_ref[0:half, :], lower_ref[...])
        to_first[half:, :] = first_ref[half:, :]
        to_second[0:half, :] = second_ref[0:half, :]
        to_second[half:, :] = add_half(second_ref[half:, :], upper_ref[...])

    return pl.pallas_call(
        kernel,
        out_shape=[jax.ShapeDtypeStruct((rows, width), jnp.bfloat16)] * 2,
        in_specs=[in_vmem] * 4,
        out_specs=[in_vmem] * 2,
        compiler_params=kernel_params(),
        cost_estimate=cost(0.1),
        name="scatter_two",
    )(blocks[1], blocks[2], *one)


def scatter_three(two, bits):
    first, second = bit_order(bits)[:2]
    return swap(two[0], first, bits), swap(two[1], second, bits)


def finish_sum(blocks, three, widths=None):
    rows, width = blocks[0].shape
    widths = widths or [width]

    def kernel(own_ref, first_ref, second_ref, *out_refs):
        start = 0
        for out_ref in out_refs:
            here = slice(start, start + out_ref.shape[1])
            total = own_ref[:, here].astype(jnp.float32) + first_ref[:, here].astype(jnp.float32)
            out_ref[...] = total + second_ref[:, here].astype(jnp.float32)
            start += out_ref.shape[1]

    return pl.pallas_call(
        kernel,
        out_shape=[jax.ShapeDtypeStruct((rows, each), jnp.float32) for each in widths],
        in_specs=[in_vmem] * 3,
        out_specs=[in_vmem] * len(widths),
        compiler_params=kernel_params(),
        cost_estimate=cost(0.1),
        name="finish_sum",
    )(blocks[0], *three)


def sum_small(array, axis):
    size = lax.axis_size(axis)
    shift = 1
    while shift < size:
        array = array + lax.ppermute(array, axis, [(i, i ^ shift) for i in range(size)])
        shift *= 2
    return array


def tp_shift(array, distance):
    size = lax.axis_size("tp")
    return lax.ppermute(array, "tp", [(i, (i + distance) % size) for i in range(size)])


def tp_gather(array):
    return [array] + [tp_shift(array, d) for d in range(1, lax.axis_size("tp"))]


def tp_ordered(pieces, tp):
    stacked = jnp.stack(pieces)
    count = len(pieces)
    return jnp.concatenate(
        [lax.dynamic_index_in_dim(stacked, (tp - j) % count, 0, keepdims=False) for j in range(count)]
    )


def tp_exchange(array):
    return [array[0]] + [tp_shift(array[d], d) for d in range(1, array.shape[0])]


def tp_sum(pieces):
    return sum(piece.astype(jnp.float32) for piece in pieces)


def after(value, *others):
    return lax.optimization_barrier((value, *others))


def to_relative(array, me, bits):
    width = array.shape[1] // (1 << bits)
    return jnp.concatenate(
        [
            lax.dynamic_slice_in_dim(array, (me ^ block_key(p, bits)) * width, width, 1)
            for p in range(1 << bits)
        ],
        axis=1,
    )


def to_absolute(array, me, bits):
    width = array.shape[1] // (1 << bits)
    return jnp.concatenate(
        [
            lax.dynamic_slice_in_dim(array, key_position(me ^ c, bits) * width, width, 1)
            for c in range(1 << bits)
        ],
        axis=1,
    )


def reorder(place, array, bits, inverse=False):
    width = array.shape[1] // (1 << bits)
    if width % LANES:
        return (to_absolute if inverse else to_relative)(array, place[0], bits)

    def kernel(place, in_ref, out_ref):
        for p in range(1 << bits):
            other = pl.multiple_of((place[0] ^ block_key(p, bits)) * width, LANES)
            if inverse:
                out_ref[:, pl.ds(other, width)] = in_ref[:, p * width : (p + 1) * width]
            else:
                out_ref[:, p * width : (p + 1) * width] = in_ref[:, pl.ds(other, width)]

    return pl.pallas_call(
        kernel,
        out_shape=jax.ShapeDtypeStruct(array.shape, array.dtype),
        in_specs=[in_smem, in_vmem],
        out_specs=in_vmem,
        compiler_params=kernel_params(),
        cost_estimate=cost(0.1),
        name="reorder",
    )(place, array)


def block_positions(pair_slot, block_len):
    pair_count = pair_slot.shape[0]
    offsets = jnp.arange(2 * block_len, dtype=jnp.int32)
    lower_half = offsets < block_len
    block_index = jnp.where(
        lower_half[None, :], pair_slot[:, None], 2 * pair_count - 1 - pair_slot[:, None]
    )
    return (block_index * block_len + (offsets % block_len)[None, :]).reshape(-1)


def inverse_freqs(head_dim):
    exponent = jnp.arange(0, head_dim, 2).astype(jnp.float32) / head_dim
    base_freq = 500000.0 ** (-exponent)
    wavelength = 2.0 * math.pi / base_freq
    smooth = (8192.0 / wavelength - 1.0) / 3.0
    blended = (1.0 - smooth) * base_freq / 32.0 + smooth * base_freq
    scaled = jnp.where(wavelength > 8192.0, base_freq / 32.0, base_freq)
    middle = (wavelength >= 2048.0) & (wavelength <= 8192.0)
    return jnp.where(middle, blended, scaled)


def rope_tables(positions):
    angles = positions.astype(jnp.float32)[:, None] * inverse_freqs(HEAD_SIZE)[None, :]
    wide = LANES // (HEAD_SIZE // 2)
    return (jnp.tile(jnp.cos(angles), (1, wide)), jnp.tile(jnp.sin(angles), (1, wide)))


def rms_scale(values):
    return lax.rsqrt(jnp.mean(values * values, axis=-1, keepdims=True) + eps_norm)


def norm_back(gradient, normed, factor):
    return factor * (gradient - normed * jnp.mean(gradient * normed, axis=-1, keepdims=True))


def inner_rows(left, right):
    return lax.dot_general(
        left, right, (((0,), (0,)), ((), ())), preferred_element_type=jnp.float32
    )


def nt(left, right):
    return lax.dot_general(
        left, right, (((1,), (1,)), ((), ())), preferred_element_type=jnp.float32
    )


def nn(left, right):
    return lax.dot_general(
        left, right, (((1,), (0,)), ((), ())), preferred_element_type=jnp.float32
    )


def turned_lanes(values):
    half = HEAD_SIZE // 2
    lane = lax.broadcasted_iota(jnp.int32, values.shape, 1)
    up = pltpu.roll(values, LANES - half, 1)
    down = pltpu.roll(values, half, 1)
    return jnp.where(lane % HEAD_SIZE < half, -up, down)


def rotate(values, cosine, sine):
    return values * cosine + turned_lanes(values) * sine


def rotate_back(gradient, cosine, sine):
    return gradient * cosine - turned_lanes(gradient * sine)


def norm_rows(place, rows, gain, bits):
    width = rows.shape[1] // (1 << bits)
    whole_lanes = width % LANES == 0
    if not whole_lanes:
        rows = to_relative(rows, place[0], bits)

    def kernel(place, in_ref, gain_ref, rows_ref, out_ref):
        for p in range(1 << bits):
            here = slice(p * width, (p + 1) * width)
            if whole_lanes:
                other = pl.multiple_of((place[0] ^ block_key(p, bits)) * width, LANES)
                rows_ref[:, here] = in_ref[:, pl.ds(other, width)]
        if not whole_lanes:
            rows_ref[...] = in_ref[...]
        values = rows_ref[...].astype(jnp.float32)
        out_ref[...] = (values * rms_scale(values) * gain_ref[...]).astype(jnp.bfloat16)

    shape = jax.ShapeDtypeStruct(rows.shape, jnp.bfloat16)
    return pl.pallas_call(
        kernel,
        out_shape=(shape, shape),
        in_specs=[in_smem, in_vmem, in_vmem],
        out_specs=(in_vmem, in_vmem),
        compiler_params=kernel_params(),
        cost_estimate=cost(0.1),
        name="norm_rows",
    )(place, rows, gain)


def qkv_kernel(count, x_ref, *refs):
    weights, (cos_ref, sin_ref), (q_ref, kv_ref) = refs[:count], refs[count : count + 2], refs[-2:]
    depth = x_ref.shape[1] // count
    width_q = q_ref.shape[1]
    width_k = kv_ref.shape[1] // 2
    total = width_q + 2 * width_k
    tile = 2 * LANES
    for start in range(0, total, tile):
        product = 0.0
        for index, weight in enumerate(weights):
            product = product + nn(
                x_ref[:, index * depth : (index + 1) * depth], weight[:, start : start + tile]
            )
        for offset in range(0, tile, LANES):
            at = start + offset
            piece = product[:, offset : offset + LANES]
            if at < width_q + width_k:
                piece = rotate(piece, cos_ref[...], sin_ref[...])
            piece = piece.astype(jnp.bfloat16)
            if at < width_q:
                q_ref[:, at : at + LANES] = piece
            else:
                kv_ref[:, at - width_q : at - width_q + LANES] = piece


def project_qkv(attn_in, weights, cosine, sine, width_q, width_k, after=()):
    rows, depth = attn_in.shape
    return pl.pallas_call(
        functools.partial(qkv_kernel, len(weights)),
        out_shape=(
            jax.ShapeDtypeStruct((rows, width_q), jnp.bfloat16),
            jax.ShapeDtypeStruct((rows, 2 * width_k), jnp.bfloat16),
        ),
        in_specs=[in_vmem] * (3 + len(weights)) + [unread] * len(after),
        out_specs=(in_vmem, in_vmem),
        compiler_params=kernel_params(),
        cost_estimate=cost(0.1),
        name="qkv",
    )(attn_in, *weights, cosine, sine, *after)


def sequence_block(slots, me, half_block, bits):
    slot = slots[me ^ block_key(half_block // 2, bits)]
    return jnp.where(half_block % 2 == 0, slot, 2 * (1 << bits) - 1 - slot)


def head_lanes(pair, head, heads_per_kv, scale):
    wide = pair.astype(jnp.float32) * scale
    group = head // heads_per_kv
    source = wide if head % 2 == group else pltpu.roll(wide, HEAD_SIZE, 1)
    low = lax.broadcasted_iota(jnp.int32, wide.shape, 1) < HEAD_SIZE
    keep = low if group == 0 else jnp.logical_not(low)
    return jnp.where(keep, source, 0.0).astype(jnp.bfloat16)


def causal_tile(size):
    key_at = lax.broadcasted_iota(jnp.int32, (size, size), 0)
    row_at = lax.broadcasted_iota(jnp.int32, (size, size), 1)
    return key_at <= row_at


def over_blocks(visit, slots, me, bits, half, prepare):
    visit(0, 0, True, True, True)
    visit(1, half, True, True, True)
    visit(1, 0, False, False, False)
    own = slots[me]
    blocks_of_query = (own, 2 * (1 << bits) - 1 - own)

    def step(index, carry):
        block = sequence_block(slots, me, index, bits)
        start = pl.multiple_of(index * half, half)
        prepare(start)
        for q_half in range(2):

            @pl.when(block < blocks_of_query[q_half])
            def _():
                visit(q_half, start, False, False, False)

        return carry

    lax.fori_loop(2, 2 * (1 << bits), step, 0)


def forward_kernel(bits, heads, slots, place, q_ref, kv_ref, *refs):
    out_ref, exact_ref, log_ref, qp, run_max, run_sum, acc = refs[-7:]
    rows = q_ref.shape[0]
    half = rows // 2
    per_kv = heads // 2
    for head in range(heads):
        lanes = pl.ds((head // 2) * LANES, LANES)
        qp[head] = head_lanes(q_ref[:, lanes], head, per_kv, HEAD_SIZE ** (-0.5))

    def visit(q_half, key_start, diagonal, first, _):
        keys = kv_ref[pl.ds(key_start, half), 0:LANES]
        values_t = kv_ref[pl.ds(key_start, half), LANES : 2 * LANES].T
        base = q_half * heads
        span = pl.ds(q_half * half, half)
        scores = [nt(keys, qp[head, span, :]) for head in range(heads)]
        if diagonal:
            visible = causal_tile(half)
            scores = [jnp.where(visible, score, big_negative) for score in scores]
        peaks = [jnp.max(score, axis=0, keepdims=True) for score in scores]
        if not first:
            before = [run_max[base + head] for head in range(heads)]
            peaks = [jnp.maximum(peak, old) for peak, old in zip(peaks, before)]
        weights = [jnp.exp(score - peak) for score, peak in zip(scores, peaks)]
        totals = [jnp.sum(weight, axis=0, keepdims=True) for weight in weights]
        outs = []
        for head, weight in enumerate(weights):
            group = head // per_kv
            some = values_t[group * HEAD_SIZE : (group + 1) * HEAD_SIZE]
            outs.append(nn(some, weight.astype(jnp.bfloat16)))
        if not first:
            fades = [jnp.exp(old - peak) for old, peak in zip(before, peaks)]
            totals = [t + run_sum[base + h] * f for h, (t, f) in enumerate(zip(totals, fades))]
            outs = [o + acc[base + h] * f for h, (o, f) in enumerate(zip(outs, fades))]
        for head in range(heads):
            run_max[base + head] = peaks[head]
            run_sum[base + head] = totals[head]
            acc[base + head] = outs[head]

    over_blocks(visit, slots, place[0], bits, half, lambda start: None)
    for q_half in range(2):
        span = pl.ds(q_half * half, half)
        for pair in range(heads // 2):
            parts = []
            for head in (2 * pair, 2 * pair + 1):
                slot = q_half * heads + head
                parts.append(acc[slot] / run_sum[slot])
                log_ref[pl.ds(head, 1), span] = run_max[slot] + jnp.log(run_sum[slot])
            exact = jnp.concatenate(parts, axis=0).T
            exact_ref[span, pl.ds(pair * LANES, LANES)] = exact
            out_ref[span, pl.ds(pair * LANES, LANES)] = exact.astype(jnp.bfloat16)


def attend_forward(slots, place, queries, kv, bits, after=()):
    rows, width = queries.shape
    heads = width // HEAD_SIZE
    half = rows // 2
    return pl.pallas_call(
        functools.partial(forward_kernel, bits, heads),
        out_shape=(
            jax.ShapeDtypeStruct((rows, width), jnp.bfloat16),
            jax.ShapeDtypeStruct((rows, width), jnp.float32),
            jax.ShapeDtypeStruct((heads, rows), jnp.float32),
        ),
        in_specs=[in_smem, in_smem, in_vmem, in_vmem] + [unread] * len(after),
        out_specs=(in_vmem, in_vmem, in_vmem),
        scratch_shapes=[
            pltpu.VMEM((heads, rows, LANES), jnp.bfloat16),
            pltpu.VMEM((2 * heads, 1, half), jnp.float32),
            pltpu.VMEM((2 * heads, 1, half), jnp.float32),
            pltpu.VMEM((2 * heads, HEAD_SIZE, half), jnp.float32),
        ],
        compiler_params=kernel_params(),
        cost_estimate=cost(19),
        name="attention_forward",
    )(slots, place, queries, kv, *after)


def backward_kernel(bits, heads, slots, place, *refs):
    q_ref, kv_ref, do_ref, exact_ref, log_ref, cos_ref, sin_ref = refs[:7]
    parts = max(1, (1 << bits) // 4)
    dq_ref, dkv_refs = refs[-7 - parts], refs[-6 - parts : -6]
    qp, dop, dots, dq_acc, dkv_acc, do_all = refs[-6:]
    rows = q_ref.shape[0]
    half = rows // 2
    per_kv = heads // 2
    shifts, local, _ = do_ref.shape
    for shift in range(shifts):
        source = lax.rem(place[1] - shift + shifts, shifts)
        do_all[pl.ds(pl.multiple_of(source * local, local), local), :] = do_ref[shift]
    for head in range(heads):
        lanes = pl.ds((head // 2) * LANES, LANES)
        qp[head] = head_lanes(q_ref[:, lanes], head, per_kv, HEAD_SIZE ** (-0.5))
        dop[head] = head_lanes(do_all[:, lanes], head, per_kv, 1.0)
    for pair in range(heads // 2):
        lanes = pl.ds(pair * LANES, LANES)
        product = (do_all[:, lanes].astype(jnp.float32) * exact_ref[:, lanes]).T
        dots[pl.ds(2 * pair, 1), :] = jnp.sum(product[:HEAD_SIZE], axis=0, keepdims=True)
        dots[pl.ds(2 * pair + 1, 1), :] = jnp.sum(product[HEAD_SIZE:], axis=0, keepdims=True)

    def clear(start):
        dkv_acc[pl.ds(start, half), :] = jnp.zeros((half, 2 * LANES), jnp.float32)

    def visit(q_half, key_start, diagonal, first_query, first_key):
        rows_of_key = pl.ds(key_start, half)
        keys = kv_ref[rows_of_key, 0:LANES]
        values = kv_ref[rows_of_key, LANES : 2 * LANES]
        keys_t = keys.T
        base = q_half * heads
        span = pl.ds(q_half * half, half)
        q_heads = [qp[head, span, :] for head in range(heads)]
        do_heads = [dop[head, span, :] for head in range(heads)]
        scores = [nt(keys, q_head) for q_head in q_heads]
        grad_ws = [nt(values, do_head) for do_head in do_heads]
        weights = [
            jnp.exp(score - log_ref[pl.ds(head, 1), span]) for head, score in enumerate(scores)
        ]
        if diagonal:
            visible = causal_tile(half)
            weights = [jnp.where(visible, weight, 0.0) for weight in weights]
        grad_ss = [
            (weight * (grad_w - dots[pl.ds(head, 1), span])).astype(jnp.bfloat16)
            for head, (weight, grad_w) in enumerate(zip(weights, grad_ws))
        ]
        weights = [weight.astype(jnp.bfloat16) for weight in weights]
        grad_v = jnp.zeros((half, LANES), jnp.float32)
        grad_k = jnp.zeros((half, LANES), jnp.float32)
        for weight, do_head in zip(weights, do_heads):
            grad_v = grad_v + nn(weight, do_head)
        for grad_s, q_head in zip(grad_ss, q_heads):
            grad_k = grad_k + nn(grad_s, q_head)
        for head, grad_s in enumerate(grad_ss):
            group = head // per_kv
            grad_q = nn(keys_t[group * HEAD_SIZE : (group + 1) * HEAD_SIZE], grad_s)
            if not first_query:
                grad_q = grad_q + dq_acc[base + head]
            dq_acc[base + head] = grad_q
        if not first_key:
            grad_k = grad_k + dkv_acc[rows_of_key, 0:LANES]
            grad_v = grad_v + dkv_acc[rows_of_key, LANES : 2 * LANES]
        dkv_acc[rows_of_key, 0:LANES] = grad_k
        dkv_acc[rows_of_key, LANES : 2 * LANES] = grad_v

    over_blocks(visit, slots, place[0], bits, half, clear)
    size = dkv_acc.shape[0] // parts
    for part, dkv_ref in enumerate(dkv_refs):
        dkv_ref[...] = dkv_acc[part * size : (part + 1) * size, :].astype(jnp.bfloat16)
    for q_half in range(2):
        span = pl.ds(q_half * half, half)
        for pair in range(heads // 2):
            slot = q_half * heads + 2 * pair
            gradient = jnp.concatenate([dq_acc[slot], dq_acc[slot + 1]], axis=0).T
            gradient = rotate_back(
                gradient * HEAD_SIZE ** (-0.5), cos_ref[span, :], sin_ref[span, :]
            )
            dq_ref[span, pl.ds(pair * LANES, LANES)] = gradient.astype(jnp.bfloat16)


def attend_backward(
    slots, place, queries, kv, grad_parts, exact, log_total, cosine, sine, bits, after=()
):
    parts = max(1, (1 << bits) // 4)
    rows, width = queries.shape
    heads = width // HEAD_SIZE
    half = rows // 2
    return pl.pallas_call(
        functools.partial(backward_kernel, bits, heads),
        out_shape=(
            jax.ShapeDtypeStruct((rows, width), jnp.bfloat16),
            *[jax.ShapeDtypeStruct((kv.shape[0] // parts, kv.shape[1]), jnp.bfloat16)] * parts,
        ),
        in_specs=[in_smem, in_smem] + [in_vmem] * 7 + [unread] * len(after),
        out_specs=(in_vmem,) * (1 + parts),
        scratch_shapes=[
            pltpu.VMEM((heads, rows, LANES), jnp.bfloat16),
            pltpu.VMEM((heads, rows, LANES), jnp.bfloat16),
            pltpu.VMEM((heads, rows), jnp.float32),
            pltpu.VMEM((2 * heads, HEAD_SIZE, half), jnp.float32),
            pltpu.VMEM(kv.shape, jnp.float32),
            pltpu.VMEM((rows, width), jnp.bfloat16),
        ],
        compiler_params=kernel_params(),
        cost_estimate=cost(30),
        name="attention_backward",
    )(slots, place, queries, kv, grad_parts, exact, log_total, cosine, sine, *after)


def grad_qkv_kernel(dq_ref, own_ref, first_ref, second_ref, cos_ref, sin_ref, out_ref):
    width_q = dq_ref.shape[1]
    out_ref[:, 0:width_q] = dq_ref[...]
    total = own_ref[...].astype(jnp.float32) + first_ref[...].astype(jnp.float32)
    total = total + second_ref[...].astype(jnp.float32)
    keys = rotate_back(total[:, 0:LANES], cos_ref[...], sin_ref[...])
    out_ref[:, width_q : width_q + LANES] = keys.astype(jnp.bfloat16)
    out_ref[:, width_q + LANES :] = total[:, LANES:].astype(jnp.bfloat16)


def join_grad_qkv(grad_queries, pieces, cosine, sine):
    rows, width_q = grad_queries.shape
    width = width_q + pieces[0].shape[1]
    return pl.pallas_call(
        grad_qkv_kernel,
        out_shape=jax.ShapeDtypeStruct((rows, width), jnp.bfloat16),
        in_specs=[in_vmem] * 6,
        out_specs=in_vmem,
        compiler_params=kernel_params(),
        cost_estimate=cost(0.1),
        name="grad_qkv",
    )(grad_queries, *pieces, cosine, sine)


def mlp_kernel(count, x_ref, g_ref, *refs):
    weights = refs[:count], refs[count : 2 * count], refs[2 * count : 3 * count]
    hidden_ref, grad_gate_ref, grad_up_ref = refs[3 * count :]
    depth = x_ref.shape[1] // count

    def product(left, parts):
        total = 0.0
        for index, part in enumerate(parts):
            total = total + nn(left[:, index * depth : (index + 1) * depth], part[...])
        return total

    gate = product(x_ref, weights[0])
    up = product(x_ref, weights[1])
    grad_hidden = product(g_ref, weights[2])
    sigmoid = jax.nn.sigmoid(gate)
    silu = gate * sigmoid
    hidden_ref[...] = (silu * up).astype(jnp.bfloat16)
    grad_gate = grad_hidden * up * sigmoid * (1.0 + gate * (1.0 - sigmoid))
    grad_gate_ref[...] = grad_gate.astype(jnp.bfloat16)
    grad_up_ref[...] = (grad_hidden * silu).astype(jnp.bfloat16)


def mlp_inner(mlp_in, grad_rows, gates, ups, downs):
    rows, depth = mlp_in.shape
    units = gates[0].shape[1]
    count = len(gates)
    tile = min(256, units)
    whole = pl.BlockSpec((rows, depth), lambda i: (0, 0))
    part = pl.BlockSpec((depth // count, tile), lambda i: (0, i))
    out = pl.BlockSpec((rows, tile), lambda i: (0, i))
    shape = jax.ShapeDtypeStruct((rows, units), jnp.bfloat16)
    return pl.pallas_call(
        functools.partial(mlp_kernel, count),
        grid=(units // tile,),
        out_shape=(shape, shape, shape),
        in_specs=[whole, whole] + [part] * (3 * count),
        out_specs=(out, out, out),
        compiler_params=kernel_params(),
        cost_estimate=cost(0.1),
        name="mlp_inner",
    )(mlp_in, grad_rows, *gates, *ups, *downs)


def project_part(lefts, part):
    depth, rows, width = lefts.shape
    features = part.shape[1]
    tile = min(256, features)

    def kernel(left_ref, part_ref, out_ref):
        total = 0.0
        for group in range(depth):
            total = total + nt(left_ref[group], part_ref[group])
        out_ref[...] = total

    return pl.pallas_call(
        kernel,
        grid=(features // tile,),
        out_shape=jax.ShapeDtypeStruct((rows, features), jnp.float32),
        in_specs=[
            pl.BlockSpec((depth, rows, width), lambda i: (0, 0, 0)),
            pl.BlockSpec((depth, tile, width), lambda i: (0, i, 0)),
        ],
        out_specs=pl.BlockSpec((rows, tile), lambda i: (0, i)),
        compiler_params=kernel_params(),
        cost_estimate=cost(0.1),
        name="project_part",
    )(lefts, part)


def residual_kernel(place, left_ref, x_ref, gain_ref, part_ref, *refs):
    sums, (mlp_ref, here_ref, residual) = refs[:-3], refs[-3:]
    depth, rows, _ = left_ref.shape
    tile = part_ref.shape[1]
    step = pl.program_id(0)
    total = 0.0
    for group in range(depth):
        total = total + nt(left_ref[group], part_ref[group])
    residual[step] = total

    @pl.when(step == pl.num_programs(0) - 1)
    def _():
        width = x_ref.shape[1]
        before = sum(ref.shape[1] for ref in sums)
        squares = jnp.zeros((rows, 1), jnp.float32)
        pieces = []
        for ref in sums:
            pieces += [(ref, slice(k, k + tile)) for k in range(0, ref.shape[1], tile)]
        count = (width - before) // tile
        local = rows // depth
        here = pl.ds(pl.multiple_of(place[1] * local, local), local)
        for index in range(width // tile):
            columns = slice(index * tile, (index + 1) * tile)
            values = x_ref[:, columns].astype(jnp.float32)
            if index < len(pieces):
                ref, at = pieces[index]
                values = values + ref[:, at]
                ref[:, at] = values
            else:
                values = values + residual[index - len(pieces)]
                residual[index - len(pieces)] = values
            squares = squares + jnp.sum(values * values, axis=1, keepdims=True)
        factor = lax.rsqrt(squares / width + eps_norm)
        for index in range(width // tile):
            columns = slice(index * tile, (index + 1) * tile)
            if index < len(pieces):
                ref, at = pieces[index]
                values, mine = ref[:, at], ref[here, at]
            else:
                values = residual[index - len(pieces)]
                mine = residual[index - len(pieces), here, :]
            mlp_ref[:, columns] = (values * factor * gain_ref[:, columns]).astype(jnp.bfloat16)
            here_ref[:, columns] = mine


def project_residual(place, lefts, rows, gain, parts):
    depth, count, width = lefts.shape
    total = rows.shape[1]
    sums = [project_part(lefts, part) for part in parts[:-1]]
    features = parts[-1].shape[1]
    tile = min(256, features)
    whole = lambda i: (0, 0)
    return pl.pallas_call(
        residual_kernel,
        grid=(features // tile,),
        out_shape=(
            jax.ShapeDtypeStruct((count, total), jnp.bfloat16),
            jax.ShapeDtypeStruct((count // depth, total), jnp.float32),
        ),
        in_specs=[
            in_smem,
            pl.BlockSpec((depth, count, width), lambda i: (0, 0, 0)),
            pl.BlockSpec((count, total), whole),
            pl.BlockSpec((1, total), whole),
            pl.BlockSpec((depth, tile, width), lambda i: (0, i, 0)),
        ]
        + [pl.BlockSpec(each.shape, whole) for each in sums],
        out_specs=(
            pl.BlockSpec((count, total), whole),
            pl.BlockSpec((count // depth, total), whole),
        ),
        scratch_shapes=[pltpu.VMEM((features // tile, count, tile), jnp.float32)],
        compiler_params=kernel_params(),
        cost_estimate=cost(0.1),
        name="project_residual",
    )(place, lefts, rows, gain, parts[-1], *sums)


def to_features(lefts, weights, after=()):
    rows = lefts[0].shape[0]
    count = len(weights[0])
    features = weights[0][0].shape[0]
    tile = min(256, features)
    tiles = features // tile

    def kernel(*refs):
        left_refs, part_refs, out_ref = refs[: len(lefts)], refs[len(lefts) :], refs[-1]
        step = pl.program_id(0)
        for part in range(count):

            @pl.when(step // tiles == part)
            def _():
                total = 0.0
                for source, left_ref in enumerate(left_refs):
                    total = total + nt(left_ref[...], part_refs[source * count + part][...])
                out_ref[...] = total.astype(jnp.bfloat16)

    def part_at(base, i):
        return (jnp.clip(i - base, 0, tiles - 1), 0)

    return pl.pallas_call(
        kernel,
        grid=(count * tiles,),
        out_shape=jax.ShapeDtypeStruct((rows, count * features), jnp.bfloat16),
        in_specs=[pl.BlockSpec(left.shape, lambda i: (0, 0)) for left in lefts]
        + [
            pl.BlockSpec((tile, parts[part].shape[1]), functools.partial(part_at, part * tiles))
            for parts in weights
            for part in range(count)
        ]
        + [unread] * len(after),
        out_specs=pl.BlockSpec((rows, tile), lambda i: (0, i)),
        compiler_params=kernel_params(),
        cost_estimate=cost(0.1),
        name="to_features",
    )(*lefts, *[part for parts in weights for part in parts], *after)


def to_groups(place, branch, parts):
    rows, depth = branch.shape
    groups, features, width = parts[0].shape
    count = len(parts)

    def kernel(place, x_ref, *refs):
        total = 0.0
        for index, part in enumerate(refs[:count]):
            columns = x_ref[:, index * features : (index + 1) * features]
            total = total + nn(columns, part[0])
        refs[-1][0] = total.astype(jnp.bfloat16)

    def weight_at(shift, place):
        return (lax.rem(place[1] + shift, groups), 0, 0)

    return pl.pallas_call(
        kernel,
        grid_spec=pltpu.PrefetchScalarGridSpec(
            num_scalar_prefetch=1,
            grid=(groups,),
            in_specs=[pl.BlockSpec((rows, depth), lambda i, place: (0, 0))]
            + [pl.BlockSpec((1, features, width), weight_at)] * count,
            out_specs=pl.BlockSpec((1, rows, width), lambda i, place: (i, 0, 0)),
        ),
        out_shape=jax.ShapeDtypeStruct((groups, rows, width), jnp.bfloat16),
        compiler_params=kernel_params(),
        cost_estimate=cost(0.1),
        name="to_groups",
    )(place, branch, *parts)


def to_block_groups(place, rows, bits, groups):
    local, depth = rows.shape
    width = depth >> bits
    count = (1 << bits) // groups
    if width % LANES:
        blocks = to_absolute(rows, place[0], bits)
        blocks = blocks.reshape(local, groups, count, width).transpose(1, 2, 0, 3)
        return jnp.stack(
            [
                lax.dynamic_index_in_dim(blocks, (place[1] + d) % groups, 0, keepdims=False)
                for d in range(groups)
            ]
        )

    def kernel(place, in_ref, out_ref):
        for d in range(groups):
            for index in range(count):
                block = lax.rem(place[1] + d, groups) * count + index
                start = key_position(place[0] ^ block, bits) * width
                out_ref[d, index] = in_ref[:, pl.ds(pl.multiple_of(start, LANES), width)]

    return pl.pallas_call(
        kernel,
        out_shape=jax.ShapeDtypeStruct((groups, count, local, width), rows.dtype),
        in_specs=[in_smem, in_vmem],
        out_specs=in_vmem,
        compiler_params=kernel_params(),
        cost_estimate=cost(0.1),
        name="to_block_groups",
    )(place, rows)


def gradient_out(place, branch, attended, bits):
    shifts = len(branch)
    count, local, features = branch[0].shape
    groups, rows, width = attended.shape
    parts = (1 << bits) // 4

    def kernel(place, *refs):
        lefts, right_ref, outs = refs[:shifts], refs[shifts], refs[shifts + 1 :]
        for part, out_ref in enumerate(outs):
            for block in range(4):
                device = place[0] ^ block_key(4 * part + block, bits)
                index = lax.rem(device, count)
                group = device // count
                total = 0.0
                for distance, left in enumerate(lefts):
                    start = lax.rem(place[1] - distance + shifts, shifts) * local
                    here = pl.ds(pl.multiple_of(start, local), local)
                    total = total + inner_rows(left[index], right_ref[group, here, :])
                out_ref[block * features : (block + 1) * features, :] = total.astype(jnp.bfloat16)

    return pl.pallas_call(
        kernel,
        out_shape=[jax.ShapeDtypeStruct((4 * features, width), jnp.bfloat16)] * parts,
        in_specs=[in_smem] + [in_vmem] * (shifts + 1),
        out_specs=[in_vmem] * parts,
        compiler_params=kernel_params(),
        cost_estimate=cost(0.1),
        name="gradient_out",
    )(place, *branch, attended)


def to_owners(array, count):
    ctx, tp = lax.axis_size("ctx"), lax.axis_size("tp")
    moves = []
    for c in range(ctx):
        for t in range(tp):
            moves.append((c * tp + t, (count * t + c % count) * tp + c // count))
    return lax.ppermute(array, ("ctx", "tp"), moves)


def block_rows(rows):
    quarter = rows // 4
    return [quarter, quarter, quarter, quarter // 2, quarter // 2]


def gradient_part(left, right, parts, part, received=(), pieces=4, after=()):
    rows, depth = left.shape
    depth = depth // parts
    width = right.shape[1]
    tile = next(t for t in (1024, 768, 512, 256, LANES, width) if width % t == 0)
    sizes = block_rows(depth) if received else [depth // pieces] * pieces
    step = depth // max(1, len(received))

    def kernel(left_ref, right_ref, *refs):
        total = inner_rows(left_ref[...], right_ref[...])
        start = 0
        for size, out_ref in zip(sizes, refs[len(received) + len(after) :]):
            piece = total[start : start + size]
            if received:
                offset = start % step
                other = refs[start // step][offset : offset + size, :]
                piece = piece + other.astype(jnp.float32)
            out_ref[...] = piece.astype(jnp.bfloat16)
            start += size

    return pl.pallas_call(
        kernel,
        grid=(width // tile,),
        out_shape=[jax.ShapeDtypeStruct((size, width), jnp.bfloat16) for size in sizes],
        in_specs=[
            pl.BlockSpec((rows, depth), lambda i: (0, part)),
            pl.BlockSpec((rows, tile), lambda i: (0, i)),
        ]
        + [pl.BlockSpec((step, tile), lambda i: (0, i))] * len(received)
        + [unread] * len(after),
        out_specs=[pl.BlockSpec((size, tile), lambda i: (0, i)) for size in sizes],
        compiler_params=kernel_params(),
        cost_estimate=cost(0.1),
        name="gradient_part",
    )(left, right, *received, *after)


def gradient_begin(left, right, bits, pieces=4, after=()):
    parts = (1 << bits) // 4
    bit = bit_order(bits)[-1]
    return [
        [
            swap(block, bit, bits)
            for block in gradient_part(left, right, parts, part, pieces=pieces, after=after)
        ]
        for part in range(parts // 2, parts)
    ]


def gradient_end(left, right, received, bits):
    parts = (1 << bits) // 4
    if parts == 2:
        return gradient_part(left, right, parts, 0, received[0])
    kept = [jnp.concatenate(gradient_part(left, right, parts, p)) for p in range(parts // 2)]
    kept = [add_half(mine, jnp.concatenate(other)) for mine, other in zip(kept, received)]
    return sum_parts(kept, bits, bit_order(bits)[2:-1])


def finish_input(place, gradient, residual, rows, gain, bits):
    local, depth = gradient.shape
    width = depth >> bits
    whole_lanes = width % LANES == 0

    def kernel(place, grad_ref, residual_ref, rows_ref, gain_ref, out_ref, *scratch):
        start = pl.multiple_of(place[1] * local, local)
        values = rows_ref[pl.ds(start, local), :].astype(jnp.float32)
        factor = rms_scale(values)
        normed = values * factor
        scaled = grad_ref[...].astype(jnp.float32) * gain_ref[...]
        total = residual_ref[...] + norm_back(scaled, normed, factor)
        if not whole_lanes:
            out_ref[...] = total
            return
        for p in range(1 << bits):
            other = pl.multiple_of((place[0] ^ block_key(p, bits)) * width, LANES)
            out_ref[:, pl.ds(other, width)] = total[:, p * width : (p + 1) * width]

    out = pl.pallas_call(
        kernel,
        out_shape=jax.ShapeDtypeStruct((local, depth), jnp.float32),
        in_specs=[in_smem] + [in_vmem] * 4,
        out_specs=in_vmem,
        compiler_params=kernel_params(),
        cost_estimate=cost(0.1),
        name="finish_input",
    )(place, gradient, residual, rows, gain)
    return out if whole_lanes else to_absolute(out, place[0], bits)


def sum_parts(parts, bits, over):
    for bit in reversed(over):
        count = len(parts) // 2
        came = [swap(part, bit, bits) for part in parts[count:]]
        if count == 1:
            return split_blocks(parts[0], came[0])
        parts = [add_half(mine, other) for mine, other in zip(parts[:count], came)]


def split_blocks(kept, received):
    sizes = block_rows(kept.shape[0])

    def kernel(kept_ref, other_ref, *refs):
        start = 0
        for size, out_ref in zip(sizes, refs):
            here = slice(start, start + size)
            out_ref[...] = add_half(kept_ref[here, :], other_ref[here, :])
            start += size

    return pl.pallas_call(
        kernel,
        out_shape=[jax.ShapeDtypeStruct((size, kept.shape[1]), jnp.bfloat16) for size in sizes],
        in_specs=[in_vmem] * 2,
        out_specs=[in_vmem] * 5,
        compiler_params=kernel_params(),
        cost_estimate=cost(0.1),
        name="split_blocks",
    )(kept, received)


def rows_begin(parts, bits):
    return sum_parts(parts, bits, bit_order(bits)[2:])


def window(*values):
    return lax.optimization_barrier(values)


def cut(values, *sizes):
    out, start = [], 0
    for size in sizes:
        out.append(values[start : start + size])
        start += size
    return out


def on_device(
    block_in, out_grad, pair_slot, gain_attn, wq, wk, wv, wo, gain_mlp, w_gate, w_up, w_down
):
    bits = (lax.axis_size("ctx") - 1).bit_length()
    shifts = lax.axis_size("tp")
    me = lax.axis_index("ctx")
    tp = lax.axis_index("tp")
    place = jnp.stack([me, tp]).astype(jnp.int32)
    local_rows, model = block_in.shape
    group_rows = local_rows * shifts
    width_q, width_k = wq.shape[1], wk.shape[1]
    count = (1 << bits) // 4

    x_all = lax.all_gather(block_in, "tp", axis=0, tiled=True)
    qkv_here = join([wq, wk, wv], axis=1)
    qkv_one = gather_one(qkv_here, bits)
    gains = gather_small(jnp.stack([gain_attn, gain_mlp]), bits).astype(jnp.float32)
    gains = jnp.swapaxes(gains, 0, 1).reshape(2, -1)
    gate_one = gather_one(w_gate, bits)
    qkv_two = gather_two(qkv_one, bits)
    qkv_w = gather_end(qkv_here, qkv_one, qkv_two, bits)
    pos_all = block_positions(pair_slot, group_rows // 2)
    pos_rows = lax.dynamic_slice_in_dim(pos_all, me * group_rows, group_rows)
    cosine, sine = rope_tables(pos_rows)
    out_grad_here = reorder(place, out_grad, bits)
    both_sent = jnp.concatenate([out_grad_here, wo.reshape(-1, model)], axis=0)
    x_all, both_sent, w_up, gains, cosine, sine, *pieces = window(
        x_all, both_sent, w_up, gains, cosine, sine, *qkv_w, *gate_one
    )
    qkv_w, gate_one = cut(pieces, count, 2)

    g_attn, g_mlp = gains[0:1], gains[1:2]
    both_all = lax.all_gather(both_sent, "tp", axis=0)
    gate_two = gather_two(gate_one, bits)
    rows_all, attn_in = norm_rows(place, x_all, g_attn, bits)
    queries, kv = project_qkv(attn_in, qkv_w, cosine, sine, width_q, width_k)
    kv_one = gather_one(kv, bits)
    kv_all = join(gather_end(kv, kv_one, gather_two(kv_one, bits), bits))
    kv_all, w_up, w_down = window(kv_all, w_up, w_down)

    up_one = gather_one(w_up, bits)
    attended, exact, log_total = attend_forward(pair_slot, place, queries, kv_all, bits)
    attended, both_all, w_down, *pieces = window(
        attended, both_all, w_down, *gate_two, *up_one
    )
    gate_two, up_one = cut(pieces, 2, 2)

    attended_all = lax.all_gather(attended, "tp", axis=0)
    grad_rows = both_all[:, :local_rows].reshape(group_rows, model)
    wo_groups = both_all[:, local_rows:].reshape(shifts, *wo.shape)
    o_one = gather_one(wo_groups, bits)
    up_two = gather_two(up_one, bits)
    o_two = gather_two(o_one, bits, 1)
    gate_w = gather_end(w_gate, gate_one, gate_two, bits)
    attended_all, grad_rows, w_down, *pieces = window(
        attended_all, grad_rows, w_down, *o_two, *up_two, *gate_w
    )
    o_two, up_two, gate_w = cut(pieces, 2, 2, count)

    down_one = gather_one(w_down, bits)
    up_w = gather_end(w_up, up_one, up_two, bits)
    o_w = gather_end(wo_groups, o_one, o_two, bits, 1)
    mlp_in, residual_here = project_residual(place, attended_all, rows_all, g_mlp, o_w)
    mlp_in, residual_here, *pieces = window(mlp_in, residual_here, *down_one, *up_w)
    down_one, up_w = cut(pieces, 2, count)
    down_two = gather_two(down_one, bits)
    down_w = gather_end(w_down, down_one, down_two, bits)
    factor_mlp = rms_scale(residual_here)
    normed_mlp = residual_here * factor_mlp

    hidden, grad_gate, grad_up = mlp_inner(mlp_in, grad_rows, gate_w, up_w, down_w)
    grad_mlp_part = to_features([grad_gate, grad_up], [gate_w, up_w])
    grad_mlp_part, hidden, grad_gate, grad_up = window(grad_mlp_part, hidden, grad_gate, grad_up)

    grad_mlp_in = lax.psum_scatter(grad_mlp_part, "tp", scatter_dimension=0, tiled=True)
    down_sum = gradient_begin(grad_rows, hidden, bits)
    up_sum = gradient_begin(mlp_in, grad_up, bits)
    gate_sum = gradient_begin(mlp_in, grad_gate, bits)
    down_sum = gradient_end(grad_rows, hidden, down_sum, bits)
    up_sum = gradient_end(mlp_in, grad_up, up_sum, bits)
    gate_sum = gradient_end(mlp_in, grad_gate, gate_sum, bits)
    down_two = scatter_two(down_sum, scatter_one(down_sum, bits))
    up_two = scatter_two(up_sum, scatter_one(up_sum, bits))
    gate_one = scatter_one(gate_sum, bits)
    mlp_part = to_features([hidden], [down_w])
    grad_mlp_in, mlp_part, *pieces = window(
        grad_mlp_in, mlp_part, *down_two, *up_two, *gate_one, *gate_sum
    )
    down_two, up_two, gate_one, gate_sum = cut(pieces, 2, 2, 2, 5)

    down_three = scatter_three(down_two, bits)
    grad_mlp_in = grad_mlp_in.astype(jnp.float32)
    gain_mlp_part = jnp.sum(grad_mlp_in * normed_mlp, axis=0, keepdims=True)
    grad_residual = out_grad_here.astype(jnp.float32) + norm_back(
        grad_mlp_in * g_mlp, normed_mlp, factor_mlp
    )
    branch_here = grad_residual.astype(jnp.bfloat16)
    grad_groups = to_groups(place, branch_here, o_w)
    grad_parts = jnp.stack(tp_exchange(grad_groups))
    gate_two = scatter_two(gate_sum, gate_one)
    grad_parts, branch_here, mlp_part, *pieces = window(
        grad_parts, branch_here, mlp_part, *down_three, *up_two, *gate_two
    )
    down_three, up_two, gate_two = cut(pieces, 2, 2, 2)

    up_three = scatter_three(up_two, bits)
    gate_three = scatter_three(gate_two, bits)
    branch_blocks = to_block_groups(place, branch_here, bits, shifts)
    mlp_out = lax.psum_scatter(mlp_part, "tp", scatter_dimension=0, tiled=True)
    grad_queries, *grad_kv = attend_backward(
        pair_slot, place, queries, kv_all, grad_parts, exact, log_total, cosine, sine, bits
    )
    branch_blocks, *pieces = window(branch_blocks, *grad_kv, *up_three)
    grad_kv, up_three = cut(pieces, count, 2)

    kv_sum = rows_begin(grad_kv, bits)
    kv_three = scatter_three(scatter_two(kv_sum, scatter_one(kv_sum, bits)), bits)
    branch_pieces = tp_exchange(branch_blocks)
    mlp_out, *pieces = window(mlp_out, kv_sum[0], *kv_three, *branch_pieces)
    kv_pieces, branch_pieces = cut(pieces, 3, shifts)
    grad_qkv = join_grad_qkv(grad_queries, kv_pieces, cosine, sine)
    grad_attn_part = to_features([grad_qkv], [qkv_w])
    grad_attn_part, grad_qkv, *branch_pieces = window(grad_attn_part, grad_qkv, *branch_pieces)

    grad_attn_in = lax.psum_scatter(grad_attn_part, "tp", scatter_dimension=0, tiled=True)
    qkv_sum = gradient_begin(attn_in, grad_qkv, bits, pieces=1)
    qkv_sum = gradient_end(attn_in, grad_qkv, qkv_sum, bits)
    inputs = rows_all.astype(jnp.float32)
    gain_attn_part = jnp.sum(
        grad_attn_part.astype(jnp.float32) * (inputs * rms_scale(inputs)), axis=0, keepdims=True
    )
    gain_sum = jnp.concatenate([gain_attn_part, gain_mlp_part])
    gain_sum = jnp.swapaxes(gain_sum.reshape(2, 1 << bits, -1), 0, 1)
    order = bit_order(bits)
    for bit in reversed(order[2:]):
        gain_sum = scatter_step(gain_sum, bit, bits)
    o_sum = rows_begin(gradient_out(place, branch_pieces, attended_all, bits), bits)
    gain_sum, *pieces = window(gain_sum, *qkv_sum, *o_sum, *gate_three, *down_three, *up_three)
    qkv_sum, o_sum, gate_three, down_three, up_three = cut(pieces, 5, 5, 2, 2, 2)

    qkv_two = scatter_two(qkv_sum, scatter_one(qkv_sum, bits))
    o_two = scatter_two(o_sum, scatter_one(o_sum, bits))
    gain_sum = scatter_step(gain_sum, order[1], bits)
    pieces = window(gain_sum, *qkv_two, *o_two, *gate_three, *down_three, *up_three, mlp_out)
    (gain_sum,), qkv_two, o_two, gate_three, down_three, up_three, (mlp_out,) = cut(
        pieces, 1, 2, 2, 2, 2, 2, 1
    )

    qkv_three, o_three = scatter_three(qkv_two, bits), scatter_three(o_two, bits)
    gain_sum = scatter_step(gain_sum, order[0], bits)
    (sum_down_w,) = finish_sum(down_sum, down_three)
    (sum_up_w,) = finish_sum(up_sum, up_three)
    gain_sum, sum_down_w, sum_up_w, *pieces = window(
        gain_sum, sum_down_w, sum_up_w, *qkv_three, *o_three
    )
    qkv_three, o_three = cut(pieces, 2, 2)

    (sum_o_w,) = finish_sum(o_sum, o_three)
    sum_o_w = to_owners(sum_o_w.astype(jnp.bfloat16), (1 << bits) // shifts)
    gain_here, shift = gain_sum[0], 1
    while shift < shifts:
        gain_here = sum_step(gain_here, shift, "tp")
        shift *= 2
    (sum_gate_w,) = finish_sum(gate_sum, gate_three)
    block_out = (residual_here + mlp_out.astype(jnp.float32)).astype(jnp.bfloat16)
    block_out = reorder(place, block_out, bits, inverse=True)
    input_grad = finish_input(place, grad_attn_in, grad_residual, rows_all, g_attn, bits)
    sum_q_w, sum_k_w, sum_v_w = finish_sum(qkv_sum, qkv_three, [width_q, width_k, width_k])
    return (
        block_out,
        input_grad,
        gain_here[0],
        sum_q_w,
        sum_k_w,
        sum_v_w,
        sum_o_w.astype(jnp.float32),
        gain_here[1],
        sum_gate_w,
        sum_up_w,
        sum_down_w,
    )


def solution(mesh):
    placed = (
        P(("ctx", "tp"), None),
        P(("ctx", "tp"), None),
        P(),
        P("ctx"),
        P("ctx", "tp"),
        P("ctx", "tp"),
        P("ctx", "tp"),
        P("ctx", "tp"),
        P("ctx"),
        P("ctx", "tp"),
        P("ctx", "tp"),
        P("ctx", "tp"),
    )
    return jax.shard_map(
        on_device,
        mesh=mesh,
        in_specs=placed,
        out_specs=(
            P(("ctx", "tp"), None),
            P(("ctx", "tp"), None),
            P("ctx"),
            P("ctx", "tp"),
            P("ctx", "tp"),
            P("ctx", "tp"),
            P("ctx", "tp"),
            P("ctx"),
            P("ctx", "tp"),
            P("ctx", "tp"),
            P("ctx", "tp"),
        ),
        check_vma=False,
    )
```

```python
import functools
import math

import jax
import jax.numpy as jnp
from jax import lax
from jax.experimental import pallas as pl
from jax.experimental.pallas import tpu as pltpu
from jax.sharding import PartitionSpec as P

HEAD_SIZE = 64
LANES = 128
KERNEL_VMEM = 56 * 1024 * 1024

eps_norm = 1e-05
big_negative = -1e30

in_smem = pl.BlockSpec(memory_space=pltpu.SMEM)
in_vmem = pl.BlockSpec(memory_space=pltpu.VMEM)
unread = pl.BlockSpec(memory_space=pl.ANY)


def kernel_params():
    return pltpu.CompilerParams(vmem_limit_bytes=KERNEL_VMEM)


def cost(micros):
    return pl.CostEstimate(flops=int(micros * 1.1e9), bytes_accessed=1024, transcendentals=0)


def gated(value, *others):
    return pl.pallas_call(
        lambda *refs: None,
        out_shape=jax.ShapeDtypeStruct(value.shape, value.dtype),
        in_specs=[unread] * (1 + len(others)),
        out_specs=unread,
        input_output_aliases={0: 0},
        cost_estimate=cost(0.1),
        name="gated",
    )(value, *others)


def bit_order(bits):
    return [1, 2, 0] + list(range(3, bits)) if bits >= 3 else list(range(bits))


def block_key(position, bits):
    key = 0
    for place, bit in enumerate(bit_order(bits)):
        key = key | (((position >> place) & 1) << bit)
    return key


def key_position(key, bits):
    position = 0
    for place, bit in enumerate(bit_order(bits)):
        position = position | (((key >> bit) & 1) << place)
    return position


def swap(array, bit, bits):
    return lax.ppermute(array, "ctx", [(i, i ^ (1 << bit)) for i in range(1 << bits)])


def halves(array, axis):
    middle = array.shape[axis] // 2
    return (
        lax.slice_in_dim(array, 0, middle, axis=axis),
        lax.slice_in_dim(array, middle, 2 * middle, axis=axis),
    )


def gather_one(own, bits):
    first, second = bit_order(bits)[:2]
    return swap(own, first, bits), swap(own, second, bits)


def gather_two(one, bits, axis=0):
    first, second = bit_order(bits)[:2]
    lower, upper = halves(one[0], axis)[0], halves(one[1], axis)[1]
    return swap(lower, second, bits), swap(upper, first, bits)


def join(pieces, axis=0):
    shape = list(pieces[0].shape)
    shape[axis] = sum(piece.shape[axis] for piece in pieces)

    def kernel(*refs):
        in_refs, out_ref, sems = refs[: len(pieces)], refs[len(pieces)], refs[-1]
        copies, start = [], 0
        for index, in_ref in enumerate(in_refs):
            size = in_ref.shape[axis]
            place = pl.ds(start, size)
            target = out_ref.at[(slice(None),) * axis + (place,)]
            copies.append(pltpu.make_async_copy(in_ref, target, sems.at[index]))
            start += size
        for copy in copies:
            copy.start()
        for copy in copies:
            copy.wait()

    return pl.pallas_call(
        kernel,
        out_shape=jax.ShapeDtypeStruct(shape, pieces[0].dtype),
        in_specs=[unread] * len(pieces),
        out_specs=in_vmem,
        scratch_shapes=[pltpu.SemaphoreType.DMA((len(pieces),))],
        compiler_params=kernel_params(),
        cost_estimate=cost(0.1),
        name="join",
    )(*pieces)


def gather_end(own, one, two, bits, axis=0):
    parts = [join([own, *one, *two], axis)]
    for bit in bit_order(bits)[2:]:
        parts = parts + [swap(part, bit, bits) for part in parts]
    return parts


def gather_small(own, bits):
    stacked = own[None]
    for bit in bit_order(bits):
        stacked = jnp.concatenate([stacked, swap(stacked, bit, bits)], axis=0)
    return stacked


def scatter_step(stacked, bit, bits):
    kept = stacked.shape[0] // 2
    return stacked[:kept] + swap(stacked[kept:], bit, bits)


def sum_step(array, shift, axis):
    size = lax.axis_size(axis)
    return array + lax.ppermute(array, axis, [(i, i ^ shift) for i in range(size)])


def add_half(left, right):
    return (left.astype(jnp.float32) + right.astype(jnp.float32)).astype(jnp.bfloat16)


def scatter_one(blocks, bits):
    first, second = bit_order(bits)[:2]
    return swap(blocks[3], second, bits), swap(blocks[4], first, bits)


def scatter_two(blocks, one):
    rows, width = blocks[1].shape
    half = rows // 2

    def kernel(first_ref, second_ref, lower_ref, upper_ref, to_first, to_second):
        to_first[0:half, :] = add_half(first_ref[0:half, :], lower_ref[...])
        to_first[half:, :] = first_ref[half:, :]
        to_second[0:half, :] = second_ref[0:half, :]
        to_second[half:, :] = add_half(second_ref[half:, :], upper_ref[...])

    return pl.pallas_call(
        kernel,
        out_shape=[jax.ShapeDtypeStruct((rows, width), jnp.bfloat16)] * 2,
        in_specs=[in_vmem] * 4,
        out_specs=[in_vmem] * 2,
        compiler_params=kernel_params(),
        cost_estimate=cost(0.1),
        name="scatter_two",
    )(blocks[1], blocks[2], *one)


def scatter_three(two, bits):
    first, second = bit_order(bits)[:2]
    return swap(two[0], first, bits), swap(two[1], second, bits)


def finish_sum(blocks, three, widths=None):
    rows, width = blocks[0].shape
    widths = widths or [width]

    def kernel(own_ref, first_ref, second_ref, *out_refs):
        start = 0
        for out_ref in out_refs:
            here = slice(start, start + out_ref.shape[1])
            total = own_ref[:, here].astype(jnp.float32) + first_ref[:, here].astype(jnp.float32)
            out_ref[...] = total + second_ref[:, here].astype(jnp.float32)
            start += out_ref.shape[1]

    return pl.pallas_call(
        kernel,
        out_shape=[jax.ShapeDtypeStruct((rows, each), jnp.float32) for each in widths],
        in_specs=[in_vmem] * 3,
        out_specs=[in_vmem] * len(widths),
        compiler_params=kernel_params(),
        cost_estimate=cost(0.1),
        name="finish_sum",
    )(blocks[0], *three)


def sum_small(array, axis):
    size = lax.axis_size(axis)
    shift = 1
    while shift < size:
        array = array + lax.ppermute(array, axis, [(i, i ^ shift) for i in range(size)])
        shift *= 2
    return array


def tp_shift(array, distance):
    size = lax.axis_size("tp")
    return lax.ppermute(array, "tp", [(i, (i + distance) % size) for i in range(size)])


def tp_gather(array):
    return [array] + [tp_shift(array, d) for d in range(1, lax.axis_size("tp"))]


def tp_ordered(pieces, tp):
    stacked = jnp.stack(pieces)
    count = len(pieces)
    return jnp.concatenate(
        [lax.dynamic_index_in_dim(stacked, (tp - j) % count, 0, keepdims=False) for j in range(count)]
    )


def tp_exchange(array):
    return [array[0]] + [tp_shift(array[d], d) for d in range(1, array.shape[0])]


def tp_sum(pieces):
    return sum(piece.astype(jnp.float32) for piece in pieces)


def after(value, *others):
    return lax.optimization_barrier((value, *others))


def to_relative(array, me, bits):
    width = array.shape[1] // (1 << bits)
    return jnp.concatenate(
        [
            lax.dynamic_slice_in_dim(array, (me ^ block_key(p, bits)) * width, width, 1)
            for p in range(1 << bits)
        ],
        axis=1,
    )


def to_absolute(array, me, bits):
    width = array.shape[1] // (1 << bits)
    return jnp.concatenate(
        [
            lax.dynamic_slice_in_dim(array, key_position(me ^ c, bits) * width, width, 1)
            for c in range(1 << bits)
        ],
        axis=1,
    )


def reorder(place, array, bits, inverse=False):
    width = array.shape[1] // (1 << bits)
    if width % LANES:
        return (to_absolute if inverse else to_relative)(array, place[0], bits)

    def kernel(place, in_ref, out_ref):
        for p in range(1 << bits):
            other = pl.multiple_of((place[0] ^ block_key(p, bits)) * width, LANES)
            if inverse:
                out_ref[:, pl.ds(other, width)] = in_ref[:, p * width : (p + 1) * width]
            else:
                out_ref[:, p * width : (p + 1) * width] = in_ref[:, pl.ds(other, width)]

    return pl.pallas_call(
        kernel,
        out_shape=jax.ShapeDtypeStruct(array.shape, array.dtype),
        in_specs=[in_smem, in_vmem],
        out_specs=in_vmem,
        compiler_params=kernel_params(),
        cost_estimate=cost(0.1),
        name="reorder",
    )(place, array)


def block_positions(pair_slot, block_len):
    pair_count = pair_slot.shape[0]
    offsets = jnp.arange(2 * block_len, dtype=jnp.int32)
    lower_half = offsets < block_len
    block_index = jnp.where(
        lower_half[None, :], pair_slot[:, None], 2 * pair_count - 1 - pair_slot[:, None]
    )
    return (block_index * block_len + (offsets % block_len)[None, :]).reshape(-1)


def inverse_freqs(head_dim):
    exponent = jnp.arange(0, head_dim, 2).astype(jnp.float32) / head_dim
    base_freq = 500000.0 ** (-exponent)
    wavelength = 2.0 * math.pi / base_freq
    smooth = (8192.0 / wavelength - 1.0) / 3.0
    blended = (1.0 - smooth) * base_freq / 32.0 + smooth * base_freq
    scaled = jnp.where(wavelength > 8192.0, base_freq / 32.0, base_freq)
    middle = (wavelength >= 2048.0) & (wavelength <= 8192.0)
    return jnp.where(middle, blended, scaled)


def rope_tables(positions):
    angles = positions.astype(jnp.float32)[:, None] * inverse_freqs(HEAD_SIZE)[None, :]
    wide = LANES // (HEAD_SIZE // 2)
    return (jnp.tile(jnp.cos(angles), (1, wide)), jnp.tile(jnp.sin(angles), (1, wide)))


def rms_scale(values):
    return lax.rsqrt(jnp.mean(values * values, axis=-1, keepdims=True) + eps_norm)


def norm_back(gradient, normed, factor):
    return factor * (gradient - normed * jnp.mean(gradient * normed, axis=-1, keepdims=True))


def inner_rows(left, right):
    return lax.dot_general(
        left, right, (((0,), (0,)), ((), ())), preferred_element_type=jnp.float32
    )


def nt(left, right):
    return lax.dot_general(
        left, right, (((1,), (1,)), ((), ())), preferred_element_type=jnp.float32
    )


def nn(left, right):
    return lax.dot_general(
        left, right, (((1,), (0,)), ((), ())), preferred_element_type=jnp.float32
    )


def turned_lanes(values):
    half = HEAD_SIZE // 2
    lane = lax.broadcasted_iota(jnp.int32, values.shape, 1)
    up = pltpu.roll(values, LANES - half, 1)
    down = pltpu.roll(values, half, 1)
    return jnp.where(lane % HEAD_SIZE < half, -up, down)


def rotate(values, cosine, sine):
    return values * cosine + turned_lanes(values) * sine


def rotate_back(gradient, cosine, sine):
    return gradient * cosine - turned_lanes(gradient * sine)


def norm_rows(place, rows, gain, bits):
    width = rows.shape[1] // (1 << bits)
    whole_lanes = width % LANES == 0
    if not whole_lanes:
        rows = to_relative(rows, place[0], bits)

    def kernel(place, in_ref, gain_ref, rows_ref, out_ref):
        for p in range(1 << bits):
            here = slice(p * width, (p + 1) * width)
            if whole_lanes:
                other = pl.multiple_of((place[0] ^ block_key(p, bits)) * width, LANES)
                rows_ref[:, here] = in_ref[:, pl.ds(other, width)]
        if not whole_lanes:
            rows_ref[...] = in_ref[...]
        values = rows_ref[...].astype(jnp.float32)
        out_ref[...] = (values * rms_scale(values) * gain_ref[...]).astype(jnp.bfloat16)

    shape = jax.ShapeDtypeStruct(rows.shape, jnp.bfloat16)
    return pl.pallas_call(
        kernel,
        out_shape=(shape, shape),
        in_specs=[in_smem, in_vmem, in_vmem],
        out_specs=(in_vmem, in_vmem),
        compiler_params=kernel_params(),
        cost_estimate=cost(0.1),
        name="norm_rows",
    )(place, rows, gain)


def qkv_kernel(count, x_ref, *refs):
    weights, (cos_ref, sin_ref), (q_ref, kv_ref) = refs[:count], refs[count : count + 2], refs[-2:]
    depth = x_ref.shape[1] // count
    width_q = q_ref.shape[1]
    width_k = kv_ref.shape[1] // 2
    total = width_q + 2 * width_k
    tile = 2 * LANES
    for start in range(0, total, tile):
        product = 0.0
        for index, weight in enumerate(weights):
            product = product + nn(
                x_ref[:, index * depth : (index + 1) * depth], weight[:, start : start + tile]
            )
        for offset in range(0, tile, LANES):
            at = start + offset
            piece = product[:, offset : offset + LANES]
            if at < width_q + width_k:
                piece = rotate(piece, cos_ref[...], sin_ref[...])
            piece = piece.astype(jnp.bfloat16)
            if at < width_q:
                q_ref[:, at : at + LANES] = piece
            else:
                kv_ref[:, at - width_q : at - width_q + LANES] = piece


def project_qkv(attn_in, weights, cosine, sine, width_q, width_k, after=()):
    rows, depth = attn_in.shape
    return pl.pallas_call(
        functools.partial(qkv_kernel, len(weights)),
        out_shape=(
            jax.ShapeDtypeStruct((rows, width_q), jnp.bfloat16),
            jax.ShapeDtypeStruct((rows, 2 * width_k), jnp.bfloat16),
        ),
        in_specs=[in_vmem] * (3 + len(weights)) + [unread] * len(after),
        out_specs=(in_vmem, in_vmem),
        compiler_params=kernel_params(),
        cost_estimate=cost(0.1),
        name="qkv",
    )(attn_in, *weights, cosine, sine, *after)


def sequence_block(slots, me, half_block, bits):
    slot = slots[me ^ block_key(half_block // 2, bits)]
    return jnp.where(half_block % 2 == 0, slot, 2 * (1 << bits) - 1 - slot)


def head_lanes(pair, head, heads_per_kv, scale):
    wide = pair.astype(jnp.float32) * scale
    group = head // heads_per_kv
    source = wide if head % 2 == group else pltpu.roll(wide, HEAD_SIZE, 1)
    low = lax.broadcasted_iota(jnp.int32, wide.shape, 1) < HEAD_SIZE
    keep = low if group == 0 else jnp.logical_not(low)
    return jnp.where(keep, source, 0.0).astype(jnp.bfloat16)


def causal_tile(size):
    key_at = lax.broadcasted_iota(jnp.int32, (size, size), 0)
    row_at = lax.broadcasted_iota(jnp.int32, (size, size), 1)
    return key_at <= row_at


def over_blocks(visit, slots, me, bits, half, prepare):
    visit(0, 0, True, True, True)
    visit(1, half, True, True, True)
    visit(1, 0, False, False, False)
    own = slots[me]
    blocks_of_query = (own, 2 * (1 << bits) - 1 - own)

    def step(index, carry):
        block = sequence_block(slots, me, index, bits)
        start = pl.multiple_of(index * half, half)
        prepare(start)
        for q_half in range(2):

            @pl.when(block < blocks_of_query[q_half])
            def _():
                visit(q_half, start, False, False, False)

        return carry

    lax.fori_loop(2, 2 * (1 << bits), step, 0)


def forward_kernel(bits, heads, slots, place, q_ref, kv_ref, *refs):
    out_ref, exact_ref, log_ref, qp, run_max, run_sum, acc = refs[-7:]
    rows = q_ref.shape[0]
    half = rows // 2
    per_kv = heads // 2
    for head in range(heads):
        lanes = pl.ds((head // 2) * LANES, LANES)
        qp[head] = head_lanes(q_ref[:, lanes], head, per_kv, HEAD_SIZE ** (-0.5))

    def visit(q_half, key_start, diagonal, first, _):
        keys = kv_ref[pl.ds(key_start, half), 0:LANES]
        values_t = kv_ref[pl.ds(key_start, half), LANES : 2 * LANES].T
        base = q_half * heads
        span = pl.ds(q_half * half, half)
        scores = [nt(keys, qp[head, span, :]) for head in range(heads)]
        if diagonal:
            visible = causal_tile(half)
            scores = [jnp.where(visible, score, big_negative) for score in scores]
        peaks = [jnp.max(score, axis=0, keepdims=True) for score in scores]
        if not first:
            before = [run_max[base + head] for head in range(heads)]
            peaks = [jnp.maximum(peak, old) for peak, old in zip(peaks, before)]
        weights = [jnp.exp(score - peak) for score, peak in zip(scores, peaks)]
        totals = [jnp.sum(weight, axis=0, keepdims=True) for weight in weights]
        outs = []
        for head, weight in enumerate(weights):
            group = head // per_kv
            some = values_t[group * HEAD_SIZE : (group + 1) * HEAD_SIZE]
            outs.append(nn(some, weight.astype(jnp.bfloat16)))
        if not first:
            fades = [jnp.exp(old - peak) for old, peak in zip(before, peaks)]
            totals = [t + run_sum[base + h] * f for h, (t, f) in enumerate(zip(totals, fades))]
            outs = [o + acc[base + h] * f for h, (o, f) in enumerate(zip(outs, fades))]
        for head in range(heads):
            run_max[base + head] = peaks[head]
            run_sum[base + head] = totals[head]
            acc[base + head] = outs[head]

    over_blocks(visit, slots, place[0], bits, half, lambda start: None)
    for q_half in range(2):
        span = pl.ds(q_half * half, half)
        for pair in range(heads // 2):
            parts = []
            for head in (2 * pair, 2 * pair + 1):
                slot = q_half * heads + head
                parts.append(acc[slot] / run_sum[slot])
                log_ref[pl.ds(head, 1), span] = run_max[slot] + jnp.log(run_sum[slot])
            exact = jnp.concatenate(parts, axis=0).T
            exact_ref[span, pl.ds(pair * LANES, LANES)] = exact
            out_ref[span, pl.ds(pair * LANES, LANES)] = exact.astype(jnp.bfloat16)


def attend_forward(slots, place, queries, kv, bits, after=()):
    rows, width = queries.shape
    heads = width // HEAD_SIZE
    half = rows // 2
    return pl.pallas_call(
        functools.partial(forward_kernel, bits, heads),
        out_shape=(
            jax.ShapeDtypeStruct((rows, width), jnp.bfloat16),
            jax.ShapeDtypeStruct((rows, width), jnp.float32),
            jax.ShapeDtypeStruct((heads, rows), jnp.float32),
        ),
        in_specs=[in_smem, in_smem, in_vmem, in_vmem] + [unread] * len(after),
        out_specs=(in_vmem, in_vmem, in_vmem),
        scratch_shapes=[
            pltpu.VMEM((heads, rows, LANES), jnp.bfloat16),
            pltpu.VMEM((2 * heads, 1, half), jnp.float32),
            pltpu.VMEM((2 * heads, 1, half), jnp.float32),
            pltpu.VMEM((2 * heads, HEAD_SIZE, half), jnp.float32),
        ],
        compiler_params=kernel_params(),
        cost_estimate=cost(19),
        name="attention_forward",
    )(slots, place, queries, kv, *after)


def backward_kernel(bits, heads, slots, place, *refs):
    q_ref, kv_ref, do_ref, exact_ref, log_ref, cos_ref, sin_ref = refs[:7]
    parts = max(1, (1 << bits) // 4)
    dq_ref, dkv_refs = refs[-7 - parts], refs[-6 - parts : -6]
    qp, dop, dots, dq_acc, dkv_acc, do_all = refs[-6:]
    rows = q_ref.shape[0]
    half = rows // 2
    per_kv = heads // 2
    shifts, local, _ = do_ref.shape
    for shift in range(shifts):
        source = lax.rem(place[1] - shift + shifts, shifts)
        do_all[pl.ds(pl.multiple_of(source * local, local), local), :] = do_ref[shift]
    for head in range(heads):
        lanes = pl.ds((head // 2) * LANES, LANES)
        qp[head] = head_lanes(q_ref[:, lanes], head, per_kv, HEAD_SIZE ** (-0.5))
        dop[head] = head_lanes(do_all[:, lanes], head, per_kv, 1.0)
    for pair in range(heads // 2):
        lanes = pl.ds(pair * LANES, LANES)
        product = (do_all[:, lanes].astype(jnp.float32) * exact_ref[:, lanes]).T
        dots[pl.ds(2 * pair, 1), :] = jnp.sum(product[:HEAD_SIZE], axis=0, keepdims=True)
        dots[pl.ds(2 * pair + 1, 1), :] = jnp.sum(product[HEAD_SIZE:], axis=0, keepdims=True)

    def clear(start):
        dkv_acc[pl.ds(start, half), :] = jnp.zeros((half, 2 * LANES), jnp.float32)

    def visit(q_half, key_start, diagonal, first_query, first_key):
        rows_of_key = pl.ds(key_start, half)
        keys = kv_ref[rows_of_key, 0:LANES]
        values = kv_ref[rows_of_key, LANES : 2 * LANES]
        keys_t = keys.T
        base = q_half * heads
        span = pl.ds(q_half * half, half)
        q_heads = [qp[head, span, :] for head in range(heads)]
        do_heads = [dop[head, span, :] for head in range(heads)]
        scores = [nt(keys, q_head) for q_head in q_heads]
        grad_ws = [nt(values, do_head) for do_head in do_heads]
        weights = [
            jnp.exp(score - log_ref[pl.ds(head, 1), span]) for head, score in enumerate(scores)
        ]
        if diagonal:
            visible = causal_tile(half)
            weights = [jnp.where(visible, weight, 0.0) for weight in weights]
        grad_ss = [
            (weight * (grad_w - dots[pl.ds(head, 1), span])).astype(jnp.bfloat16)
            for head, (weight, grad_w) in enumerate(zip(weights, grad_ws))
        ]
        weights = [weight.astype(jnp.bfloat16) for weight in weights]
        grad_v = jnp.zeros((half, LANES), jnp.float32)
        grad_k = jnp.zeros((half, LANES), jnp.float32)
        for weight, do_head in zip(weights, do_heads):
            grad_v = grad_v + nn(weight, do_head)
        for grad_s, q_head in zip(grad_ss, q_heads):
            grad_k = grad_k + nn(grad_s, q_head)
        for head, grad_s in enumerate(grad_ss):
            group = head // per_kv
            grad_q = nn(keys_t[group * HEAD_SIZE : (group + 1) * HEAD_SIZE], grad_s)
            if not first_query:
                grad_q = grad_q + dq_acc[base + head]
            dq_acc[base + head] = grad_q
        if not first_key:
            grad_k = grad_k + dkv_acc[rows_of_key, 0:LANES]
            grad_v = grad_v + dkv_acc[rows_of_key, LANES : 2 * LANES]
        dkv_acc[rows_of_key, 0:LANES] = grad_k
        dkv_acc[rows_of_key, LANES : 2 * LANES] = grad_v

    over_blocks(visit, slots, place[0], bits, half, clear)
    size = dkv_acc.shape[0] // parts
    for part, dkv_ref in enumerate(dkv_refs):
        dkv_ref[...] = dkv_acc[part * size : (part + 1) * size, :].astype(jnp.bfloat16)
    for q_half in range(2):
        span = pl.ds(q_half * half, half)
        for pair in range(heads // 2):
            slot = q_half * heads + 2 * pair
            gradient = jnp.concatenate([dq_acc[slot], dq_acc[slot + 1]], axis=0).T
            gradient = rotate_back(
                gradient * HEAD_SIZE ** (-0.5), cos_ref[span, :], sin_ref[span, :]
            )
            dq_ref[span, pl.ds(pair * LANES, LANES)] = gradient.astype(jnp.bfloat16)


def attend_backward(
    slots, place, queries, kv, grad_parts, exact, log_total, cosine, sine, bits, after=()
):
    parts = max(1, (1 << bits) // 4)
    rows, width = queries.shape
    heads = width // HEAD_SIZE
    half = rows // 2
    return pl.pallas_call(
        functools.partial(backward_kernel, bits, heads),
        out_shape=(
            jax.ShapeDtypeStruct((rows, width), jnp.bfloat16),
            *[jax.ShapeDtypeStruct((kv.shape[0] // parts, kv.shape[1]), jnp.bfloat16)] * parts,
        ),
        in_specs=[in_smem, in_smem] + [in_vmem] * 7 + [unread] * len(after),
        out_specs=(in_vmem,) * (1 + parts),
        scratch_shapes=[
            pltpu.VMEM((heads, rows, LANES), jnp.bfloat16),
            pltpu.VMEM((heads, rows, LANES), jnp.bfloat16),
            pltpu.VMEM((heads, rows), jnp.float32),
            pltpu.VMEM((2 * heads, HEAD_SIZE, half), jnp.float32),
            pltpu.VMEM(kv.shape, jnp.float32),
            pltpu.VMEM((rows, width), jnp.bfloat16),
        ],
        compiler_params=kernel_params(),
        cost_estimate=cost(30),
        name="attention_backward",
    )(slots, place, queries, kv, grad_parts, exact, log_total, cosine, sine, *after)


def grad_qkv_kernel(dq_ref, own_ref, first_ref, second_ref, cos_ref, sin_ref, out_ref):
    width_q = dq_ref.shape[1]
    out_ref[:, 0:width_q] = dq_ref[...]
    total = own_ref[...].astype(jnp.float32) + first_ref[...].astype(jnp.float32)
    total = total + second_ref[...].astype(jnp.float32)
    keys = rotate_back(total[:, 0:LANES], cos_ref[...], sin_ref[...])
    out_ref[:, width_q : width_q + LANES] = keys.astype(jnp.bfloat16)
    out_ref[:, width_q + LANES :] = total[:, LANES:].astype(jnp.bfloat16)


def join_grad_qkv(grad_queries, pieces, cosine, sine):
    rows, width_q = grad_queries.shape
    width = width_q + pieces[0].shape[1]
    return pl.pallas_call(
        grad_qkv_kernel,
        out_shape=jax.ShapeDtypeStruct((rows, width), jnp.bfloat16),
        in_specs=[in_vmem] * 6,
        out_specs=in_vmem,
        compiler_params=kernel_params(),
        cost_estimate=cost(0.1),
        name="grad_qkv",
    )(grad_queries, *pieces, cosine, sine)


def mlp_kernel(count, x_ref, g_ref, *refs):
    weights = refs[:count], refs[count : 2 * count], refs[2 * count : 3 * count]
    hidden_ref, grad_gate_ref, grad_up_ref = refs[3 * count :]
    depth = x_ref.shape[1] // count

    def product(left, parts):
        total = 0.0
        for index, part in enumerate(parts):
            total = total + nn(left[:, index * depth : (index + 1) * depth], part[...])
        return total

    gate = product(x_ref, weights[0])
    up = product(x_ref, weights[1])
    grad_hidden = product(g_ref, weights[2])
    sigmoid = jax.nn.sigmoid(gate)
    silu = gate * sigmoid
    hidden_ref[...] = (silu * up).astype(jnp.bfloat16)
    grad_gate = grad_hidden * up * sigmoid * (1.0 + gate * (1.0 - sigmoid))
    grad_gate_ref[...] = grad_gate.astype(jnp.bfloat16)
    grad_up_ref[...] = (grad_hidden * silu).astype(jnp.bfloat16)


def mlp_inner(mlp_in, grad_rows, gates, ups, downs):
    rows, depth = mlp_in.shape
    units = gates[0].shape[1]
    count = len(gates)
    tile = min(256, units)
    whole = pl.BlockSpec((rows, depth), lambda i: (0, 0))
    part = pl.BlockSpec((depth // count, tile), lambda i: (0, i))
    out = pl.BlockSpec((rows, tile), lambda i: (0, i))
    shape = jax.ShapeDtypeStruct((rows, units), jnp.bfloat16)
    return pl.pallas_call(
        functools.partial(mlp_kernel, count),
        grid=(units // tile,),
        out_shape=(shape, shape, shape),
        in_specs=[whole, whole] + [part] * (3 * count),
        out_specs=(out, out, out),
        compiler_params=kernel_params(),
        cost_estimate=cost(0.1),
        name="mlp_inner",
    )(mlp_in, grad_rows, *gates, *ups, *downs)


def project_part(lefts, part):
    depth, rows, width = lefts.shape
    features = part.shape[1]
    tile = min(256, features)

    def kernel(left_ref, part_ref, out_ref):
        total = 0.0
        for group in range(depth):
            total = total + nt(left_ref[group], part_ref[group])
        out_ref[...] = total

    return pl.pallas_call(
        kernel,
        grid=(features // tile,),
        out_shape=jax.ShapeDtypeStruct((rows, features), jnp.float32),
        in_specs=[
            pl.BlockSpec((depth, rows, width), lambda i: (0, 0, 0)),
            pl.BlockSpec((depth, tile, width), lambda i: (0, i, 0)),
        ],
        out_specs=pl.BlockSpec((rows, tile), lambda i: (0, i)),
        compiler_params=kernel_params(),
        cost_estimate=cost(0.1),
        name="project_part",
    )(lefts, part)


def residual_kernel(place, left_ref, x_ref, gain_ref, part_ref, *refs):
    sums, (mlp_ref, here_ref, residual) = refs[:-3], refs[-3:]
    depth, rows, _ = left_ref.shape
    tile = part_ref.shape[1]
    step = pl.program_id(0)
    total = 0.0
    for group in range(depth):
        total = total + nt(left_ref[group], part_ref[group])
    residual[step] = total

    @pl.when(step == pl.num_programs(0) - 1)
    def _():
        width = x_ref.shape[1]
        before = sum(ref.shape[1] for ref in sums)
        squares = jnp.zeros((rows, 1), jnp.float32)
        pieces = []
        for ref in sums:
            pieces += [(ref, slice(k, k + tile)) for k in range(0, ref.shape[1], tile)]
        count = (width - before) // tile
        local = rows // depth
        here = pl.ds(pl.multiple_of(place[1] * local, local), local)
        for index in range(width // tile):
            columns = slice(index * tile, (index + 1) * tile)
            values = x_ref[:, columns].astype(jnp.float32)
            if index < len(pieces):
                ref, at = pieces[index]
                values = values + ref[:, at]
                ref[:, at] = values
            else:
                values = values + residual[index - len(pieces)]
                residual[index - len(pieces)] = values
            squares = squares + jnp.sum(values * values, axis=1, keepdims=True)
        factor = lax.rsqrt(squares / width + eps_norm)
        for index in range(width // tile):
            columns = slice(index * tile, (index + 1) * tile)
            if index < len(pieces):
                ref, at = pieces[index]
                values, mine = ref[:, at], ref[here, at]
            else:
                values = residual[index - len(pieces)]
                mine = residual[index - len(pieces), here, :]
            mlp_ref[:, columns] = (values * factor * gain_ref[:, columns]).astype(jnp.bfloat16)
            here_ref[:, columns] = mine


def project_residual(place, lefts, rows, gain, parts):
    depth, count, width = lefts.shape
    total = rows.shape[1]
    sums = [project_part(lefts, part) for part in parts[:-1]]
    features = parts[-1].shape[1]
    tile = min(256, features)
    whole = lambda i: (0, 0)
    return pl.pallas_call(
        residual_kernel,
        grid=(features // tile,),
        out_shape=(
            jax.ShapeDtypeStruct((count, total), jnp.bfloat16),
            jax.ShapeDtypeStruct((count // depth, total), jnp.float32),
        ),
        in_specs=[
            in_smem,
            pl.BlockSpec((depth, count, width), lambda i: (0, 0, 0)),
            pl.BlockSpec((count, total), whole),
            pl.BlockSpec((1, total), whole),
            pl.BlockSpec((depth, tile, width), lambda i: (0, i, 0)),
        ]
        + [pl.BlockSpec(each.shape, whole) for each in sums],
        out_specs=(
            pl.BlockSpec((count, total), whole),
            pl.BlockSpec((count // depth, total), whole),
        ),
        scratch_shapes=[pltpu.VMEM((features // tile, count, tile), jnp.float32)],
        compiler_params=kernel_params(),
        cost_estimate=cost(0.1),
        name="project_residual",
    )(place, lefts, rows, gain, parts[-1], *sums)


def to_features(lefts, weights, after=()):
    rows = lefts[0].shape[0]
    count = len(weights[0])
    features = weights[0][0].shape[0]
    tile = min(256, features)
    tiles = features // tile

    def kernel(*refs):
        left_refs, part_refs, out_ref = refs[: len(lefts)], refs[len(lefts) :], refs[-1]
        step = pl.program_id(0)
        for part in range(count):

            @pl.when(step // tiles == part)
            def _():
                total = 0.0
                for source, left_ref in enumerate(left_refs):
                    total = total + nt(left_ref[...], part_refs[source * count + part][...])
                out_ref[...] = total.astype(jnp.bfloat16)

    def part_at(base, i):
        return (jnp.clip(i - base, 0, tiles - 1), 0)

    return pl.pallas_call(
        kernel,
        grid=(count * tiles,),
        out_shape=jax.ShapeDtypeStruct((rows, count * features), jnp.bfloat16),
        in_specs=[pl.BlockSpec(left.shape, lambda i: (0, 0)) for left in lefts]
        + [
            pl.BlockSpec((tile, parts[part].shape[1]), functools.partial(part_at, part * tiles))
            for parts in weights
            for part in range(count)
        ]
        + [unread] * len(after),
        out_specs=pl.BlockSpec((rows, tile), lambda i: (0, i)),
        compiler_params=kernel_params(),
        cost_estimate=cost(0.1),
        name="to_features",
    )(*lefts, *[part for parts in weights for part in parts], *after)


def to_groups(place, branch, parts):
    rows, depth = branch.shape
    groups, features, width = parts[0].shape
    count = len(parts)

    def kernel(place, x_ref, *refs):
        total = 0.0
        for index, part in enumerate(refs[:count]):
            columns = x_ref[:, index * features : (index + 1) * features]
            total = total + nn(columns, part[0])
        refs[-1][0] = total.astype(jnp.bfloat16)

    def weight_at(shift, place):
        return (lax.rem(place[1] + shift, groups), 0, 0)

    return pl.pallas_call(
        kernel,
        grid_spec=pltpu.PrefetchScalarGridSpec(
            num_scalar_prefetch=1,
            grid=(groups,),
            in_specs=[pl.BlockSpec((rows, depth), lambda i, place: (0, 0))]
            + [pl.BlockSpec((1, features, width), weight_at)] * count,
            out_specs=pl.BlockSpec((1, rows, width), lambda i, place: (i, 0, 0)),
        ),
        out_shape=jax.ShapeDtypeStruct((groups, rows, width), jnp.bfloat16),
        compiler_params=kernel_params(),
        cost_estimate=cost(0.1),
        name="to_groups",
    )(place, branch, *parts)


def to_block_groups(place, rows, bits, groups):
    local, depth = rows.shape
    width = depth >> bits
    count = (1 << bits) // groups
    if width % LANES:
        blocks = to_absolute(rows, place[0], bits)
        blocks = blocks.reshape(local, groups, count, width).transpose(1, 2, 0, 3)
        return jnp.stack(
            [
                lax.dynamic_index_in_dim(blocks, (place[1] + d) % groups, 0, keepdims=False)
                for d in range(groups)
            ]
        )

    def kernel(place, in_ref, out_ref):
        for d in range(groups):
            for index in range(count):
                block = lax.rem(place[1] + d, groups) * count + index
                start = key_position(place[0] ^ block, bits) * width
                out_ref[d, index] = in_ref[:, pl.ds(pl.multiple_of(start, LANES), width)]

    return pl.pallas_call(
        kernel,
        out_shape=jax.ShapeDtypeStruct((groups, count, local, width), rows.dtype),
        in_specs=[in_smem, in_vmem],
        out_specs=in_vmem,
        compiler_params=kernel_params(),
        cost_estimate=cost(0.1),
        name="to_block_groups",
    )(place, rows)


def gradient_out(place, branch, attended, bits):
    shifts = len(branch)
    count, local, features = branch[0].shape
    groups, rows, width = attended.shape
    parts = (1 << bits) // 4

    def kernel(place, *refs):
        lefts, right_ref, outs = refs[:shifts], refs[shifts], refs[shifts + 1 :]
        for part, out_ref in enumerate(outs):
            for block in range(4):
                device = place[0] ^ block_key(4 * part + block, bits)
                index = lax.rem(device, count)
                group = device // count
                total = 0.0
                for distance, left in enumerate(lefts):
                    start = lax.rem(place[1] - distance + shifts, shifts) * local
                    here = pl.ds(pl.multiple_of(start, local), local)
                    total = total + inner_rows(left[index], right_ref[group, here, :])
                out_ref[block * features : (block + 1) * features, :] = total.astype(jnp.bfloat16)

    return pl.pallas_call(
        kernel,
        out_shape=[jax.ShapeDtypeStruct((4 * features, width), jnp.bfloat16)] * parts,
        in_specs=[in_smem] + [in_vmem] * (shifts + 1),
        out_specs=[in_vmem] * parts,
        compiler_params=kernel_params(),
        cost_estimate=cost(0.1),
        name="gradient_out",
    )(place, *branch, attended)


def to_owners(array, count):
    ctx, tp = lax.axis_size("ctx"), lax.axis_size("tp")
    moves = []
    for c in range(ctx):
        for t in range(tp):
            moves.append((c * tp + t, (count * t + c % count) * tp + c // count))
    return lax.ppermute(array, ("ctx", "tp"), moves)


def block_rows(rows):
    quarter = rows // 4
    return [quarter, quarter, quarter, quarter // 2, quarter // 2]


def gradient_part(left, right, parts, part, received=(), pieces=4, after=()):
    rows, depth = left.shape
    depth = depth // parts
    width = right.shape[1]
    tile = next(t for t in (1024, 768, 512, 256, LANES, width) if width % t == 0)
    sizes = block_rows(depth) if received else [depth // pieces] * pieces
    step = depth // max(1, len(received))

    def kernel(left_ref, right_ref, *refs):
        total = inner_rows(left_ref[...], right_ref[...])
        start = 0
        for size, out_ref in zip(sizes, refs[len(received) + len(after) :]):
            piece = total[start : start + size]
            if received:
                offset = start % step
                other = refs[start // step][offset : offset + size, :]
                piece = piece + other.astype(jnp.float32)
            out_ref[...] = piece.astype(jnp.bfloat16)
            start += size

    return pl.pallas_call(
        kernel,
        grid=(width // tile,),
        out_shape=[jax.ShapeDtypeStruct((size, width), jnp.bfloat16) for size in sizes],
        in_specs=[
            pl.BlockSpec((rows, depth), lambda i: (0, part)),
            pl.BlockSpec((rows, tile), lambda i: (0, i)),
        ]
        + [pl.BlockSpec((step, tile), lambda i: (0, i))] * len(received)
        + [unread] * len(after),
        out_specs=[pl.BlockSpec((size, tile), lambda i: (0, i)) for size in sizes],
        compiler_params=kernel_params(),
        cost_estimate=cost(0.1),
        name="gradient_part",
    )(left, right, *received, *after)


def gradient_begin(left, right, bits, pieces=4, after=()):
    parts = (1 << bits) // 4
    bit = bit_order(bits)[-1]
    return [
        [
            swap(block, bit, bits)
            for block in gradient_part(left, right, parts, part, pieces=pieces, after=after)
        ]
        for part in range(parts // 2, parts)
    ]


def gradient_end(left, right, received, bits):
    parts = (1 << bits) // 4
    if parts == 2:
        return gradient_part(left, right, parts, 0, received[0])
    kept = [jnp.concatenate(gradient_part(left, right, parts, p)) for p in range(parts // 2)]
    kept = [add_half(mine, jnp.concatenate(other)) for mine, other in zip(kept, received)]
    return sum_parts(kept, bits, bit_order(bits)[2:-1])


def finish_input(place, gradient, residual, rows, gain, bits):
    local, depth = gradient.shape
    width = depth >> bits
    whole_lanes = width % LANES == 0

    def kernel(place, grad_ref, residual_ref, rows_ref, gain_ref, out_ref, *scratch):
        start = pl.multiple_of(place[1] * local, local)
        values = rows_ref[pl.ds(start, local), :].astype(jnp.float32)
        factor = rms_scale(values)
        normed = values * factor
        scaled = grad_ref[...].astype(jnp.float32) * gain_ref[...]
        total = residual_ref[...] + norm_back(scaled, normed, factor)
        if not whole_lanes:
            out_ref[...] = total
            return
        for p in range(1 << bits):
            other = pl.multiple_of((place[0] ^ block_key(p, bits)) * width, LANES)
            out_ref[:, pl.ds(other, width)] = total[:, p * width : (p + 1) * width]

    out = pl.pallas_call(
        kernel,
        out_shape=jax.ShapeDtypeStruct((local, depth), jnp.float32),
        in_specs=[in_smem] + [in_vmem] * 4,
        out_specs=in_vmem,
        compiler_params=kernel_params(),
        cost_estimate=cost(0.1),
        name="finish_input",
    )(place, gradient, residual, rows, gain)
    return out if whole_lanes else to_absolute(out, place[0], bits)


def sum_parts(parts, bits, over):
    for bit in reversed(over):
        count = len(parts) // 2
        came = [swap(part, bit, bits) for part in parts[count:]]
        if count == 1:
            return split_blocks(parts[0], came[0])
        parts = [add_half(mine, other) for mine, other in zip(parts[:count], came)]


def split_blocks(kept, received):
    sizes = block_rows(kept.shape[0])

    def kernel(kept_ref, other_ref, *refs):
        start = 0
        for size, out_ref in zip(sizes, refs):
            here = slice(start, start + size)
            out_ref[...] = add_half(kept_ref[here, :], other_ref[here, :])
            start += size

    return pl.pallas_call(
        kernel,
        out_shape=[jax.ShapeDtypeStruct((size, kept.shape[1]), jnp.bfloat16) for size in sizes],
        in_specs=[in_vmem] * 2,
        out_specs=[in_vmem] * 5,
        compiler_params=kernel_params(),
        cost_estimate=cost(0.1),
        name="split_blocks",
    )(kept, received)


def rows_begin(parts, bits):
    return sum_parts(parts, bits, bit_order(bits)[2:])


def window(*values):
    return lax.optimization_barrier(values)


def cut(values, *sizes):
    out, start = [], 0
    for size in sizes:
        out.append(values[start : start + size])
        start += size
    return out


def on_device(
    block_in, out_grad, pair_slot, gain_attn, wq, wk, wv, wo, gain_mlp, w_gate, w_up, w_down
):
    bits = (lax.axis_size("ctx") - 1).bit_length()
    shifts = lax.axis_size("tp")
    me = lax.axis_index("ctx")
    tp = lax.axis_index("tp")
    place = jnp.stack([me, tp]).astype(jnp.int32)
    local_rows, model = block_in.shape
    group_rows = local_rows * shifts
    width_q, width_k = wq.shape[1], wk.shape[1]
    count = (1 << bits) // 4

    x_all = lax.all_gather(block_in, "tp", axis=0, tiled=True)
    qkv_here = join([wq, wk, wv], axis=1)
    qkv_one = gather_one(qkv_here, bits)
    gains = gather_small(jnp.stack([gain_attn, gain_mlp]), bits).astype(jnp.float32)
    gains = jnp.swapaxes(gains, 0, 1).reshape(2, -1)
    gate_one = gather_one(w_gate, bits)
    qkv_two = gather_two(qkv_one, bits)
    qkv_w = gather_end(qkv_here, qkv_one, qkv_two, bits)
    pos_all = block_positions(pair_slot, group_rows // 2)
    pos_rows = lax.dynamic_slice_in_dim(pos_all, me * group_rows, group_rows)
    cosine, sine = rope_tables(pos_rows)
    out_grad_here = reorder(place, out_grad, bits)
    both_sent = jnp.concatenate([out_grad_here, wo.reshape(-1, model)], axis=0)
    x_all, both_sent, w_up, gains, cosine, sine, *pieces = window(
        x_all, both_sent, w_up, gains, cosine, sine, *qkv_w, *gate_one
    )
    qkv_w, gate_one = cut(pieces, count, 2)

    g_attn, g_mlp = gains[0:1], gains[1:2]
    both_all = lax.all_gather(both_sent, "tp", axis=0)
    gate_two = gather_two(gate_one, bits)
    rows_all, attn_in = norm_rows(place, x_all, g_attn, bits)
    queries, kv = project_qkv(attn_in, qkv_w, cosine, sine, width_q, width_k)
    kv_one = gather_one(kv, bits)
    kv_all = join(gather_end(kv, kv_one, gather_two(kv_one, bits), bits))
    kv_all, w_up, w_down = window(kv_all, w_up, w_down)

    up_one = gather_one(w_up, bits)
    attended, exact, log_total = attend_forward(pair_slot, place, queries, kv_all, bits)
    attended, both_all, w_down, *pieces = window(
        attended, both_all, w_down, *gate_two, *up_one
    )
    gate_two, up_one = cut(pieces, 2, 2)

    attended_all = lax.all_gather(attended, "tp", axis=0)
    grad_rows = both_all[:, :local_rows].reshape(group_rows, model)
    wo_groups = both_all[:, local_rows:].reshape(shifts, *wo.shape)
    o_one = gather_one(wo_groups, bits)
    up_two = gather_two(up_one, bits)
    o_two = gather_two(o_one, bits, 1)
    gate_w = gather_end(w_gate, gate_one, gate_two, bits)
    attended_all, grad_rows, w_down, *pieces = window(
        attended_all, grad_rows, w_down, *o_two, *up_two, *gate_w
    )
    o_two, up_two, gate_w = cut(pieces, 2, 2, count)

    down_one = gather_one(w_down, bits)
    up_w = gather_end(w_up, up_one, up_two, bits)
    o_w = gather_end(wo_groups, o_one, o_two, bits, 1)
    mlp_in, residual_here = project_residual(place, attended_all, rows_all, g_mlp, o_w)
    mlp_in, residual_here, *pieces = window(mlp_in, residual_here, *down_one, *up_w)
    down_one, up_w = cut(pieces, 2, count)
    down_two = gather_two(down_one, bits)
    down_w = gather_end(w_down, down_one, down_two, bits)
    factor_mlp = rms_scale(residual_here)
    normed_mlp = residual_here * factor_mlp

    hidden, grad_gate, grad_up = mlp_inner(mlp_in, grad_rows, gate_w, up_w, down_w)
    grad_mlp_part = to_features([grad_gate, grad_up], [gate_w, up_w])
    grad_mlp_part, hidden, grad_gate, grad_up = window(grad_mlp_part, hidden, grad_gate, grad_up)

    grad_mlp_in = lax.psum_scatter(grad_mlp_part, "tp", scatter_dimension=0, tiled=True)
    down_sum = gradient_begin(grad_rows, hidden, bits)
    up_sum = gradient_begin(mlp_in, grad_up, bits)
    gate_sum = gradient_begin(mlp_in, grad_gate, bits)
    down_sum = gradient_end(grad_rows, hidden, down_sum, bits)
    up_sum = gradient_end(mlp_in, grad_up, up_sum, bits)
    gate_sum = gradient_end(mlp_in, grad_gate, gate_sum, bits)
    down_two = scatter_two(down_sum, scatter_one(down_sum, bits))
    up_two = scatter_two(up_sum, scatter_one(up_sum, bits))
    gate_one = scatter_one(gate_sum, bits)
    mlp_part = to_features([hidden], [down_w])
    grad_mlp_in, mlp_part, *pieces = window(
        grad_mlp_in, mlp_part, *down_two, *up_two, *gate_one, *gate_sum
    )
    down_two, up_two, gate_one, gate_sum = cut(pieces, 2, 2, 2, 5)

    down_three = scatter_three(down_two, bits)
    grad_mlp_in = grad_mlp_in.astype(jnp.float32)
    gain_mlp_part = jnp.sum(grad_mlp_in * normed_mlp, axis=0, keepdims=True)
    grad_residual = out_grad_here.astype(jnp.float32) + norm_back(
        grad_mlp_in * g_mlp, normed_mlp, factor_mlp
    )
    branch_here = grad_residual.astype(jnp.bfloat16)
    grad_groups = to_groups(place, branch_here, o_w)
    grad_parts = jnp.stack(tp_exchange(grad_groups))
    gate_two = scatter_two(gate_sum, gate_one)
    grad_parts, branch_here, mlp_part, *pieces = window(
        grad_parts, branch_here, mlp_part, *down_three, *up_two, *gate_two
    )
    down_three, up_two, gate_two = cut(pieces, 2, 2, 2)

    up_three = scatter_three(up_two, bits)
    gate_three = scatter_three(gate_two, bits)
    branch_blocks = to_block_groups(place, branch_here, bits, shifts)
    mlp_out = lax.psum_scatter(mlp_part, "tp", scatter_dimension=0, tiled=True)
    grad_queries, *grad_kv = attend_backward(
        pair_slot, place, queries, kv_all, grad_parts, exact, log_total, cosine, sine, bits
    )
    branch_blocks, *pieces = window(branch_blocks, *grad_kv, *up_three)
    grad_kv, up_three = cut(pieces, count, 2)

    kv_sum = rows_begin(grad_kv, bits)
    kv_three = scatter_three(scatter_two(kv_sum, scatter_one(kv_sum, bits)), bits)
    branch_pieces = tp_exchange(branch_blocks)
    mlp_out, *pieces = window(mlp_out, kv_sum[0], *kv_three, *branch_pieces)
    kv_pieces, branch_pieces = cut(pieces, 3, shifts)
    grad_qkv = join_grad_qkv(grad_queries, kv_pieces, cosine, sine)
    grad_attn_part = to_features([grad_qkv], [qkv_w])
    grad_attn_part, grad_qkv, *branch_pieces = window(grad_attn_part, grad_qkv, *branch_pieces)

    grad_attn_in = lax.psum_scatter(grad_attn_part, "tp", scatter_dimension=0, tiled=True)
    qkv_sum = gradient_begin(attn_in, grad_qkv, bits, pieces=1)
    qkv_sum = gradient_end(attn_in, grad_qkv, qkv_sum, bits)
    inputs = rows_all.astype(jnp.float32)
    gain_attn_part = jnp.sum(
        grad_attn_part.astype(jnp.float32) * (inputs * rms_scale(inputs)), axis=0, keepdims=True
    )
    gain_sum = jnp.concatenate([gain_attn_part, gain_mlp_part])
    gain_sum = jnp.swapaxes(gain_sum.reshape(2, 1 << bits, -1), 0, 1)
    order = bit_order(bits)
    for bit in reversed(order[2:]):
        gain_sum = scatter_step(gain_sum, bit, bits)
    o_sum = rows_begin(gradient_out(place, branch_pieces, attended_all, bits), bits)
    gain_sum, *pieces = window(gain_sum, *qkv_sum, *o_sum, *gate_three, *down_three, *up_three)
    qkv_sum, o_sum, gate_three, down_three, up_three = cut(pieces, 5, 5, 2, 2, 2)

    qkv_two = scatter_two(qkv_sum, scatter_one(qkv_sum, bits))
    o_two = scatter_two(o_sum, scatter_one(o_sum, bits))
    gain_sum = scatter_step(gain_sum, order[1], bits)
    gain_sum = scatter_step(gain_sum, order[0], bits)
    (sum_down_w,) = finish_sum(down_sum, down_three)
    pieces = window(gain_sum, *qkv_two, *o_two, *gate_three, *up_three, mlp_out, sum_down_w)
    (gain_sum,), qkv_two, o_two, gate_three, up_three, (mlp_out, sum_down_w) = cut(
        pieces, 1, 2, 2, 2, 2, 2
    )
    gate_three, up_three = list(gate_three), list(up_three)

    qkv_three, o_three = scatter_three(qkv_two, bits), scatter_three(o_two, bits)
    gain_here, shift = gain_sum[0], 1
    while shift < shifts:
        gain_here = sum_step(gain_here, shift, "tp")
        shift *= 2
    (sum_up_w,) = finish_sum(up_sum, up_three)
    input_grad = finish_input(place, grad_attn_in, grad_residual, rows_all, g_attn, bits)
    gain_here, sum_up_w, input_grad, gate_three[0], *pieces = window(
        gain_here, sum_up_w, input_grad, gate_three[0], *qkv_three, *o_three
    )
    qkv_three, o_three = cut(pieces, 2, 2)

    (sum_o_w,) = finish_sum(o_sum, o_three)
    sum_o_w = to_owners(sum_o_w.astype(jnp.bfloat16), (1 << bits) // shifts)
    (sum_gate_w,) = finish_sum(gate_sum, gate_three)
    block_out = (residual_here + mlp_out.astype(jnp.float32)).astype(jnp.bfloat16)
    block_out = reorder(place, block_out, bits, inverse=True)
    sum_q_w, sum_k_w, sum_v_w = finish_sum(qkv_sum, qkv_three, [width_q, width_k, width_k])
    return (
        block_out,
        input_grad,
        gain_here[0],
        sum_q_w,
        sum_k_w,
        sum_v_w,
        sum_o_w.astype(jnp.float32),
        gain_here[1],
        sum_gate_w,
        sum_up_w,
        sum_down_w,
    )


def solution(mesh):
    placed = (
        P(("ctx", "tp"), None),
        P(("ctx", "tp"), None),
        P(),
        P("ctx"),
        P("ctx", "tp"),
        P("ctx", "tp"),
        P("ctx", "tp"),
        P("ctx", "tp"),
        P("ctx"),
        P("ctx", "tp"),
        P("ctx", "tp"),
        P("ctx", "tp"),
    )
    return jax.shard_map(
        on_device,
        mesh=mesh,
        in_specs=placed,
        out_specs=(
            P(("ctx", "tp"), None),
            P(("ctx", "tp"), None),
            P("ctx"),
            P("ctx", "tp"),
            P("ctx", "tp"),
            P("ctx", "tp"),
            P("ctx", "tp"),
            P("ctx"),
            P("ctx", "tp"),
            P("ctx", "tp"),
            P("ctx", "tp"),
        ),
        check_vma=False,
    )
```

```python
import functools
import math

import jax
import jax.numpy as jnp
from jax import lax
from jax.experimental import pallas as pl
from jax.experimental.pallas import tpu as pltpu
from jax.sharding import PartitionSpec as P

HEAD_SIZE = 64
LANES = 128
KERNEL_VMEM = 56 * 1024 * 1024

eps_norm = 1e-05
big_negative = -1e30

in_smem = pl.BlockSpec(memory_space=pltpu.SMEM)
in_vmem = pl.BlockSpec(memory_space=pltpu.VMEM)
unread = pl.BlockSpec(memory_space=pl.ANY)


def kernel_params():
    return pltpu.CompilerParams(vmem_limit_bytes=KERNEL_VMEM)


def cost(micros):
    return pl.CostEstimate(flops=int(micros * 1.1e9), bytes_accessed=1024, transcendentals=0)


def gated(value, *others):
    return pl.pallas_call(
        lambda *refs: None,
        out_shape=jax.ShapeDtypeStruct(value.shape, value.dtype),
        in_specs=[unread] * (1 + len(others)),
        out_specs=unread,
        input_output_aliases={0: 0},
        cost_estimate=cost(0.1),
        name="gated",
    )(value, *others)


def bit_order(bits):
    return [1, 2, 0] + list(range(3, bits)) if bits >= 3 else list(range(bits))


def block_key(position, bits):
    key = 0
    for place, bit in enumerate(bit_order(bits)):
        key = key | (((position >> place) & 1) << bit)
    return key


def key_position(key, bits):
    position = 0
    for place, bit in enumerate(bit_order(bits)):
        position = position | (((key >> bit) & 1) << place)
    return position


def swap(array, bit, bits):
    return lax.ppermute(array, "ctx", [(i, i ^ (1 << bit)) for i in range(1 << bits)])


def halves(array, axis):
    middle = array.shape[axis] // 2
    return (
        lax.slice_in_dim(array, 0, middle, axis=axis),
        lax.slice_in_dim(array, middle, 2 * middle, axis=axis),
    )


def gather_one(own, bits):
    first, second = bit_order(bits)[:2]
    return swap(own, first, bits), swap(own, second, bits)


def gather_two(one, bits, axis=0):
    first, second = bit_order(bits)[:2]
    lower, upper = halves(one[0], axis)[0], halves(one[1], axis)[1]
    return swap(lower, second, bits), swap(upper, first, bits)


def join(pieces, axis=0):
    shape = list(pieces[0].shape)
    shape[axis] = sum(piece.shape[axis] for piece in pieces)
    count = len(pieces)

    def kernel(*refs):
        in_refs, out_ref, buffer, in_sems, out_sems = refs[:count], *refs[count:]
        brought, sent, start = [], [], 0
        for index, in_ref in enumerate(in_refs):
            size = in_ref.shape[axis]
            here = (slice(None),) * axis + (pl.ds(start, size),)
            brought.append(pltpu.make_async_copy(in_ref, buffer.at[here], in_sems.at[index]))
            sent.append(
                pltpu.make_async_copy(buffer.at[here], out_ref.at[here], out_sems.at[index])
            )
            start += size
        for copy in brought:
            copy.start()
        for bring, send in zip(brought, sent):
            bring.wait()
            send.start()
        for copy in sent:
            copy.wait()

    return pl.pallas_call(
        kernel,
        out_shape=jax.ShapeDtypeStruct(shape, pieces[0].dtype),
        in_specs=[unread] * count,
        out_specs=unread,
        scratch_shapes=[
            pltpu.VMEM(tuple(shape), pieces[0].dtype),
            pltpu.SemaphoreType.DMA((count,)),
            pltpu.SemaphoreType.DMA((count,)),
        ],
        compiler_params=kernel_params(),
        cost_estimate=cost(0.1),
        name="join",
    )(*pieces)


def gather_end(own, one, two, bits, axis=0):
    parts = [join([own, *one, *two], axis)]
    for bit in bit_order(bits)[2:]:
        parts = parts + [swap(part, bit, bits) for part in parts]
    return parts


def gather_small(own, bits):
    stacked = own[None]
    for bit in bit_order(bits):
        stacked = jnp.concatenate([stacked, swap(stacked, bit, bits)], axis=0)
    return stacked


def scatter_step(stacked, bit, bits):
    kept = stacked.shape[0] // 2
    return stacked[:kept] + swap(stacked[kept:], bit, bits)


def sum_step(array, shift, axis):
    size = lax.axis_size(axis)
    return array + lax.ppermute(array, axis, [(i, i ^ shift) for i in range(size)])


def add_half(left, right):
    return (left.astype(jnp.float32) + right.astype(jnp.float32)).astype(jnp.bfloat16)


def scatter_one(blocks, bits):
    first, second = bit_order(bits)[:2]
    return swap(blocks[3], second, bits), swap(blocks[4], first, bits)


def scatter_two(blocks, one):
    rows, width = blocks[1].shape
    half = rows // 2

    def kernel(first_ref, second_ref, lower_ref, upper_ref, to_first, to_second):
        to_first[0:half, :] = add_half(first_ref[0:half, :], lower_ref[...])
        to_first[half:, :] = first_ref[half:, :]
        to_second[0:half, :] = second_ref[0:half, :]
        to_second[half:, :] = add_half(second_ref[half:, :], upper_ref[...])

    return pl.pallas_call(
        kernel,
        out_shape=[jax.ShapeDtypeStruct((rows, width), jnp.bfloat16)] * 2,
        in_specs=[in_vmem] * 4,
        out_specs=[in_vmem] * 2,
        compiler_params=kernel_params(),
        cost_estimate=cost(0.1),
        name="scatter_two",
    )(blocks[1], blocks[2], *one)


def scatter_three(two, bits):
    first, second = bit_order(bits)[:2]
    return swap(two[0], first, bits), swap(two[1], second, bits)


def finish_sum(blocks, three, widths=None):
    rows, width = blocks[0].shape
    widths = widths or [width]

    def kernel(own_ref, first_ref, second_ref, *out_refs):
        start = 0
        for out_ref in out_refs:
            here = slice(start, start + out_ref.shape[1])
            total = own_ref[:, here].astype(jnp.float32) + first_ref[:, here].astype(jnp.float32)
            out_ref[...] = total + second_ref[:, here].astype(jnp.float32)
            start += out_ref.shape[1]

    return pl.pallas_call(
        kernel,
        out_shape=[jax.ShapeDtypeStruct((rows, each), jnp.float32) for each in widths],
        in_specs=[in_vmem] * 3,
        out_specs=[in_vmem] * len(widths),
        compiler_params=kernel_params(),
        cost_estimate=cost(0.1),
        name="finish_sum",
    )(blocks[0], *three)


def sum_small(array, axis):
    size = lax.axis_size(axis)
    shift = 1
    while shift < size:
        array = array + lax.ppermute(array, axis, [(i, i ^ shift) for i in range(size)])
        shift *= 2
    return array


def tp_shift(array, distance):
    size = lax.axis_size("tp")
    return lax.ppermute(array, "tp", [(i, (i + distance) % size) for i in range(size)])


def tp_gather(array):
    return [array] + [tp_shift(array, d) for d in range(1, lax.axis_size("tp"))]


def tp_ordered(pieces, tp):
    stacked = jnp.stack(pieces)
    count = len(pieces)
    return jnp.concatenate(
        [lax.dynamic_index_in_dim(stacked, (tp - j) % count, 0, keepdims=False) for j in range(count)]
    )


def tp_exchange(array):
    return [array[0]] + [tp_shift(array[d], d) for d in range(1, array.shape[0])]


def tp_sum(pieces):
    return sum(piece.astype(jnp.float32) for piece in pieces)


def after(value, *others):
    return lax.optimization_barrier((value, *others))


def to_relative(array, me, bits):
    width = array.shape[1] // (1 << bits)
    return jnp.concatenate(
        [
            lax.dynamic_slice_in_dim(array, (me ^ block_key(p, bits)) * width, width, 1)
            for p in range(1 << bits)
        ],
        axis=1,
    )


def to_absolute(array, me, bits):
    width = array.shape[1] // (1 << bits)
    return jnp.concatenate(
        [
            lax.dynamic_slice_in_dim(array, key_position(me ^ c, bits) * width, width, 1)
            for c in range(1 << bits)
        ],
        axis=1,
    )


def reorder(place, array, bits, inverse=False):
    width = array.shape[1] // (1 << bits)
    if width % LANES:
        return (to_absolute if inverse else to_relative)(array, place[0], bits)

    def kernel(place, in_ref, out_ref):
        for p in range(1 << bits):
            other = pl.multiple_of((place[0] ^ block_key(p, bits)) * width, LANES)
            if inverse:
                out_ref[:, pl.ds(other, width)] = in_ref[:, p * width : (p + 1) * width]
            else:
                out_ref[:, p * width : (p + 1) * width] = in_ref[:, pl.ds(other, width)]

    return pl.pallas_call(
        kernel,
        out_shape=jax.ShapeDtypeStruct(array.shape, array.dtype),
        in_specs=[in_smem, in_vmem],
        out_specs=in_vmem,
        compiler_params=kernel_params(),
        cost_estimate=cost(0.1),
        name="reorder",
    )(place, array)


def block_positions(pair_slot, block_len):
    pair_count = pair_slot.shape[0]
    offsets = jnp.arange(2 * block_len, dtype=jnp.int32)
    lower_half = offsets < block_len
    block_index = jnp.where(
        lower_half[None, :], pair_slot[:, None], 2 * pair_count - 1 - pair_slot[:, None]
    )
    return (block_index * block_len + (offsets % block_len)[None, :]).reshape(-1)


def inverse_freqs(head_dim):
    exponent = jnp.arange(0, head_dim, 2).astype(jnp.float32) / head_dim
    base_freq = 500000.0 ** (-exponent)
    wavelength = 2.0 * math.pi / base_freq
    smooth = (8192.0 / wavelength - 1.0) / 3.0
    blended = (1.0 - smooth) * base_freq / 32.0 + smooth * base_freq
    scaled = jnp.where(wavelength > 8192.0, base_freq / 32.0, base_freq)
    middle = (wavelength >= 2048.0) & (wavelength <= 8192.0)
    return jnp.where(middle, blended, scaled)


def rope_tables(positions):
    angles = positions.astype(jnp.float32)[:, None] * inverse_freqs(HEAD_SIZE)[None, :]
    wide = LANES // (HEAD_SIZE // 2)
    return (jnp.tile(jnp.cos(angles), (1, wide)), jnp.tile(jnp.sin(angles), (1, wide)))


def rms_scale(values):
    return lax.rsqrt(jnp.mean(values * values, axis=-1, keepdims=True) + eps_norm)


def norm_back(gradient, normed, factor):
    return factor * (gradient - normed * jnp.mean(gradient * normed, axis=-1, keepdims=True))


def inner_rows(left, right):
    return lax.dot_general(
        left, right, (((0,), (0,)), ((), ())), preferred_element_type=jnp.float32
    )


def nt(left, right):
    return lax.dot_general(
        left, right, (((1,), (1,)), ((), ())), preferred_element_type=jnp.float32
    )


def nn(left, right):
    return lax.dot_general(
        left, right, (((1,), (0,)), ((), ())), preferred_element_type=jnp.float32
    )


def turned_lanes(values):
    half = HEAD_SIZE // 2
    lane = lax.broadcasted_iota(jnp.int32, values.shape, 1)
    up = pltpu.roll(values, LANES - half, 1)
    down = pltpu.roll(values, half, 1)
    return jnp.where(lane % HEAD_SIZE < half, -up, down)


def rotate(values, cosine, sine):
    return values * cosine + turned_lanes(values) * sine


def rotate_back(gradient, cosine, sine):
    return gradient * cosine - turned_lanes(gradient * sine)


def norm_rows(place, rows, gain, bits):
    width = rows.shape[1] // (1 << bits)
    whole_lanes = width % LANES == 0
    if not whole_lanes:
        rows = to_relative(rows, place[0], bits)

    def kernel(place, in_ref, gain_ref, rows_ref, out_ref):
        for p in range(1 << bits):
            here = slice(p * width, (p + 1) * width)
            if whole_lanes:
                other = pl.multiple_of((place[0] ^ block_key(p, bits)) * width, LANES)
                rows_ref[:, here] = in_ref[:, pl.ds(other, width)]
        if not whole_lanes:
            rows_ref[...] = in_ref[...]
        values = rows_ref[...].astype(jnp.float32)
        out_ref[...] = (values * rms_scale(values) * gain_ref[...]).astype(jnp.bfloat16)

    shape = jax.ShapeDtypeStruct(rows.shape, jnp.bfloat16)
    return pl.pallas_call(
        kernel,
        out_shape=(shape, shape),
        in_specs=[in_smem, in_vmem, in_vmem],
        out_specs=(in_vmem, in_vmem),
        compiler_params=kernel_params(),
        cost_estimate=cost(0.1),
        name="norm_rows",
    )(place, rows, gain)


def qkv_kernel(count, x_ref, *refs):
    weights, (cos_ref, sin_ref), (q_ref, kv_ref) = refs[:count], refs[count : count + 2], refs[-2:]
    depth = x_ref.shape[1] // count
    width_q = q_ref.shape[1]
    width_k = kv_ref.shape[1] // 2
    total = width_q + 2 * width_k
    tile = 2 * LANES
    for start in range(0, total, tile):
        product = 0.0
        for index, weight in enumerate(weights):
            product = product + nn(
                x_ref[:, index * depth : (index + 1) * depth], weight[:, start : start + tile]
            )
        for offset in range(0, tile, LANES):
            at = start + offset
            piece = product[:, offset : offset + LANES]
            if at < width_q + width_k:
                piece = rotate(piece, cos_ref[...], sin_ref[...])
            piece = piece.astype(jnp.bfloat16)
            if at < width_q:
                q_ref[:, at : at + LANES] = piece
            else:
                kv_ref[:, at - width_q : at - width_q + LANES] = piece


def project_qkv(attn_in, weights, cosine, sine, width_q, width_k, after=()):
    rows, depth = attn_in.shape
    return pl.pallas_call(
        functools.partial(qkv_kernel, len(weights)),
        out_shape=(
            jax.ShapeDtypeStruct((rows, width_q), jnp.bfloat16),
            jax.ShapeDtypeStruct((rows, 2 * width_k), jnp.bfloat16),
        ),
        in_specs=[in_vmem] * (3 + len(weights)) + [unread] * len(after),
        out_specs=(in_vmem, in_vmem),
        compiler_params=kernel_params(),
        cost_estimate=cost(0.1),
        name="qkv",
    )(attn_in, *weights, cosine, sine, *after)


def sequence_block(slots, me, half_block, bits):
    slot = slots[me ^ block_key(half_block // 2, bits)]
    return jnp.where(half_block % 2 == 0, slot, 2 * (1 << bits) - 1 - slot)


def head_lanes(pair, head, heads_per_kv, scale):
    wide = pair.astype(jnp.float32) * scale
    group = head // heads_per_kv
    source = wide if head % 2 == group else pltpu.roll(wide, HEAD_SIZE, 1)
    low = lax.broadcasted_iota(jnp.int32, wide.shape, 1) < HEAD_SIZE
    keep = low if group == 0 else jnp.logical_not(low)
    return jnp.where(keep, source, 0.0).astype(jnp.bfloat16)


def causal_tile(size):
    key_at = lax.broadcasted_iota(jnp.int32, (size, size), 0)
    row_at = lax.broadcasted_iota(jnp.int32, (size, size), 1)
    return key_at <= row_at


def over_blocks(visit, slots, me, bits, half, prepare):
    visit(0, 0, True, True, True)
    visit(1, half, True, True, True)
    visit(1, 0, False, False, False)
    own = slots[me]
    blocks_of_query = (own, 2 * (1 << bits) - 1 - own)

    def step(index, carry):
        block = sequence_block(slots, me, index, bits)
        start = pl.multiple_of(index * half, half)
        prepare(start)
        for q_half in range(2):

            @pl.when(block < blocks_of_query[q_half])
            def _():
                visit(q_half, start, False, False, False)

        return carry

    lax.fori_loop(2, 2 * (1 << bits), step, 0)


def forward_kernel(bits, heads, slots, place, q_ref, kv_ref, *refs):
    out_ref, exact_ref, log_ref, qp, run_max, run_sum, acc = refs[-7:]
    rows = q_ref.shape[0]
    half = rows // 2
    per_kv = heads // 2
    for head in range(heads):
        lanes = pl.ds((head // 2) * LANES, LANES)
        qp[head] = head_lanes(q_ref[:, lanes], head, per_kv, HEAD_SIZE ** (-0.5))

    def visit(q_half, key_start, diagonal, first, _):
        keys = kv_ref[pl.ds(key_start, half), 0:LANES]
        values_t = kv_ref[pl.ds(key_start, half), LANES : 2 * LANES].T
        base = q_half * heads
        span = pl.ds(q_half * half, half)
        scores = [nt(keys, qp[head, span, :]) for head in range(heads)]
        if diagonal:
            visible = causal_tile(half)
            scores = [jnp.where(visible, score, big_negative) for score in scores]
        peaks = [jnp.max(score, axis=0, keepdims=True) for score in scores]
        if not first:
            before = [run_max[base + head] for head in range(heads)]
            peaks = [jnp.maximum(peak, old) for peak, old in zip(peaks, before)]
        weights = [jnp.exp(score - peak) for score, peak in zip(scores, peaks)]
        totals = [jnp.sum(weight, axis=0, keepdims=True) for weight in weights]
        outs = []
        for head, weight in enumerate(weights):
            group = head // per_kv
            some = values_t[group * HEAD_SIZE : (group + 1) * HEAD_SIZE]
            outs.append(nn(some, weight.astype(jnp.bfloat16)))
        if not first:
            fades = [jnp.exp(old - peak) for old, peak in zip(before, peaks)]
            totals = [t + run_sum[base + h] * f for h, (t, f) in enumerate(zip(totals, fades))]
            outs = [o + acc[base + h] * f for h, (o, f) in enumerate(zip(outs, fades))]
        for head in range(heads):
            run_max[base + head] = peaks[head]
            run_sum[base + head] = totals[head]
            acc[base + head] = outs[head]

    over_blocks(visit, slots, place[0], bits, half, lambda start: None)
    for q_half in range(2):
        span = pl.ds(q_half * half, half)
        for pair in range(heads // 2):
            parts = []
            for head in (2 * pair, 2 * pair + 1):
                slot = q_half * heads + head
                parts.append(acc[slot] / run_sum[slot])
                log_ref[pl.ds(head, 1), span] = run_max[slot] + jnp.log(run_sum[slot])
            exact = jnp.concatenate(parts, axis=0).T
            exact_ref[span, pl.ds(pair * LANES, LANES)] = exact
            out_ref[span, pl.ds(pair * LANES, LANES)] = exact.astype(jnp.bfloat16)


def attend_forward(slots, place, queries, kv, bits, after=()):
    rows, width = queries.shape
    heads = width // HEAD_SIZE
    half = rows // 2
    return pl.pallas_call(
        functools.partial(forward_kernel, bits, heads),
        out_shape=(
            jax.ShapeDtypeStruct((rows, width), jnp.bfloat16),
            jax.ShapeDtypeStruct((rows, width), jnp.float32),
            jax.ShapeDtypeStruct((heads, rows), jnp.float32),
        ),
        in_specs=[in_smem, in_smem, in_vmem, in_vmem] + [unread] * len(after),
        out_specs=(in_vmem, in_vmem, in_vmem),
        scratch_shapes=[
            pltpu.VMEM((heads, rows, LANES), jnp.bfloat16),
            pltpu.VMEM((2 * heads, 1, half), jnp.float32),
            pltpu.VMEM((2 * heads, 1, half), jnp.float32),
            pltpu.VMEM((2 * heads, HEAD_SIZE, half), jnp.float32),
        ],
        compiler_params=kernel_params(),
        cost_estimate=cost(19),
        name="attention_forward",
    )(slots, place, queries, kv, *after)


def backward_kernel(bits, heads, slots, place, *refs):
    q_ref, kv_ref, do_ref, exact_ref, log_ref, cos_ref, sin_ref = refs[:7]
    parts = max(1, (1 << bits) // 4)
    dq_ref, dkv_refs = refs[-7 - parts], refs[-6 - parts : -6]
    qp, dop, dots, dq_acc, dkv_acc, do_all = refs[-6:]
    rows = q_ref.shape[0]
    half = rows // 2
    per_kv = heads // 2
    shifts, local, _ = do_ref.shape
    for shift in range(shifts):
        source = lax.rem(place[1] - shift + shifts, shifts)
        do_all[pl.ds(pl.multiple_of(source * local, local), local), :] = do_ref[shift]
    for head in range(heads):
        lanes = pl.ds((head // 2) * LANES, LANES)
        qp[head] = head_lanes(q_ref[:, lanes], head, per_kv, HEAD_SIZE ** (-0.5))
        dop[head] = head_lanes(do_all[:, lanes], head, per_kv, 1.0)
    for pair in range(heads // 2):
        lanes = pl.ds(pair * LANES, LANES)
        product = (do_all[:, lanes].astype(jnp.float32) * exact_ref[:, lanes]).T
        dots[pl.ds(2 * pair, 1), :] = jnp.sum(product[:HEAD_SIZE], axis=0, keepdims=True)
        dots[pl.ds(2 * pair + 1, 1), :] = jnp.sum(product[HEAD_SIZE:], axis=0, keepdims=True)

    def clear(start):
        dkv_acc[pl.ds(start, half), :] = jnp.zeros((half, 2 * LANES), jnp.float32)

    def visit(q_half, key_start, diagonal, first_query, first_key):
        rows_of_key = pl.ds(key_start, half)
        keys = kv_ref[rows_of_key, 0:LANES]
        values = kv_ref[rows_of_key, LANES : 2 * LANES]
        keys_t = keys.T
        base = q_half * heads
        span = pl.ds(q_half * half, half)
        q_heads = [qp[head, span, :] for head in range(heads)]
        do_heads = [dop[head, span, :] for head in range(heads)]
        scores = [nt(keys, q_head) for q_head in q_heads]
        grad_ws = [nt(values, do_head) for do_head in do_heads]
        weights = [
            jnp.exp(score - log_ref[pl.ds(head, 1), span]) for head, score in enumerate(scores)
        ]
        if diagonal:
            visible = causal_tile(half)
            weights = [jnp.where(visible, weight, 0.0) for weight in weights]
        grad_ss = [
            (weight * (grad_w - dots[pl.ds(head, 1), span])).astype(jnp.bfloat16)
            for head, (weight, grad_w) in enumerate(zip(weights, grad_ws))
        ]
        weights = [weight.astype(jnp.bfloat16) for weight in weights]
        grad_v = jnp.zeros((half, LANES), jnp.float32)
        grad_k = jnp.zeros((half, LANES), jnp.float32)
        for weight, do_head in zip(weights, do_heads):
            grad_v = grad_v + nn(weight, do_head)
        for grad_s, q_head in zip(grad_ss, q_heads):
            grad_k = grad_k + nn(grad_s, q_head)
        for head, grad_s in enumerate(grad_ss):
            group = head // per_kv
            grad_q = nn(keys_t[group * HEAD_SIZE : (group + 1) * HEAD_SIZE], grad_s)
            if not first_query:
                grad_q = grad_q + dq_acc[base + head]
            dq_acc[base + head] = grad_q
        if not first_key:
            grad_k = grad_k + dkv_acc[rows_of_key, 0:LANES]
            grad_v = grad_v + dkv_acc[rows_of_key, LANES : 2 * LANES]
        dkv_acc[rows_of_key, 0:LANES] = grad_k
        dkv_acc[rows_of_key, LANES : 2 * LANES] = grad_v

    over_blocks(visit, slots, place[0], bits, half, clear)
    size = dkv_acc.shape[0] // parts
    for part, dkv_ref in enumerate(dkv_refs):
        dkv_ref[...] = dkv_acc[part * size : (part + 1) * size, :].astype(jnp.bfloat16)
    for q_half in range(2):
        span = pl.ds(q_half * half, half)
        for pair in range(heads // 2):
            slot = q_half * heads + 2 * pair
            gradient = jnp.concatenate([dq_acc[slot], dq_acc[slot + 1]], axis=0).T
            gradient = rotate_back(
                gradient * HEAD_SIZE ** (-0.5), cos_ref[span, :], sin_ref[span, :]
            )
            dq_ref[span, pl.ds(pair * LANES, LANES)] = gradient.astype(jnp.bfloat16)


def attend_backward(
    slots, place, queries, kv, grad_parts, exact, log_total, cosine, sine, bits, after=()
):
    parts = max(1, (1 << bits) // 4)
    rows, width = queries.shape
    heads = width // HEAD_SIZE
    half = rows // 2
    return pl.pallas_call(
        functools.partial(backward_kernel, bits, heads),
        out_shape=(
            jax.ShapeDtypeStruct((rows, width), jnp.bfloat16),
            *[jax.ShapeDtypeStruct((kv.shape[0] // parts, kv.shape[1]), jnp.bfloat16)] * parts,
        ),
        in_specs=[in_smem, in_smem] + [in_vmem] * 7 + [unread] * len(after),
        out_specs=(in_vmem,) * (1 + parts),
        scratch_shapes=[
            pltpu.VMEM((heads, rows, LANES), jnp.bfloat16),
            pltpu.VMEM((heads, rows, LANES), jnp.bfloat16),
            pltpu.VMEM((heads, rows), jnp.float32),
            pltpu.VMEM((2 * heads, HEAD_SIZE, half), jnp.float32),
            pltpu.VMEM(kv.shape, jnp.float32),
            pltpu.VMEM((rows, width), jnp.bfloat16),
        ],
        compiler_params=kernel_params(),
        cost_estimate=cost(30),
        name="attention_backward",
    )(slots, place, queries, kv, grad_parts, exact, log_total, cosine, sine, *after)


def grad_qkv_kernel(dq_ref, own_ref, first_ref, second_ref, cos_ref, sin_ref, out_ref):
    width_q = dq_ref.shape[1]
    out_ref[:, 0:width_q] = dq_ref[...]
    total = own_ref[...].astype(jnp.float32) + first_ref[...].astype(jnp.float32)
    total = total + second_ref[...].astype(jnp.float32)
    keys = rotate_back(total[:, 0:LANES], cos_ref[...], sin_ref[...])
    out_ref[:, width_q : width_q + LANES] = keys.astype(jnp.bfloat16)
    out_ref[:, width_q + LANES :] = total[:, LANES:].astype(jnp.bfloat16)


def join_grad_qkv(grad_queries, pieces, cosine, sine):
    rows, width_q = grad_queries.shape
    width = width_q + pieces[0].shape[1]
    return pl.pallas_call(
        grad_qkv_kernel,
        out_shape=jax.ShapeDtypeStruct((rows, width), jnp.bfloat16),
        in_specs=[in_vmem] * 6,
        out_specs=in_vmem,
        compiler_params=kernel_params(),
        cost_estimate=cost(0.1),
        name="grad_qkv",
    )(grad_queries, *pieces, cosine, sine)


def mlp_kernel(count, x_ref, g_ref, *refs):
    weights = refs[:count], refs[count : 2 * count], refs[2 * count : 3 * count]
    hidden_ref, grad_gate_ref, grad_up_ref = refs[3 * count :]
    depth = x_ref.shape[1] // count

    def product(left, parts):
        total = 0.0
        for index, part in enumerate(parts):
            total = total + nn(left[:, index * depth : (index + 1) * depth], part[...])
        return total

    gate = product(x_ref, weights[0])
    up = product(x_ref, weights[1])
    grad_hidden = product(g_ref, weights[2])
    sigmoid = jax.nn.sigmoid(gate)
    silu = gate * sigmoid
    hidden_ref[...] = (silu * up).astype(jnp.bfloat16)
    grad_gate = grad_hidden * up * sigmoid * (1.0 + gate * (1.0 - sigmoid))
    grad_gate_ref[...] = grad_gate.astype(jnp.bfloat16)
    grad_up_ref[...] = (grad_hidden * silu).astype(jnp.bfloat16)


def mlp_inner(mlp_in, grad_rows, gates, ups, downs):
    rows, depth = mlp_in.shape
    units = gates[0].shape[1]
    count = len(gates)
    tile = min(256, units)
    whole = pl.BlockSpec((rows, depth), lambda i: (0, 0))
    part = pl.BlockSpec((depth // count, tile), lambda i: (0, i))
    out = pl.BlockSpec((rows, tile), lambda i: (0, i))
    shape = jax.ShapeDtypeStruct((rows, units), jnp.bfloat16)
    return pl.pallas_call(
        functools.partial(mlp_kernel, count),
        grid=(units // tile,),
        out_shape=(shape, shape, shape),
        in_specs=[whole, whole] + [part] * (3 * count),
        out_specs=(out, out, out),
        compiler_params=kernel_params(),
        cost_estimate=cost(0.1),
        name="mlp_inner",
    )(mlp_in, grad_rows, *gates, *ups, *downs)


def project_part(lefts, part):
    depth, rows, width = lefts.shape
    features = part.shape[1]
    tile = min(256, features)

    def kernel(left_ref, part_ref, out_ref):
        total = 0.0
        for group in range(depth):
            total = total + nt(left_ref[group], part_ref[group])
        out_ref[...] = total

    return pl.pallas_call(
        kernel,
        grid=(features // tile,),
        out_shape=jax.ShapeDtypeStruct((rows, features), jnp.float32),
        in_specs=[
            pl.BlockSpec((depth, rows, width), lambda i: (0, 0, 0)),
            pl.BlockSpec((depth, tile, width), lambda i: (0, i, 0)),
        ],
        out_specs=pl.BlockSpec((rows, tile), lambda i: (0, i)),
        compiler_params=kernel_params(),
        cost_estimate=cost(0.1),
        name="project_part",
    )(lefts, part)


def residual_kernel(place, left_ref, x_ref, gain_ref, part_ref, *refs):
    sums, (mlp_ref, here_ref, residual) = refs[:-3], refs[-3:]
    depth, rows, _ = left_ref.shape
    tile = part_ref.shape[1]
    step = pl.program_id(0)
    total = 0.0
    for group in range(depth):
        total = total + nt(left_ref[group], part_ref[group])
    residual[step] = total

    @pl.when(step == pl.num_programs(0) - 1)
    def _():
        width = x_ref.shape[1]
        before = sum(ref.shape[1] for ref in sums)
        squares = jnp.zeros((rows, 1), jnp.float32)
        pieces = []
        for ref in sums:
            pieces += [(ref, slice(k, k + tile)) for k in range(0, ref.shape[1], tile)]
        count = (width - before) // tile
        local = rows // depth
        here = pl.ds(pl.multiple_of(place[1] * local, local), local)
        for index in range(width // tile):
            columns = slice(index * tile, (index + 1) * tile)
            values = x_ref[:, columns].astype(jnp.float32)
            if index < len(pieces):
                ref, at = pieces[index]
                values = values + ref[:, at]
                ref[:, at] = values
            else:
                values = values + residual[index - len(pieces)]
                residual[index - len(pieces)] = values
            squares = squares + jnp.sum(values * values, axis=1, keepdims=True)
        factor = lax.rsqrt(squares / width + eps_norm)
        for index in range(width // tile):
            columns = slice(index * tile, (index + 1) * tile)
            if index < len(pieces):
                ref, at = pieces[index]
                values, mine = ref[:, at], ref[here, at]
            else:
                values = residual[index - len(pieces)]
                mine = residual[index - len(pieces), here, :]
            mlp_ref[:, columns] = (values * factor * gain_ref[:, columns]).astype(jnp.bfloat16)
            here_ref[:, columns] = mine


def project_residual(place, lefts, rows, gain, parts):
    depth, count, width = lefts.shape
    total = rows.shape[1]
    sums = [project_part(lefts, part) for part in parts[:-1]]
    features = parts[-1].shape[1]
    tile = min(256, features)
    whole = lambda i: (0, 0)
    return pl.pallas_call(
        residual_kernel,
        grid=(features // tile,),
        out_shape=(
            jax.ShapeDtypeStruct((count, total), jnp.bfloat16),
            jax.ShapeDtypeStruct((count // depth, total), jnp.float32),
        ),
        in_specs=[
            in_smem,
            pl.BlockSpec((depth, count, width), lambda i: (0, 0, 0)),
            pl.BlockSpec((count, total), whole),
            pl.BlockSpec((1, total), whole),
            pl.BlockSpec((depth, tile, width), lambda i: (0, i, 0)),
        ]
        + [pl.BlockSpec(each.shape, whole) for each in sums],
        out_specs=(
            pl.BlockSpec((count, total), whole),
            pl.BlockSpec((count // depth, total), whole),
        ),
        scratch_shapes=[pltpu.VMEM((features // tile, count, tile), jnp.float32)],
        compiler_params=kernel_params(),
        cost_estimate=cost(0.1),
        name="project_residual",
    )(place, lefts, rows, gain, parts[-1], *sums)


def to_features(lefts, weights, after=()):
    rows = lefts[0].shape[0]
    count = len(weights[0])
    features = weights[0][0].shape[0]
    tile = min(256, features)
    tiles = features // tile

    def kernel(*refs):
        left_refs, part_refs, out_ref = refs[: len(lefts)], refs[len(lefts) :], refs[-1]
        step = pl.program_id(0)
        for part in range(count):

            @pl.when(step // tiles == part)
            def _():
                total = 0.0
                for source, left_ref in enumerate(left_refs):
                    total = total + nt(left_ref[...], part_refs[source * count + part][...])
                out_ref[...] = total.astype(jnp.bfloat16)

    def part_at(base, i):
        return (jnp.clip(i - base, 0, tiles - 1), 0)

    return pl.pallas_call(
        kernel,
        grid=(count * tiles,),
        out_shape=jax.ShapeDtypeStruct((rows, count * features), jnp.bfloat16),
        in_specs=[pl.BlockSpec(left.shape, lambda i: (0, 0)) for left in lefts]
        + [
            pl.BlockSpec((tile, parts[part].shape[1]), functools.partial(part_at, part * tiles))
            for parts in weights
            for part in range(count)
        ]
        + [unread] * len(after),
        out_specs=pl.BlockSpec((rows, tile), lambda i: (0, i)),
        compiler_params=kernel_params(),
        cost_estimate=cost(0.1),
        name="to_features",
    )(*lefts, *[part for parts in weights for part in parts], *after)


def to_groups(place, branch, parts):
    rows, depth = branch.shape
    groups, features, width = parts[0].shape
    count = len(parts)

    def kernel(place, x_ref, *refs):
        total = 0.0
        for index, part in enumerate(refs[:count]):
            columns = x_ref[:, index * features : (index + 1) * features]
            total = total + nn(columns, part[0])
        refs[-1][0] = total.astype(jnp.bfloat16)

    def weight_at(shift, place):
        return (lax.rem(place[1] + shift, groups), 0, 0)

    return pl.pallas_call(
        kernel,
        grid_spec=pltpu.PrefetchScalarGridSpec(
            num_scalar_prefetch=1,
            grid=(groups,),
            in_specs=[pl.BlockSpec((rows, depth), lambda i, place: (0, 0))]
            + [pl.BlockSpec((1, features, width), weight_at)] * count,
            out_specs=pl.BlockSpec((1, rows, width), lambda i, place: (i, 0, 0)),
        ),
        out_shape=jax.ShapeDtypeStruct((groups, rows, width), jnp.bfloat16),
        compiler_params=kernel_params(),
        cost_estimate=cost(0.1),
        name="to_groups",
    )(place, branch, *parts)


def to_block_groups(place, rows, bits, groups):
    local, depth = rows.shape
    width = depth >> bits
    count = (1 << bits) // groups
    if width % LANES:
        blocks = to_absolute(rows, place[0], bits)
        blocks = blocks.reshape(local, groups, count, width).transpose(1, 2, 0, 3)
        return jnp.stack(
            [
                lax.dynamic_index_in_dim(blocks, (place[1] + d) % groups, 0, keepdims=False)
                for d in range(groups)
            ]
        )

    def kernel(place, in_ref, out_ref):
        for d in range(groups):
            for index in range(count):
                block = lax.rem(place[1] + d, groups) * count + index
                start = key_position(place[0] ^ block, bits) * width
                out_ref[d, index] = in_ref[:, pl.ds(pl.multiple_of(start, LANES), width)]

    return pl.pallas_call(
        kernel,
        out_shape=jax.ShapeDtypeStruct((groups, count, local, width), rows.dtype),
        in_specs=[in_smem, in_vmem],
        out_specs=in_vmem,
        compiler_params=kernel_params(),
        cost_estimate=cost(0.1),
        name="to_block_groups",
    )(place, rows)


def gradient_out(place, branch, attended, bits):
    shifts = len(branch)
    count, local, features = branch[0].shape
    groups, rows, width = attended.shape
    parts = (1 << bits) // 4

    def kernel(place, *refs):
        lefts, right_ref, outs = refs[:shifts], refs[shifts], refs[shifts + 1 :]
        for part, out_ref in enumerate(outs):
            for block in range(4):
                device = place[0] ^ block_key(4 * part + block, bits)
                index = lax.rem(device, count)
                group = device // count
                total = 0.0
                for distance, left in enumerate(lefts):
                    start = lax.rem(place[1] - distance + shifts, shifts) * local
                    here = pl.ds(pl.multiple_of(start, local), local)
                    total = total + inner_rows(left[index], right_ref[group, here, :])
                out_ref[block * features : (block + 1) * features, :] = total.astype(jnp.bfloat16)

    return pl.pallas_call(
        kernel,
        out_shape=[jax.ShapeDtypeStruct((4 * features, width), jnp.bfloat16)] * parts,
        in_specs=[in_smem] + [in_vmem] * (shifts + 1),
        out_specs=[in_vmem] * parts,
        compiler_params=kernel_params(),
        cost_estimate=cost(0.1),
        name="gradient_out",
    )(place, *branch, attended)


def to_owners(array, count):
    ctx, tp = lax.axis_size("ctx"), lax.axis_size("tp")
    moves = []
    for c in range(ctx):
        for t in range(tp):
            moves.append((c * tp + t, (count * t + c % count) * tp + c // count))
    return lax.ppermute(array, ("ctx", "tp"), moves)


def block_rows(rows):
    quarter = rows // 4
    return [quarter, quarter, quarter, quarter // 2, quarter // 2]


def gradient_part(left, right, parts, part, received=(), pieces=4, after=()):
    rows, depth = left.shape
    depth = depth // parts
    width = right.shape[1]
    tile = next(t for t in (1024, 768, 512, 256, LANES, width) if width % t == 0)
    sizes = block_rows(depth) if received else [depth // pieces] * pieces
    step = depth // max(1, len(received))

    def kernel(left_ref, right_ref, *refs):
        total = inner_rows(left_ref[...], right_ref[...])
        start = 0
        for size, out_ref in zip(sizes, refs[len(received) + len(after) :]):
            piece = total[start : start + size]
            if received:
                offset = start % step
                other = refs[start // step][offset : offset + size, :]
                piece = piece + other.astype(jnp.float32)
            out_ref[...] = piece.astype(jnp.bfloat16)
            start += size

    return pl.pallas_call(
        kernel,
        grid=(width // tile,),
        out_shape=[jax.ShapeDtypeStruct((size, width), jnp.bfloat16) for size in sizes],
        in_specs=[
            pl.BlockSpec((rows, depth), lambda i: (0, part)),
            pl.BlockSpec((rows, tile), lambda i: (0, i)),
        ]
        + [pl.BlockSpec((step, tile), lambda i: (0, i))] * len(received)
        + [unread] * len(after),
        out_specs=[pl.BlockSpec((size, tile), lambda i: (0, i)) for size in sizes],
        compiler_params=kernel_params(),
        cost_estimate=cost(0.1),
        name="gradient_part",
    )(left, right, *received, *after)


def gradient_begin(left, right, bits, pieces=4, after=()):
    parts = (1 << bits) // 4
    bit = bit_order(bits)[-1]
    return [
        [
            swap(block, bit, bits)
            for block in gradient_part(left, right, parts, part, pieces=pieces, after=after)
        ]
        for part in range(parts // 2, parts)
    ]


def gradient_end(left, right, received, bits):
    parts = (1 << bits) // 4
    if parts == 2:
        return gradient_part(left, right, parts, 0, received[0])
    kept = [jnp.concatenate(gradient_part(left, right, parts, p)) for p in range(parts // 2)]
    kept = [add_half(mine, jnp.concatenate(other)) for mine, other in zip(kept, received)]
    return sum_parts(kept, bits, bit_order(bits)[2:-1])


def finish_input(place, gradient, residual, rows, gain, bits):
    local, depth = gradient.shape
    width = depth >> bits
    whole_lanes = width % LANES == 0

    def kernel(place, grad_ref, residual_ref, rows_ref, gain_ref, out_ref, *scratch):
        start = pl.multiple_of(place[1] * local, local)
        values = rows_ref[pl.ds(start, local), :].astype(jnp.float32)
        factor = rms_scale(values)
        normed = values * factor
        scaled = grad_ref[...].astype(jnp.float32) * gain_ref[...]
        total = residual_ref[...] + norm_back(scaled, normed, factor)
        if not whole_lanes:
            out_ref[...] = total
            return
        for p in range(1 << bits):
            other = pl.multiple_of((place[0] ^ block_key(p, bits)) * width, LANES)
            out_ref[:, pl.ds(other, width)] = total[:, p * width : (p + 1) * width]

    out = pl.pallas_call(
        kernel,
        out_shape=jax.ShapeDtypeStruct((local, depth), jnp.float32),
        in_specs=[in_smem] + [in_vmem] * 4,
        out_specs=in_vmem,
        compiler_params=kernel_params(),
        cost_estimate=cost(0.1),
        name="finish_input",
    )(place, gradient, residual, rows, gain)
    return out if whole_lanes else to_absolute(out, place[0], bits)


def sum_parts(parts, bits, over):
    for bit in reversed(over):
        count = len(parts) // 2
        came = [swap(part, bit, bits) for part in parts[count:]]
        if count == 1:
            return split_blocks(parts[0], came[0])
        parts = [add_half(mine, other) for mine, other in zip(parts[:count], came)]


def split_blocks(kept, received):
    sizes = block_rows(kept.shape[0])

    def kernel(kept_ref, other_ref, *refs):
        start = 0
        for size, out_ref in zip(sizes, refs):
            here = slice(start, start + size)
            out_ref[...] = add_half(kept_ref[here, :], other_ref[here, :])
            start += size

    return pl.pallas_call(
        kernel,
        out_shape=[jax.ShapeDtypeStruct((size, kept.shape[1]), jnp.bfloat16) for size in sizes],
        in_specs=[in_vmem] * 2,
        out_specs=[in_vmem] * 5,
        compiler_params=kernel_params(),
        cost_estimate=cost(0.1),
        name="split_blocks",
    )(kept, received)


def rows_begin(parts, bits):
    return sum_parts(parts, bits, bit_order(bits)[2:])


def window(*values):
    return lax.optimization_barrier(values)


def cut(values, *sizes):
    out, start = [], 0
    for size in sizes:
        out.append(values[start : start + size])
        start += size
    return out


def on_device(
    block_in, out_grad, pair_slot, gain_attn, wq, wk, wv, wo, gain_mlp, w_gate, w_up, w_down
):
    bits = (lax.axis_size("ctx") - 1).bit_length()
    shifts = lax.axis_size("tp")
    me = lax.axis_index("ctx")
    tp = lax.axis_index("tp")
    place = jnp.stack([me, tp]).astype(jnp.int32)
    local_rows, model = block_in.shape
    group_rows = local_rows * shifts
    width_q, width_k = wq.shape[1], wk.shape[1]
    count = (1 << bits) // 4

    x_all = lax.all_gather(block_in, "tp", axis=0, tiled=True)
    qkv_here = join([wq, wk, wv], axis=1)
    qkv_one = gather_one(qkv_here, bits)
    gains = gather_small(jnp.stack([gain_attn, gain_mlp]), bits).astype(jnp.float32)
    gains = jnp.swapaxes(gains, 0, 1).reshape(2, -1)
    gate_one = gather_one(w_gate, bits)
    qkv_two = gather_two(qkv_one, bits)
    qkv_w = gather_end(qkv_here, qkv_one, qkv_two, bits)
    pos_all = block_positions(pair_slot, group_rows // 2)
    pos_rows = lax.dynamic_slice_in_dim(pos_all, me * group_rows, group_rows)
    cosine, sine = rope_tables(pos_rows)
    out_grad_here = reorder(place, out_grad, bits)
    both_sent = jnp.concatenate([out_grad_here, wo.reshape(-1, model)], axis=0)
    x_all, both_sent, w_up, gains, cosine, sine, *pieces = window(
        x_all, both_sent, w_up, gains, cosine, sine, *qkv_w, *gate_one
    )
    qkv_w, gate_one = cut(pieces, count, 2)

    g_attn, g_mlp = gains[0:1], gains[1:2]
    both_all = lax.all_gather(both_sent, "tp", axis=0)
    gate_two = gather_two(gate_one, bits)
    rows_all, attn_in = norm_rows(place, x_all, g_attn, bits)
    queries, kv = project_qkv(attn_in, qkv_w, cosine, sine, width_q, width_k)
    kv_one = gather_one(kv, bits)
    kv_all = join(gather_end(kv, kv_one, gather_two(kv_one, bits), bits))
    kv_all, w_up, w_down = window(kv_all, w_up, w_down)

    up_one = gather_one(w_up, bits)
    attended, exact, log_total = attend_forward(pair_slot, place, queries, kv_all, bits)
    attended, both_all, w_down, *pieces = window(
        attended, both_all, w_down, *gate_two, *up_one
    )
    gate_two, up_one = cut(pieces, 2, 2)

    attended_all = lax.all_gather(attended, "tp", axis=0)
    grad_rows = both_all[:, :local_rows].reshape(group_rows, model)
    wo_groups = both_all[:, local_rows:].reshape(shifts, *wo.shape)
    o_one = gather_one(wo_groups, bits)
    up_two = gather_two(up_one, bits)
    o_two = gather_two(o_one, bits, 1)
    gate_w = gather_end(w_gate, gate_one, gate_two, bits)
    attended_all, grad_rows, w_down, *pieces = window(
        attended_all, grad_rows, w_down, *o_two, *up_two, *gate_w
    )
    o_two, up_two, gate_w = cut(pieces, 2, 2, count)

    down_one = gather_one(w_down, bits)
    o_w = gather_end(wo_groups, o_one, o_two, bits, 1)
    mlp_in, residual_here = project_residual(place, attended_all, rows_all, g_mlp, o_w)
    mlp_in, residual_here, *pieces = window(
        mlp_in, residual_here, *down_one, *up_one, *up_two
    )
    down_one, up_one, up_two = cut(pieces, 2, 2, 2)
    up_w = gather_end(w_up, up_one, up_two, bits)
    down_two = gather_two(down_one, bits)
    down_w = gather_end(w_down, down_one, down_two, bits)
    factor_mlp = rms_scale(residual_here)
    normed_mlp = residual_here * factor_mlp

    hidden, grad_gate, grad_up = mlp_inner(mlp_in, grad_rows, gate_w, up_w, down_w)
    grad_mlp_part = to_features([grad_gate, grad_up], [gate_w, up_w])
    grad_mlp_part, hidden, grad_gate, grad_up = window(grad_mlp_part, hidden, grad_gate, grad_up)

    grad_mlp_in = lax.psum_scatter(grad_mlp_part, "tp", scatter_dimension=0, tiled=True)
    down_sum = gradient_begin(grad_rows, hidden, bits)
    up_sum = gradient_begin(mlp_in, grad_up, bits)
    gate_sum = gradient_begin(mlp_in, grad_gate, bits)
    down_sum = gradient_end(grad_rows, hidden, down_sum, bits)
    up_sum = gradient_end(mlp_in, grad_up, up_sum, bits)
    gate_sum = gradient_end(mlp_in, grad_gate, gate_sum, bits)
    down_two = scatter_two(down_sum, scatter_one(down_sum, bits))
    up_two = scatter_two(up_sum, scatter_one(up_sum, bits))
    gate_one = scatter_one(gate_sum, bits)
    mlp_part = to_features([hidden], [down_w])
    grad_mlp_in, mlp_part, *pieces = window(
        grad_mlp_in, mlp_part, *down_two, *up_two, *gate_one, *gate_sum
    )
    down_two, up_two, gate_one, gate_sum = cut(pieces, 2, 2, 2, 5)

    down_three = scatter_three(down_two, bits)
    grad_mlp_in = grad_mlp_in.astype(jnp.float32)
    gain_mlp_part = jnp.sum(grad_mlp_in * normed_mlp, axis=0, keepdims=True)
    grad_residual = out_grad_here.astype(jnp.float32) + norm_back(
        grad_mlp_in * g_mlp, normed_mlp, factor_mlp
    )
    branch_here = grad_residual.astype(jnp.bfloat16)
    grad_groups = to_groups(place, branch_here, o_w)
    grad_parts = jnp.stack(tp_exchange(grad_groups))
    gate_two = scatter_two(gate_sum, gate_one)
    grad_parts, branch_here, mlp_part, *pieces = window(
        grad_parts, branch_here, mlp_part, *down_three, *up_two, *gate_two
    )
    down_three, up_two, gate_two = cut(pieces, 2, 2, 2)

    up_three = scatter_three(up_two, bits)
    gate_three = scatter_three(gate_two, bits)
    branch_blocks = to_block_groups(place, branch_here, bits, shifts)
    mlp_out = lax.psum_scatter(mlp_part, "tp", scatter_dimension=0, tiled=True)
    grad_queries, *grad_kv = attend_backward(
        pair_slot, place, queries, kv_all, grad_parts, exact, log_total, cosine, sine, bits
    )
    branch_blocks, *pieces = window(branch_blocks, *grad_kv, *up_three)
    grad_kv, up_three = cut(pieces, count, 2)

    kv_sum = rows_begin(grad_kv, bits)
    kv_three = scatter_three(scatter_two(kv_sum, scatter_one(kv_sum, bits)), bits)
    branch_pieces = tp_exchange(branch_blocks)
    mlp_out, *pieces = window(mlp_out, kv_sum[0], *kv_three, *branch_pieces)
    kv_pieces, branch_pieces = cut(pieces, 3, shifts)
    grad_qkv = join_grad_qkv(grad_queries, kv_pieces, cosine, sine)
    grad_attn_part = to_features([grad_qkv], [qkv_w])
    grad_attn_part, grad_qkv, *branch_pieces = window(grad_attn_part, grad_qkv, *branch_pieces)

    grad_attn_in = lax.psum_scatter(grad_attn_part, "tp", scatter_dimension=0, tiled=True)
    qkv_sum = gradient_begin(attn_in, grad_qkv, bits, pieces=1)
    qkv_sum = gradient_end(attn_in, grad_qkv, qkv_sum, bits)
    inputs = rows_all.astype(jnp.float32)
    gain_attn_part = jnp.sum(
        grad_attn_part.astype(jnp.float32) * (inputs * rms_scale(inputs)), axis=0, keepdims=True
    )
    gain_sum = jnp.concatenate([gain_attn_part, gain_mlp_part])
    gain_sum = jnp.swapaxes(gain_sum.reshape(2, 1 << bits, -1), 0, 1)
    order = bit_order(bits)
    for bit in reversed(order[2:]):
        gain_sum = scatter_step(gain_sum, bit, bits)
    o_sum = rows_begin(gradient_out(place, branch_pieces, attended_all, bits), bits)
    gain_sum, *pieces = window(gain_sum, *qkv_sum, *o_sum, *gate_three, *down_three, *up_three)
    qkv_sum, o_sum, gate_three, down_three, up_three = cut(pieces, 5, 5, 2, 2, 2)

    qkv_two = scatter_two(qkv_sum, scatter_one(qkv_sum, bits))
    o_two = scatter_two(o_sum, scatter_one(o_sum, bits))
    gain_sum = scatter_step(gain_sum, order[1], bits)
    gain_sum = scatter_step(gain_sum, order[0], bits)
    (sum_down_w,) = finish_sum(down_sum, down_three)
    pieces = window(gain_sum, *qkv_two, *o_two, *gate_three, *up_three, mlp_out, sum_down_w)
    (gain_sum,), qkv_two, o_two, gate_three, up_three, (mlp_out, sum_down_w) = cut(
        pieces, 1, 2, 2, 2, 2, 2
    )
    gate_three, up_three = list(gate_three), list(up_three)

    qkv_three, o_three = scatter_three(qkv_two, bits), scatter_three(o_two, bits)
    gain_here, shift = gain_sum[0], 1
    while shift < shifts:
        gain_here = sum_step(gain_here, shift, "tp")
        shift *= 2
    (sum_up_w,) = finish_sum(up_sum, up_three)
    input_grad = finish_input(place, grad_attn_in, grad_residual, rows_all, g_attn, bits)
    gain_here, sum_up_w, input_grad, gate_three[0], *pieces = window(
        gain_here, sum_up_w, input_grad, gate_three[0], *qkv_three, *o_three
    )
    qkv_three, o_three = cut(pieces, 2, 2)

    (sum_o_w,) = finish_sum(o_sum, o_three)
    sum_o_w = to_owners(sum_o_w.astype(jnp.bfloat16), (1 << bits) // shifts)
    (sum_gate_w,) = finish_sum(gate_sum, gate_three)
    block_out = (residual_here + mlp_out.astype(jnp.float32)).astype(jnp.bfloat16)
    block_out = reorder(place, block_out, bits, inverse=True)
    sum_q_w, sum_k_w, sum_v_w = finish_sum(qkv_sum, qkv_three, [width_q, width_k, width_k])
    return (
        block_out,
        input_grad,
        gain_here[0],
        sum_q_w,
        sum_k_w,
        sum_v_w,
        sum_o_w.astype(jnp.float32),
        gain_here[1],
        sum_gate_w,
        sum_up_w,
        sum_down_w,
    )


def solution(mesh):
    placed = (
        P(("ctx", "tp"), None),
        P(("ctx", "tp"), None),
        P(),
        P("ctx"),
        P("ctx", "tp"),
        P("ctx", "tp"),
        P("ctx", "tp"),
        P("ctx", "tp"),
        P("ctx"),
        P("ctx", "tp"),
        P("ctx", "tp"),
        P("ctx", "tp"),
    )
    return jax.shard_map(
        on_device,
        mesh=mesh,
        in_specs=placed,
        out_specs=(
            P(("ctx", "tp"), None),
            P(("ctx", "tp"), None),
            P("ctx"),
            P("ctx", "tp"),
            P("ctx", "tp"),
            P("ctx", "tp"),
            P("ctx", "tp"),
            P("ctx"),
            P("ctx", "tp"),
            P("ctx", "tp"),
            P("ctx", "tp"),
        ),
        check_vma=False,
    )
```
